32 devices in a mesh: dp: 8 (over z, y), seq: 4 (over x, core).
Axes of the slice: x: 2, y: 2, z: 4, core: 2. Of those that a mesh axis runs over, the one named last changes fastest.
Arguments:
- layer_input: bfloat16 [16384, 768], P(('dp', 'seq')), may hold values from -6 to 6
- cotangent: bfloat16 [16384, 768], P(('dp', 'seq')), may hold values from -6 to 6
- segments: int32 [8, 2048], P('dp'), may hold values from 0 to 3, as said below
- routes: int32 [16384, 2], P(('dp', 'seq')), may hold values from 0 to 7, all different within a row
- order: int32 [16384], P(('dp', 'seq')), may hold values from 0 to 511, as said below
- norm1_gain: bfloat16 [768], P(('dp', 'seq')), may hold values from 0.5 to 1.5
- attn_qkv: bfloat16 [768, 2304], P(('dp', 'seq')), may hold values from -0.21875 to 0.21875
- attn_out: bfloat16 [768, 768], P(('dp', 'seq')), may hold values from -0.875 to 0.875
- norm2_gain: bfloat16 [768], P(('dp', 'seq')), may hold values from 0.5 to 1.5
- router: bfloat16 [768, 8], P(('dp', 'seq')), may hold values from -0.15625 to 0.15625
- shared_in: bfloat16 [768, 4096], P(('dp', 'seq')), may hold values from -0.21875 to 0.21875
- shared_out: bfloat16 [2048, 768], P(('dp', 'seq')), may hold values from -0.125 to 0.125
- expert_in: bfloat16 [8, 768, 4096], P('dp'), may hold values from -0.21875 to 0.21875
- expert_out: bfloat16 [8, 2048, 768], P('dp'), may hold values from -0.125 to 0.125
Outputs:
- layer_output: float32 [16384, 768], P(('dp', 'seq'))
- input_grad: float32 [16384, 768], P(('dp', 'seq'))
- norm1_gain_grad: float32 [768], P(('dp', 'seq'))
- attn_qkv_grad: float32 [768, 2304], P(('dp', 'seq'))
- attn_out_grad: float32 [768, 768], P(('dp', 'seq'))
- norm2_gain_grad: float32 [768], P(('dp', 'seq'))
- router_grad: float32 [768, 8], P(('dp', 'seq'))
- shared_in_grad: float32 [768, 4096], P(('dp', 'seq'))
- shared_out_grad: float32 [2048, 768], P(('dp', 'seq'))
- expert_in_grad: float32 [8, 768, 4096], P('dp', None, 'seq')
- expert_out_grad: float32 [8, 2048, 768], P('dp', 'seq')
The draws below stay inside these ranges and needn't reach their ends.
Inputs may be any that keep to these rules, and one draw needn't show every extreme that they name: `segments`: each sequence holds four documents numbered 0, 1, 2, 3 in order, each of one token or more. `routes`: each token names two different experts. `order`: within the tokens of one device (512 in a row) each number from 0 to 511 stands once.
All inputs are finite; a program needn't handle non-finite values.
Results may differ from the reference program's by a relative error of at most 0.015.
Values may be sent and summed in bfloat16 or wider, within the bound.
No kernel may reach another device: no remote copies, remote signals or barrier semaphores. Data moves between devices by JAX's collectives and lax.ppermute only.
A program may use at most 192 MiB of HBM per device.

```python
import jax
import jax.numpy as jnp
from jax import lax

D = 768
HEADS = 12
HD = 64
FF = 2048
SFF = 2048
TOP = 2
TOK_DEV = 512
LEN = 2048
SEQS = 8
TOKENS = 16384
EXPERTS = 8
CAP = 144


def draw_segments(key, part):
    key = jax.random.fold_in(key, 11)
    keys = jax.random.split(key, SEQS)

    def one_sequence(seq_key):
        key_start, key_end, key_last = jax.random.split(seq_key, 3)
        start = jax.random.randint(key_start, (), 1, TOK_DEV // 2 + 1)
        finish = jax.random.randint(key_end, (), LEN - TOK_DEV // 2, LEN - 1)
        last_start = jax.random.randint(key_last, (), finish + 1, LEN)
        places = jnp.arange(LEN)
        return (places >= start).astype(jnp.int32) + (places >= finish).astype(jnp.int32) + (places >= last_start).astype(jnp.int32)
    return jax.vmap(one_sequence)(keys).astype(jnp.int32)


def draw_order(key, part):
    key = jax.random.fold_in(key, 12)
    keys = jax.random.split(key, TOKENS // TOK_DEV)
    ranks = jax.vmap(lambda block_key: jax.random.permutation(block_key, TOK_DEV))(keys)
    return ranks.reshape(TOKENS).astype(jnp.int32)


def steps_of(key, extent, cuts, low, largest):
    level = 1.0
    for dim, blocks in cuts:
        draws = jax.random.uniform(jax.random.fold_in(jax.random.fold_in(key, 6), dim), (blocks,), jnp.float32, low / len(cuts), largest / len(cuts))
        level = level * jnp.repeat(jnp.exp(draws), extent[dim] // blocks).reshape((-1,) + (1,) * (len(extent) - 1 - dim))
    return level


def different_ones(stream_key, rows, amount, top, lift):
    order = jax.random.permutation(jax.random.fold_in(stream_key, 1), amount)
    favour = order
    for power in range(3):
        favour = favour * favour // amount
    favour = favour * lift // amount
    tickets = jax.random.randint(jax.random.fold_in(stream_key, 2), (rows, amount), 0, 4096) + favour
    holders = jax.random.permutation(jax.random.fold_in(stream_key, 3), rows)[jnp.arange(amount) % rows]
    tickets = jnp.where(jnp.arange(rows)[:, None] == holders[None, :], 1 << 14, tickets)
    priority = tickets * amount + jnp.arange(amount)
    return lax.top_k(priority.astype(jnp.int32), top)[1].astype(jnp.int32)


def centred(rng, dims, deviation, bound, cuts=(), kind=jnp.bfloat16):
    drawn = deviation * jax.random.normal(rng, dims, jnp.float32)
    if cuts:
        drawn = drawn * steps_of(rng, dims, cuts, -0.22, 0.18)
    return jnp.clip(drawn, -bound, bound).astype(kind)


def setup_inputs(seed: int = 0) -> dict:
    key_of = jax.random.split(jax.random.key(seed), 15)
    layer_input = centred(key_of[0], (TOKENS, D), 1.0, 6.0, ((0, 32),))
    cotangent = centred(key_of[1], (TOKENS, D), 1.0, 6.0, ((0, 32),))
    segments = draw_segments(jax.random.fold_in(key_of[14], 71), 0)
    routes = different_ones(key_of[3], TOKENS, EXPERTS, TOP, 2048)
    order = draw_order(jax.random.fold_in(key_of[14], 71), 0)
    norm1_gain = jnp.clip(1.0 + 0.1 * jax.random.normal(key_of[5], (D,), jnp.float32), 0.5, 1.5).astype(jnp.bfloat16)
    attn_qkv = centred(key_of[6], (D, 3 * D), D ** -0.5, 0.21875, ((0, 32),))
    attn_out = centred(key_of[7], (D, D), (D // 16) ** -0.5, 0.875, ((0, 32),))
    norm2_gain = jnp.clip(1.0 + 0.1 * jax.random.normal(key_of[8], (D,), jnp.float32), 0.5, 1.5).astype(jnp.bfloat16)
    router = centred(key_of[9], (D, EXPERTS), (2 * D) ** -0.5, 0.15625, ((0, 32),))
    shared_in = centred(key_of[10], (D, 2 * SFF), D ** -0.5, 0.21875, ((0, 32),))
    shared_out = centred(key_of[11], (SFF, D), SFF ** -0.5, 0.125, ((0, 32),))
    expert_in = centred(key_of[12], (EXPERTS, D, 2 * FF), D ** -0.5, 0.21875, ((0, 8),))
    expert_out = centred(key_of[13], (EXPERTS, FF, D), FF ** -0.5, 0.125, ((0, 8),))
    return {"layer_input": layer_input, "cotangent": cotangent, "segments": segments, "routes": routes, "order": order, "norm1_gain": norm1_gain, "attn_qkv": attn_qkv, "attn_out": attn_out, "norm2_gain": norm2_gain, "router": router, "shared_in": shared_in, "shared_out": shared_out, "expert_in": expert_in, "expert_out": expert_out}


EPS = 1e-06
HIGH = lax.Precision.HIGHEST
BASE = 10000.0
MASKED = -1e+30

@jax.custom_vjp
def low(v):
    return lax.optimization_barrier(v.astype(jnp.bfloat16)).astype(jnp.float32)

@jax.custom_vjp
def low_back(v):
    return v

def low_keep(v):
    return (low(v), None)

def low_pass(kept, grad):
    return (grad,)

def back_keep(v):
    return (v, None)

def back_low(kept, grad):
    return (low(grad),)
low.defvjp(low_keep, low_pass)
low_back.defvjp(back_keep, back_low)

def swish(values):
    return values * jax.nn.sigmoid(values)

def rotate(values, places, direction):
    half_width = values.shape[-1] // 2
    frequency = BASE ** (-(jnp.arange(half_width, dtype=jnp.float32) * 2.0 / values.shape[-1]))
    bcast_shape = (places.shape[0],) + (1,) * (values.ndim - 1)
    angles = places.astype(jnp.float32).reshape(bcast_shape) * frequency
    cosine = jnp.cos(angles)
    sine_part = jnp.sin(angles) * direction
    leading = values[..., :half_width]
    trailing = values[..., half_width:]
    return jnp.concatenate([leading * cosine - trailing * sine_part, trailing * cosine + leading * sine_part], axis=-1)

def slot_plan(route_ids, ranks, experts, capacity):
    row_count = route_ids.shape[0]
    rank_of = ranks[:, None] + row_count * jnp.arange(2, dtype=jnp.int32)[None, :]
    flat_rank = rank_of.reshape(-1)
    by_rank = jnp.zeros((2 * row_count,), jnp.int32).at[flat_rank].set(route_ids.reshape(-1))
    onehot = (by_rank[:, None] == jnp.arange(experts, dtype=jnp.int32)[None, :]).astype(jnp.int32)
    earlier = jnp.cumsum(onehot, axis=0, dtype=jnp.int32) - onehot
    place_by_rank = lax.optimization_barrier(jnp.sum(earlier * onehot, axis=1, dtype=jnp.int32))
    position = place_by_rank[flat_rank].reshape(row_count, 2)
    slot_of = jnp.where(position < capacity, route_ids * capacity + position, experts * capacity).astype(jnp.int32)
    owner_ids = jnp.full((experts * capacity + 1,), 2 * row_count, jnp.int32)
    owner_ids = owner_ids.at[slot_of.reshape(-1)].set(jnp.arange(2 * row_count, dtype=jnp.int32))
    return (slot_of, owner_ids[:experts * capacity])

def reference(layer_input, cotangent, segments, routes, order, norm1_gain, attn_qkv, attn_out, norm2_gain, router, shared_in, shared_out, expert_in, expert_out):
    blocks = TOKENS // TOK_DEV
    slot_of, owner_ids = jax.vmap(lambda route_ids, ranks: slot_plan(route_ids, ranks, EXPERTS, CAP))(routes.reshape(blocks, TOK_DEV, 2), order.reshape(blocks, TOK_DEV))
    source_rows = owner_ids // 2
    places = jnp.arange(TOKENS, dtype=jnp.int32) % LEN
    qblock = min(512, LEN)
    scale = HD ** (-0.5)
    key_places = jnp.arange(LEN, dtype=jnp.int32)

    def one_sequence(inputs):
        queries, keys_seq, values_seq, doc_ids = inputs

        def one_block(start):
            q_rows = lax.dynamic_slice_in_dim(queries, start, qblock, 0)
            q_places = start + jnp.arange(qblock, dtype=jnp.int32)
            q_docs = lax.dynamic_slice_in_dim(doc_ids, start, qblock, 0)
            scores = low_back(jnp.einsum('qhd,khd->hqk', q_rows, keys_seq, precision=HIGH) * scale)
            allowed = (key_places[None, :] <= q_places[:, None]) & (doc_ids[None, :] == q_docs[:, None])
            scores = jnp.where(allowed[None], scores, MASKED)
            top_score = lax.optimization_barrier(jnp.max(scores, axis=-1, keepdims=True))
            weights = jnp.exp(scores - top_score)
            probs = weights / lax.optimization_barrier(jnp.sum(weights, axis=-1, keepdims=True))
            return jnp.einsum('hqk,khd->qhd', low(probs), values_seq, precision=HIGH)
        starts = jnp.arange(LEN // qblock, dtype=jnp.int32) * qblock
        return lax.map(jax.checkpoint(one_block), starts).reshape(LEN, HEADS, HD)

    def expert_rows(inputs):
        rows, w_in, w_down = inputs
        pre_act = low_back(jnp.dot(rows, w_in, precision=HIGH))
        activity = low(swish(pre_act[:, :FF]) * pre_act[:, FF:])
        return low_back(low(jnp.dot(activity, w_down, precision=HIGH)))

    def forward(tokens, gain_one, w_qkv, w_attn, gain_two, w_router, w_sin, w_sout, w_ein, w_eout):
        rms_one = lax.rsqrt(lax.optimization_barrier(jnp.mean(tokens * tokens, axis=-1, keepdims=True)) + EPS)
        normed = low(tokens * rms_one * gain_one)
        projected = low_back(jnp.dot(normed, w_qkv, precision=HIGH)).reshape(TOKENS, HEADS, 3, HD)
        turned = rotate(projected[:, :, :2], places, 1.0)
        queries = low_back(low(turned[:, :, 0]))
        keys_all = low_back(low(turned[:, :, 1]))
        values_all = low_back(low(projected[:, :, 2]))
        context = lax.map(jax.checkpoint(one_sequence), (queries.reshape(SEQS, LEN, HEADS, HD), keys_all.reshape(SEQS, LEN, HEADS, HD), values_all.reshape(SEQS, LEN, HEADS, HD), segments))
        context = low_back(low(context.reshape(TOKENS, D)))
        hidden = tokens + low_back(jnp.dot(context, w_attn, precision=HIGH))
        rms_two = lax.rsqrt(lax.optimization_barrier(jnp.mean(hidden * hidden, axis=-1, keepdims=True)) + EPS)
        normed_two = low(hidden * rms_two * gain_two)
        logits = low_back(jnp.dot(normed_two, w_router, precision=HIGH))
        chosen = jnp.take_along_axis(logits, routes, axis=1)
        top_logit = lax.optimization_barrier(jnp.max(chosen, axis=-1, keepdims=True))
        expd = jnp.exp(chosen - top_logit)
        gates = expd / lax.optimization_barrier(jnp.sum(expd, axis=-1, keepdims=True))
        shared_pre = low_back(jnp.dot(normed_two, w_sin, precision=HIGH))
        shared_act = low(swish(shared_pre[:, :SFF]) * shared_pre[:, SFF:])
        shared_res = low_back(jnp.dot(shared_act, w_sout, precision=HIGH))
        padded = jnp.concatenate([normed_two.reshape(blocks, TOK_DEV, D), jnp.zeros((blocks, 1, D), jnp.float32)], axis=1)
        dispatched = low_back(jax.vmap(lambda rows, index_rows: rows[index_rows])(padded, source_rows))
        by_expert = dispatched.reshape(blocks, EXPERTS, CAP, D).transpose(1, 0, 2, 3).reshape(EXPERTS, blocks * CAP, D)
        returned = lax.map(jax.checkpoint(expert_rows), (by_expert, w_ein, w_eout))
        returned = returned.reshape(EXPERTS, blocks, CAP, D).transpose(1, 0, 2, 3).reshape(blocks, EXPERTS * CAP, D)
        returned = jnp.concatenate([returned, jnp.zeros((blocks, 1, D), jnp.float32)], axis=1)
        picked = jax.vmap(lambda rows, index_rows: rows[index_rows])(returned, slot_of).reshape(TOKENS, 2, D)
        mixture = lax.optimization_barrier(jnp.sum(gates[:, :, None] * picked, axis=1))
        return hidden + shared_res + mixture
    primals = tuple((arg.astype(jnp.float32) for arg in (layer_input, norm1_gain, attn_qkv, attn_out, norm2_gain, router, shared_in, shared_out, expert_in, expert_out)))
    output, pullback = jax.vjp(forward, *primals)
    grads = pullback(cotangent.astype(jnp.float32))
    return (output, grads[0], grads[1], grads[2], grads[3], grads[4], grads[5], grads[6], grads[7], grads[8], grads[9])
```

```python
import functools

import jax
import jax.numpy as jnp
from jax import lax
from jax.experimental import pallas as pl
from jax.experimental.pallas import tpu as pltpu
from jax.sharding import PartitionSpec as P

HEADS = 12
EPS = 1e-06
BASE = 10000.0
MASKED = -1e30
AXES = ("dp", "seq")
LANES = 128
F32 = jnp.float32
BF16 = jnp.bfloat16
NN = (((1,), (0,)), ((), ()))
NT = (((1,), (1,)), ((), ()))
TN = (((0,), (0,)), ((), ()))


def mm(left, right, dims=NN):
    return lax.dot_general(left, right, dims, preferred_element_type=F32)


def params(steps=0, mib=56):
    semantics = ("arbitrary",) * steps if steps else None
    return pltpu.CompilerParams(dimension_semantics=semantics, vmem_limit_bytes=mib << 20)


def cost(flops, moved):
    return pl.CostEstimate(flops=int(flops), bytes_accessed=int(moved), transcendentals=0)


def whole():
    return pl.BlockSpec(memory_space=pltpu.VMEM)


def pairs(place):
    found = []
    for device in range(32):
        z, y, x, c = device // 8, (device // 4) % 2, (device // 2) % 2, device % 2
        z, y, x, c = place(z, y, x, c)
        found.append((device, ((z * 2 + y) * 2 + x) * 2 + c))
    return found


FLIP = {
    "y": pairs(lambda z, y, x, c: (z, 1 - y, x, c)),
    "x": pairs(lambda z, y, x, c: (z, y, 1 - x, c)),
    "c": pairs(lambda z, y, x, c: (z, y, x, 1 - c)),
}


def turn_z(step):
    return pairs(lambda z, y, x, c: ((z + step) % 4, y, x, c))


def coordinates():
    dp, seq = lax.axis_index("dp"), lax.axis_index("seq")
    return {"z": dp // 2, "y": dp % 2, "x": seq // 2, "c": seq % 2}


def small_torus():
    return lax.axis_size("dp") == 8 and lax.axis_size("seq") == 4


def gather(shard, path):
    if not small_torus():
        return lax.all_gather(shard, AXES, axis=0, tiled=True)
    here = coordinates()
    block, done = shard, []
    for name in path:
        axis = sum(1 for other in done if "zyxc".index(other) < "zyxc".index(name))
        if name == "z":
            grown = jnp.zeros(block.shape[:axis] + (4,) + block.shape[axis:], block.dtype)
            parts = [(here["z"], block)]
            for step in (2, 1, 3):
                came = lax.ppermute(block, AXES, turn_z(-step))
                parts.append(((here["z"] + step) % 4, came))
            for place, part in parts:
                grown = lax.dynamic_update_slice_in_dim(
                    grown, jnp.expand_dims(part, axis), place, axis
                )
            block = grown
        else:
            came = lax.ppermute(block, AXES, FLIP[name])
            block = jnp.where(
                here[name] == 0,
                jnp.stack([block, came], axis),
                jnp.stack([came, block], axis),
            )
        done.append(name)
    return block.reshape((-1,) + shard.shape[1:])


def scatter_sum(grad, path):
    devices = lax.axis_size("dp") * lax.axis_size("seq")
    if not small_torus():
        return lax.psum_scatter(grad, AXES, scatter_dimension=0, tiled=True).astype(F32)
    here = coordinates()
    part = grad.reshape((4, 2, 2, 2, grad.shape[0] // devices) + grad.shape[1:])
    dims = list("zyxc")
    for count, name in enumerate(path):
        axis = dims.index(name)
        if name == "z":
            total = lax.dynamic_index_in_dim(part, here["z"], axis, False).astype(F32)
            for step in (2, 1, 3):
                away = lax.dynamic_index_in_dim(part, (here["z"] + step) % 4, axis, False)
                total = total + lax.ppermute(away, AXES, turn_z(step)).astype(F32)
        else:
            away = lax.dynamic_index_in_dim(part, 1 - here[name], axis, False)
            kept = lax.dynamic_index_in_dim(part, here[name], axis, False)
            total = kept.astype(F32) + lax.ppermute(away, AXES, FLIP[name]).astype(F32)
        part = total if count == 3 else total.astype(BF16)
        dims.pop(axis)
    return part


def copies_sum(parts):
    seq = lax.axis_size("seq")
    if not small_torus():
        flat = parts.reshape((seq * parts.shape[1],) + parts.shape[2:])
        return lax.psum_scatter(flat, "seq", scatter_dimension=0, tiled=True).astype(F32)
    here = coordinates()
    part = parts.reshape((2, 2) + parts.shape[1:])
    away = lax.dynamic_index_in_dim(part, 1 - here["c"], 1, False)
    kept = lax.dynamic_index_in_dim(part, here["c"], 1, False)
    part = (kept.astype(F32) + lax.ppermute(away, AXES, FLIP["c"]).astype(F32)).astype(BF16)
    away = lax.dynamic_index_in_dim(part, 1 - here["x"], 0, False)
    kept = lax.dynamic_index_in_dim(part, here["x"], 0, False)
    return kept.astype(F32) + lax.ppermute(away, AXES, FLIP["x"]).astype(F32)


def swap(blocks, axis):
    return lax.all_to_all(blocks, axis, split_axis=0, concat_axis=0, tiled=True)


def turned(rows, cosine, sine):
    a, b = rows[:32], rows[32:]
    return a * cosine - b * sine, b * cosine + a * sine


def qkv_kernel(x_ref, w1_ref, w2_ref, misc_ref, cos_ref, sin_ref, out_ref, xn_ref):
    step = pl.program_id(0)

    @pl.when(step == 0)
    def _():
        x = x_ref[...].astype(F32)
        r1 = lax.rsqrt(jnp.mean(x * x, axis=1, keepdims=True) + EPS)
        gain = misc_ref[...].astype(F32).T[0:1, :]
        xn_ref[...] = (x * r1 * gain).astype(BF16)

    def project(w_ref):
        rows = mm(xn_ref[...], w_ref[...]).T
        cosine, sine = cos_ref[...], sin_ref[...]
        for base in range(0, rows.shape[0], 192):
            for c in range(2):
                at = base + c * 64
                a, b = turned(rows[at : at + 64], cosine, sine)
                out_ref[at : at + 32, :] = a.astype(BF16)
                out_ref[at + 32 : at + 64, :] = b.astype(BF16)
            out_ref[base + 128 : base + 192, :] = rows[base + 128 : base + 192].astype(BF16)

    @pl.when(step < 3)
    def _():
        project(w1_ref)

    @pl.when(step >= 3)
    def _():
        project(w2_ref)


def qkv_project(x, w1, w2, cosine, sine):
    tokens, width = x.shape
    return pl.pallas_call(
        qkv_kernel,
        grid=(6,),
        in_specs=[
            pl.BlockSpec((tokens, width), lambda i: (0, 0)),
            pl.BlockSpec((width, 384), lambda i: (0, jnp.minimum(i, 2))),
            pl.BlockSpec((width, 384), lambda i: (0, jnp.maximum(i - 3, 0))),
            pl.BlockSpec((width, LANES), lambda i: (0, 9)),
            pl.BlockSpec(cosine.shape, lambda i: (0, 0)),
            pl.BlockSpec(sine.shape, lambda i: (0, 0)),
        ],
        out_specs=pl.BlockSpec((384, tokens), lambda i: (i, 0)),
        out_shape=jax.ShapeDtypeStruct((3 * width, tokens), BF16),
        scratch_shapes=[pltpu.VMEM((tokens, width), BF16)],
        compiler_params=params(1),
        cost_estimate=cost(6 * tokens * width * width, 8 << 20),
        name="qkv_project",
    )(x, w1, w2, w2, cosine, sine)


TILE = 256


def tile_of(ref, row, rows, index):
    per = ref.shape[2] // TILE
    at = (index % per) * TILE
    return ref[index // per, row : row + rows, at : at + TILE]


def flipped(block):
    return block.astype(F32).T.astype(BF16)


def masked(scores, start, i, j, diagonal):
    key = lax.broadcasted_iota(jnp.int32, scores.shape, 0)
    allowed = key >= start - j * TILE
    if diagonal:
        query = lax.broadcasted_iota(jnp.int32, scores.shape, 1)
        allowed = allowed & (key <= query)
    return jnp.where(allowed, scores, MASKED)


def attend_kernel(buf_ref, start_ref, ctx_ref, lse_ref, k_ref, s_ref):
    tiles = buf_ref.shape[0] * buf_ref.shape[2] // TILE
    per = buf_ref.shape[2] // TILE
    for i in range(tiles):
        rows = slice(i * TILE, (i + 1) * TILE)
        k_ref[rows, :] = flipped(tile_of(buf_ref, 64, 64, i))
        q = (tile_of(buf_ref, 0, 64, i).astype(F32) * 0.125).astype(BF16)
        start = start_ref[0:1, rows]
        top = jnp.full((1, TILE), MASKED, F32)
        for j in range(i + 1):
            keys = slice(j * TILE, (j + 1) * TILE)
            scores = masked(mm(k_ref[keys, :], q), start, i, j, i == j)
            s_ref[keys, :] = scores
            top = jnp.maximum(top, jnp.max(scores, axis=0, keepdims=True))
        total = jnp.zeros((1, TILE), F32)
        context = jnp.zeros((64, TILE), F32)
        for j in range(i + 1):
            probs = jnp.exp(s_ref[j * TILE : (j + 1) * TILE, :] - top)
            total = total + jnp.sum(probs, axis=0, keepdims=True)
            context = context + mm(tile_of(buf_ref, 128, 64, j), probs.astype(BF16))
        at = (i % per) * TILE
        ctx_ref[i // per, :, at : at + TILE] = (context / total).astype(BF16)
        lse_ref[0, 0:1, rows] = top + jnp.log(total)


def attend(buf, start):
    blocks, rows, tokens = buf.shape
    heads, length = rows // 192, blocks * tokens
    return pl.pallas_call(
        attend_kernel,
        grid=(heads,),
        in_specs=[
            pl.BlockSpec((blocks, 192, tokens), lambda h: (0, h, 0)),
            pl.BlockSpec((1, length), lambda h: (0, 0)),
        ],
        out_specs=[
            pl.BlockSpec((blocks, 64, tokens), lambda h: (0, h, 0)),
            pl.BlockSpec((1, 1, length), lambda h: (h, 0, 0)),
        ],
        out_shape=[
            jax.ShapeDtypeStruct((blocks, heads * 64, tokens), BF16),
            jax.ShapeDtypeStruct((heads, 1, length), F32),
        ],
        scratch_shapes=[pltpu.VMEM((length, 64), BF16), pltpu.VMEM((length, TILE), F32)],
        compiler_params=params(1),
        cost_estimate=cost(20e9, 4 << 20),
        name="attend",
    )(buf, start)


def attend_back_kernel(
    buf_ref, dctx_ref, ctx_ref, lse_ref, start_ref, out_ref, k_ref, v_ref, q_ref, d_ref, dk_ref, dv_ref
):
    tiles = buf_ref.shape[0] * buf_ref.shape[2] // TILE
    per = buf_ref.shape[2] // TILE
    for i in range(tiles):
        rows = slice(i * TILE, (i + 1) * TILE)
        k_ref[rows, :] = flipped(tile_of(buf_ref, 64, 64, i))
        v_ref[rows, :] = flipped(tile_of(buf_ref, 128, 64, i))
        q_t = (tile_of(buf_ref, 0, 64, i).astype(F32) * 0.125).astype(BF16)
        d_t = tile_of(dctx_ref, 0, 64, i)
        q_rows, d_rows = flipped(q_t), flipped(d_t)
        delta = jnp.sum(
            d_t.astype(F32) * tile_of(ctx_ref, 0, 64, i).astype(F32), axis=0, keepdims=True
        )
        start, log_total = start_ref[0:1, rows], lse_ref[0, 0:1, rows]
        d_query = jnp.zeros((64, TILE), F32)
        for j in range(i + 1):
            keys = slice(j * TILE, (j + 1) * TILE)
            scores = masked(mm(k_ref[keys, :], q_t), start, i, j, i == j)
            probs = jnp.exp(scores - log_total)
            d_probs = mm(v_ref[keys, :], d_t)
            d_scores = (probs * (d_probs - delta)).astype(BF16)
            d_query = d_query + mm(tile_of(buf_ref, 64, 64, j), d_scores)
            d_key = mm(d_scores, q_rows)
            d_value = mm(probs.astype(BF16), d_rows)
            if i == j:
                dk_ref[keys, :] = d_key
                dv_ref[keys, :] = d_value
            else:
                dk_ref[keys, :] += d_key
                dv_ref[keys, :] += d_value
        at = (i % per) * TILE
        out_ref[i // per, 0:64, at : at + TILE] = (d_query * 0.125).astype(BF16)
    for i in range(tiles):
        at = (i % per) * TILE
        rows = slice(i * TILE, (i + 1) * TILE)
        out_ref[i // per, 64:128, at : at + TILE] = dk_ref[rows, :].T.astype(BF16)
        out_ref[i // per, 128:192, at : at + TILE] = dv_ref[rows, :].T.astype(BF16)


def attend_back(buf, dctx, ctx, lse, start):
    blocks, rows, tokens = buf.shape
    heads, length = rows // 192, blocks * tokens
    return pl.pallas_call(
        attend_back_kernel,
        grid=(heads,),
        in_specs=[
            pl.BlockSpec((blocks, 192, tokens), lambda h: (0, h, 0)),
            pl.BlockSpec((blocks, 64, tokens), lambda h: (0, h, 0)),
            pl.BlockSpec((blocks, 64, tokens), lambda h: (0, h, 0)),
            pl.BlockSpec((1, 1, length), lambda h: (h, 0, 0)),
            pl.BlockSpec((1, length), lambda h: (0, 0)),
        ],
        out_specs=pl.BlockSpec((blocks, 192, tokens), lambda h: (0, h, 0)),
        out_shape=jax.ShapeDtypeStruct(buf.shape, BF16),
        scratch_shapes=[pltpu.VMEM((length, 64), BF16)] * 2
        + [pltpu.VMEM((TILE, 64), BF16)] * 2
        + [pltpu.VMEM((length, 64), F32)] * 2,
        compiler_params=params(1),
        cost_estimate=cost(40e9, 6 << 20),
        name="attend_back",
    )(buf, dctx, ctx, lse, start)


def middle_kernel(
    ctx_ref, x_ref, w_ref, misc_ref, pick_ref, routes_ref, hidden_ref, hn_ref, send_ref, gates_ref, *, experts
):
    hidden = x_ref[...].astype(F32) + mm(ctx_ref[...], w_ref[...], TN)
    hidden_ref[...] = hidden
    r2 = lax.rsqrt(jnp.mean(hidden * hidden, axis=1, keepdims=True) + EPS)
    gain = misc_ref[...].astype(F32).T[experts : experts + 1, :]
    hn = (hidden * r2 * gain).astype(BF16)
    hn_ref[...] = hn
    send_ref[...] = mm(pick_ref[...], hn).astype(BF16)
    logits = mm(hn, misc_ref[...])
    lane = lax.broadcasted_iota(jnp.int32, logits.shape, 1)
    first = jnp.sum(jnp.where(lane == routes_ref[:, 0:1], logits, 0.0), axis=1, keepdims=True)
    second = jnp.sum(jnp.where(lane == routes_ref[:, 1:2], logits, 0.0), axis=1, keepdims=True)
    top = jnp.maximum(first, second)
    first, second = jnp.exp(first - top), jnp.exp(second - top)
    total = first + second
    gates_ref[...] = jnp.where(lane == 0, first / total, jnp.where(lane == 1, second / total, 0.0))


def middle(ctx, x, w_attn, misc, pick, routes, experts):
    tokens, width = x.shape
    slots = pick.shape[0]
    return pl.pallas_call(
        functools.partial(middle_kernel, experts=experts),
        in_specs=[whole()] * 6,
        out_specs=[whole()] * 4,
        out_shape=[
            jax.ShapeDtypeStruct((tokens, width), F32),
            jax.ShapeDtypeStruct((tokens, width), BF16),
            jax.ShapeDtypeStruct((slots, width), BF16),
            jax.ShapeDtypeStruct((tokens, LANES), F32),
        ],
        compiler_params=params(),
        cost_estimate=cost(2e9, 8 << 20),
        name="middle",
    )(ctx, x, w_attn, misc, pick, routes)


def swiglu(gate, up, d_act):
    sigma = jax.nn.sigmoid(gate)
    act = (gate * sigma * up).astype(BF16)
    d_gate = (d_act * up * sigma * (1.0 + gate * (1.0 - sigma))).astype(BF16)
    d_up = (d_act * gate * sigma).astype(BF16)
    return act, d_gate, d_up


def dense_kernel(
    x_ref, dy_ref, wg_ref, wu_ref, wo_ref, y_ref, dx_ref, gg_ref, gu_ref, go_ref, xt_ref
):
    @pl.when(pl.program_id(0) == 0)
    def _():
        y_ref[...] = jnp.zeros_like(y_ref)
        dx_ref[...] = jnp.zeros_like(dx_ref)
        xt_ref[...] = flipped(x_ref[...])

    x, dy = x_ref[...], dy_ref[...]
    act, d_gate, d_up = swiglu(mm(x, wg_ref[...]), mm(x, wu_ref[...]), mm(dy, wo_ref[...], NT))
    y_ref[...] += mm(act, wo_ref[...])
    dx_ref[...] += mm(d_gate, wg_ref[...], NT) + mm(d_up, wu_ref[...], NT)
    gg_ref[...] = mm(xt_ref[...], d_gate).astype(BF16)
    gu_ref[...] = mm(xt_ref[...], d_up).astype(BF16)
    go_ref[...] = mm(act, dy, TN).astype(BF16)


def dense(x, dy, w_gate, w_up, w_out, tile=256):
    tokens, width = x.shape
    units = w_out.shape[0]
    rows = pl.BlockSpec((tokens, width), lambda j: (0, 0))
    tall = pl.BlockSpec((width, tile), lambda j: (0, j))
    wide = pl.BlockSpec((tile, width), lambda j: (j, 0))
    return pl.pallas_call(
        dense_kernel,
        grid=(units // tile,),
        in_specs=[rows, rows, tall, tall, wide],
        out_specs=[rows, rows, tall, tall, wide],
        out_shape=[
            jax.ShapeDtypeStruct((tokens, width), F32),
            jax.ShapeDtypeStruct((tokens, width), F32),
            jax.ShapeDtypeStruct((width, units), BF16),
            jax.ShapeDtypeStruct((width, units), BF16),
            jax.ShapeDtypeStruct((units, width), BF16),
        ],
        scratch_shapes=[pltpu.VMEM((width, tokens), BF16)],
        compiler_params=params(1),
        cost_estimate=cost(18 * tokens * width * units, 30 << 20),
        name="dense",
    )(x, dy, w_gate, w_up, w_out)


def expert_kernel(
    own_ref, x_ref, dy_ref, other_ref, misc_ref, wg_ref, wu_ref, wo_ref,
    y_ref, dx_ref, dgate_ref, deo_ref, act_ref, dg_ref, du_ref, y_acc, dx_acc,
):
    step = pl.program_id(0)

    @pl.when(step == 0)
    def _():
        y_acc[...] = jnp.zeros_like(y_acc)
        dx_acc[...] = jnp.zeros_like(dx_acc)
        logits = mm(x_ref[...], misc_ref[...])
        lane = lax.broadcasted_iota(jnp.int32, logits.shape, 1)
        other = other_ref[...].astype(jnp.int32)
        mine = jnp.sum(jnp.where(lane == own_ref[0], logits, 0.0), axis=1, keepdims=True)
        theirs = jnp.sum(jnp.where(lane == other, logits, 0.0), axis=1, keepdims=True)
        top = jnp.maximum(mine, theirs)
        mine, theirs = jnp.exp(mine - top), jnp.exp(theirs - top)
        deo_ref[...] = (mine / (mine + theirs) * dy_ref[...].astype(F32)).astype(BF16)

    x, deo = x_ref[...], deo_ref[...]
    wg, wu, wo = wg_ref[0], wu_ref[0], wo_ref[0]
    act, d_gate, d_up = swiglu(mm(x, wg), mm(x, wu), mm(deo, wo, NT))
    y_acc[...] += mm(act, wo)
    dx_acc[...] += mm(d_gate, wg, NT) + mm(d_up, wu, NT)
    act_ref[...] = act
    dg_ref[...] = d_gate
    du_ref[...] = d_up

    @pl.when(step == pl.num_programs(0) - 1)
    def _():
        y = y_acc[...].astype(BF16)
        y_ref[...] = y
        dx_ref[...] = dx_acc[...].astype(BF16)
        dgate_ref[...] = jnp.sum(y.astype(F32) * dy_ref[...].astype(F32), axis=1, keepdims=True)


def expert(own, x, dy, other, misc, w_in, w_out, tile=256):
    slots, width = x.shape
    units = w_out.shape[1]
    steps = units // tile
    rows = pl.BlockSpec((slots, width), lambda j, s: (0, 0))
    column = pl.BlockSpec((slots, 1), lambda j, s: (0, 0))
    saved = pl.BlockSpec((slots, tile), lambda j, s: (0, j))
    return pl.pallas_call(
        expert_kernel,
        grid_spec=pltpu.PrefetchScalarGridSpec(
            num_scalar_prefetch=1,
            grid=(steps,),
            in_specs=[
                rows,
                rows,
                column,
                pl.BlockSpec(misc.shape, lambda j, s: (0, 0)),
                pl.BlockSpec((1, width, tile), lambda j, s: (0, 0, j)),
                pl.BlockSpec((1, width, tile), lambda j, s: (0, 0, j + steps)),
                pl.BlockSpec((1, tile, width), lambda j, s: (0, j, 0)),
            ],
            out_specs=[rows, rows, column, rows, saved, saved, saved],
            scratch_shapes=[pltpu.VMEM((slots, width), F32)] * 2,
        ),
        out_shape=[
            jax.ShapeDtypeStruct((slots, width), BF16),
            jax.ShapeDtypeStruct((slots, width), BF16),
            jax.ShapeDtypeStruct((slots, 1), F32),
            jax.ShapeDtypeStruct((slots, width), BF16),
        ]
        + [jax.ShapeDtypeStruct((slots, units), BF16)] * 3,
        compiler_params=params(1),
        cost_estimate=cost(12 * slots * width * units, 40 << 20),
        name="expert",
    )(own, x, dy, other, misc, w_in, w_in, w_out)


def expert_grads_kernel(x_ref, deo_ref, act_ref, dg_ref, du_ref, gg_ref, gu_ref, go_ref, xt_ref):
    @pl.when(pl.program_id(0) == 0)
    def _():
        xt_ref[...] = flipped(x_ref[...])

    gg_ref[0] = mm(xt_ref[...], dg_ref[...]).astype(BF16)
    gu_ref[0] = mm(xt_ref[...], du_ref[...]).astype(BF16)
    go_ref[0] = mm(act_ref[...], deo_ref[...], TN).astype(BF16)


def expert_grads(x, deo, act, d_gate, d_up, copies, tile=256):
    slots, width = x.shape
    units = act.shape[1]
    rows = pl.BlockSpec((slots, width), lambda j: (0, 0))
    saved = pl.BlockSpec((slots, tile), lambda j: (0, j))
    in_part, out_part = 2 * units // copies, units // copies
    in_steps, out_steps = in_part // tile, out_part // tile
    in_spec = pl.BlockSpec((1, width, tile), lambda j: (j // in_steps, 0, j % in_steps))
    return pl.pallas_call(
        expert_grads_kernel,
        grid=(units // tile,),
        in_specs=[rows, rows, saved, saved, saved],
        out_specs=[
            in_spec,
            in_spec,
            pl.BlockSpec((1, tile, width), lambda j: (j // out_steps, j % out_steps, 0)),
        ],
        out_shape=[
            jax.ShapeDtypeStruct((copies // 2, width, in_part), BF16),
            jax.ShapeDtypeStruct((copies // 2, width, in_part), BF16),
            jax.ShapeDtypeStruct((copies, out_part, width), BF16),
        ],
        scratch_shapes=[pltpu.VMEM((width, slots), BF16)],
        compiler_params=params(1),
        cost_estimate=cost(6 * slots * width * units, 30 << 20),
        name="expert_grads",
    )(x, deo, act, d_gate, d_up)


def middle_back_kernel(
    dhn_ref, back_ref, slots_ref, routes_ref, dgate_ref, gates_ref, misc_ref, hidden_ref, hn_ref,
    dy_ref, ctx_ref, w_ref, dh_ref, dctx_ref, grad_ref, *, experts,
):
    tokens = dhn_ref.shape[0]
    slots = back_ref.shape[0]
    place = lax.broadcasted_iota(jnp.int32, (tokens, slots), 1)
    is0, is1 = place == slots_ref[:, 0:1], place == slots_ref[:, 1:2]
    came = mm(jnp.where(is0 | is1, 1.0, 0.0).astype(BF16), back_ref[...])
    dgate = dgate_ref[...]
    dg0 = jnp.sum(jnp.where(is0, dgate, 0.0), axis=1, keepdims=True)
    dg1 = jnp.sum(jnp.where(is1, dgate, 0.0), axis=1, keepdims=True)
    g0, g1 = gates_ref[:, 0:1], gates_ref[:, 1:2]
    mean = g0 * dg0 + g1 * dg1
    lane = lax.broadcasted_iota(jnp.int32, (tokens, LANES), 1)
    dlogits = (
        jnp.where(lane == routes_ref[:, 0:1], g0 * (dg0 - mean), 0.0)
        + jnp.where(lane == routes_ref[:, 1:2], g1 * (dg1 - mean), 0.0)
    ).astype(BF16)
    misc = misc_ref[...]
    dhn = dhn_ref[...] + mm(dlogits, misc, NT) + came
    hidden = hidden_ref[...]
    r2 = lax.rsqrt(jnp.mean(hidden * hidden, axis=1, keepdims=True) + EPS)
    z2 = hidden * r2
    gain = misc.astype(F32).T[experts : experts + 1, :]
    gain_grad = jnp.sum(dhn * z2, axis=0, keepdims=True)
    dz2 = dhn * gain
    dh = dy_ref[...].astype(F32) + r2 * (dz2 - z2 * jnp.mean(dz2 * z2, axis=1, keepdims=True))
    dh_ref[...] = dh
    dhb = dh.astype(BF16)
    dctx_ref[...] = mm(w_ref[...], dhb, NT).astype(BF16)
    width = w_ref.shape[0]
    grad_ref[:, :width] = mm(ctx_ref[...], dhb).astype(BF16)
    small = mm(dlogits, hn_ref[...], TN)
    row = lax.broadcasted_iota(jnp.int32, small.shape, 0)
    small = jnp.where(row == experts, gain_grad, small)
    grad_ref[:, width:] = small.T.astype(BF16)


def middle_back(dhn, back, slots, routes, dgate, gates, misc, hidden, hn, dy, ctx, w_attn, experts):
    tokens, width = hidden.shape
    return pl.pallas_call(
        functools.partial(middle_back_kernel, experts=experts),
        in_specs=[whole()] * 12,
        out_specs=[whole()] * 3,
        out_shape=[
            jax.ShapeDtypeStruct((tokens, width), F32),
            jax.ShapeDtypeStruct((width, tokens), BF16),
            jax.ShapeDtypeStruct((width, width + LANES), BF16),
        ],
        compiler_params=params(),
        cost_estimate=cost(3e9, 16 << 20),
        name="middle_back",
    )(dhn, back, slots, routes, dgate, gates, misc, hidden, hn, dy, ctx, w_attn)


def output_kernel(hidden_ref, dense_ref, came_ref, slots_ref, gates_ref, out_ref):
    tokens, slots = hidden_ref.shape[0], came_ref.shape[0]
    place = lax.broadcasted_iota(jnp.int32, (tokens, slots), 1)
    mixture = jnp.zeros(hidden_ref.shape, F32)
    for k in range(2):
        pick = jnp.where(place == slots_ref[:, k : k + 1], 1.0, 0.0).astype(BF16)
        mixture = mixture + gates_ref[:, k : k + 1] * mm(pick, came_ref[...])
    out_ref[...] = hidden_ref[...] + dense_ref[...] + mixture


def output_of(hidden, shared, came, slots, gates):
    return pl.pallas_call(
        output_kernel,
        in_specs=[whole()] * 5,
        out_specs=whole(),
        out_shape=jax.ShapeDtypeStruct(hidden.shape, F32),
        compiler_params=params(),
        cost_estimate=cost(2e9, 8 << 20),
        name="output_of",
    )(hidden, shared, came, slots, gates)


def qkv_back_kernel(
    x_ref, dqkv_ref, w1_ref, w2_ref, misc_ref, cos_ref, sin_ref, dh_ref,
    dx_ref, g1_ref, g2_ref, small_ref, xt_ref, acc_ref,
):
    step = pl.program_id(0)

    def gain_row():
        return misc_ref[...].astype(F32).T[0:1, :]

    def z_of():
        x = x_ref[...].astype(F32)
        r1 = lax.rsqrt(jnp.mean(x * x, axis=1, keepdims=True) + EPS)
        return x * r1, r1

    @pl.when(step == 0)
    def _():
        z1, _ = z_of()
        xt_ref[...] = flipped((z1 * gain_row()).astype(BF16))
        acc_ref[...] = jnp.zeros_like(acc_ref)

    cosine, sine = cos_ref[...], -sin_ref[...]
    pieces = []
    for base in range(0, dqkv_ref.shape[0], 192):
        for c in range(2):
            at = base + c * 64
            pieces.extend(turned(dqkv_ref[at : at + 64, :].astype(F32), cosine, sine))
        pieces.append(dqkv_ref[base + 128 : base + 192, :].astype(F32))
    d_rows = jnp.concatenate(pieces, axis=0).T.astype(BF16)

    def back(w_ref, g_ref):
        acc_ref[...] += mm(d_rows, w_ref[...], NT)
        g_ref[...] = mm(xt_ref[...], d_rows).astype(BF16)

    @pl.when(step < 3)
    def _():
        back(w1_ref, g1_ref)

    @pl.when(step >= 3)
    def _():
        back(w2_ref, g2_ref)

    @pl.when(step == 5)
    def _():
        z1, r1 = z_of()
        dxn = acc_ref[...]
        total = jnp.sum(dxn * z1, axis=0, keepdims=True)
        row = lax.broadcasted_iota(jnp.int32, (LANES, total.shape[1]), 0)
        small_ref[...] = jnp.where(row == 0, total, 0.0).T.astype(BF16)
        dz1 = dxn * gain_row()
        dx_ref[...] = dh_ref[...] + r1 * (dz1 - z1 * jnp.mean(dz1 * z1, axis=1, keepdims=True))


def qkv_back(x, dqkv, w1, w2, cosine, sine, dh):
    tokens, width = x.shape
    rows = pl.BlockSpec((tokens, width), lambda i: (0, 0))
    half = 3 * width // 2
    return pl.pallas_call(
        qkv_back_kernel,
        grid=(6,),
        in_specs=[
            rows,
            pl.BlockSpec((384, tokens), lambda i: (i, 0)),
            pl.BlockSpec((width, 384), lambda i: (0, jnp.minimum(i, 2))),
            pl.BlockSpec((width, 384), lambda i: (0, jnp.maximum(i - 3, 0))),
            pl.BlockSpec((width, LANES), lambda i: (0, 9)),
            pl.BlockSpec(cosine.shape, lambda i: (0, 0)),
            pl.BlockSpec(sine.shape, lambda i: (0, 0)),
            rows,
        ],
        out_specs=[
            rows,
            pl.BlockSpec((width, 384), lambda i: (0, jnp.minimum(i, 2))),
            pl.BlockSpec((width, 384), lambda i: (0, jnp.maximum(i - 3, 0))),
            pl.BlockSpec((width, LANES), lambda i: (0, 0)),
        ],
        out_shape=[
            jax.ShapeDtypeStruct((tokens, width), F32),
            jax.ShapeDtypeStruct((width, half), BF16),
            jax.ShapeDtypeStruct((width, half), BF16),
            jax.ShapeDtypeStruct((width, LANES), BF16),
        ],
        scratch_shapes=[pltpu.VMEM((width, tokens), BF16), pltpu.VMEM((tokens, width), F32)],
        compiler_params=params(1),
        cost_estimate=cost(12 * tokens * width * width, 16 << 20),
        name="qkv_back",
    )(x, dqkv, w1, w2, w2, cosine, sine, dh)


def slot_plan(routes, order, experts, capacity):
    before = (order[:, None] > order[None, :]).astype(BF16)
    ids = jnp.arange(experts, dtype=jnp.int32)
    first = (routes[:, 0:1] == ids).astype(BF16)
    second = (routes[:, 1:2] == ids).astype(BF16)
    earlier = mm(before, jnp.concatenate([first, second], axis=1))
    every = jnp.sum(first.astype(F32), axis=0, keepdims=True)
    place0 = jnp.sum(earlier[:, :experts] * first.astype(F32), axis=1)
    place1 = jnp.sum((earlier[:, experts:] + every) * second.astype(F32), axis=1)
    place = jnp.stack([place0, place1], axis=1).astype(jnp.int32)
    return jnp.where(place < capacity, routes * capacity + place, experts * capacity)


def padded(shard, columns):
    return jnp.pad(shard, ((0, 0), (0, columns - shard.shape[1])))


def on_device(
    layer_input, cotangent, segments, routes, order, norm1_gain, attn_qkv, attn_out,
    norm2_gain, router, shared_in, shared_out, expert_in, expert_out,
):
    tokens, width = layer_input.shape
    seq_devs = lax.axis_size("seq")
    experts = lax.axis_size("dp")
    capacity = max(2, (18 * tokens + 8 * experts - 1) // (8 * experts))
    slots = experts * capacity
    half = 3 * width // 2
    units = shared_in.shape[1] // 2

    w1 = gather(attn_qkv[:, :half], "zyxc")
    w2 = gather(
        jnp.concatenate([attn_qkv[:, half:], padded(norm1_gain[:, None], LANES)], axis=1), "zxyc"
    )
    gate_shard, up_shard, out_shard, w1, w2 = lax.optimization_barrier(
        (
            shared_in[:, :units],
            jnp.concatenate(
                [
                    shared_in[:, units:],
                    attn_out,
                    padded(jnp.concatenate([router, norm2_gain[:, None]], axis=1), LANES),
                ],
                axis=1,
            ),
            shared_out,
            w1,
            w2,
        )
    )
    w_up = gather(up_shard, "zxyc")
    w_gate = gather(gate_shard, "zyxc")
    w_out = gather(out_shard, "zxyc")
    w_attn = w_up[:, units : units + width]
    misc = w_up[:, units + width :]

    slot_of = slot_plan(routes, order, experts, capacity)
    every_slot = jnp.arange(slots, dtype=jnp.int32)[:, None]
    slot_rows = slot_of.T
    in0, in1 = every_slot == slot_rows[0:1], every_slot == slot_rows[1:2]
    pick = (in0 | in1).astype(BF16)
    routes_f = routes.astype(F32)
    other = jnp.sum(
        jnp.where(in0, routes_f[:, 1][None, :], 0.0) + jnp.where(in1, routes_f[:, 0][None, :], 0.0),
        axis=1,
    )
    dy_send = mm(pick, cotangent).astype(BF16)
    dy_send, other, w1 = lax.optimization_barrier((dy_send, other, w1))
    dy_rows = swap(dy_send.reshape(experts, capacity, width), "dp").reshape(slots, width)
    other = swap(other.reshape(experts, capacity), "dp").reshape(slots, 1)

    frequency = BASE ** (-(jnp.arange(32, dtype=F32) * 2.0 / 64))
    places = lax.axis_index("seq") * tokens + jnp.arange(tokens, dtype=jnp.int32)
    angles = places.astype(F32)[None, :] * frequency[:, None]
    cosine, sine = jnp.cos(angles), jnp.sin(angles)
    docs = segments[0]
    start = jnp.zeros_like(docs)
    for doc in range(1, 4):
        start = jnp.where(docs >= doc, jnp.sum((docs < doc).astype(jnp.int32)), start)
    start = start[None, :]
    qkv = qkv_project(layer_input, w1, w2, cosine, sine)
    heads = swap(qkv.reshape(seq_devs, -1, tokens), "seq")
    ctx_heads, log_totals = attend(heads, start)
    ctx = swap(ctx_heads, "seq").reshape(width, tokens)
    hidden, hn, send, gates = middle(ctx, layer_input, w_attn, misc, pick, routes, experts)

    rows = swap(send.reshape(experts, capacity, width), "dp").reshape(slots, width)
    shared, dhn, grad_gate, grad_up, grad_out = dense(hn, cotangent, w_gate, w_up, w_out)
    own = lax.axis_index("dp").astype(jnp.int32)[None]
    eo, dxe, dgate, deo, act, d_gate, d_up = expert(
        own, rows, dy_rows, other, misc, expert_in, expert_out
    )
    dgate = swap(dgate.reshape(experts, capacity), "dp").reshape(1, slots)
    back = swap(dxe.reshape(experts, capacity, width), "dp").reshape(slots, width)
    ein_gate, ein_up, ein_out = expert_grads(rows, deo, act, d_gate, d_up, seq_devs)
    dh, dctx, grad_attn = middle_back(
        dhn, back, slot_of, routes, dgate, gates, misc, hidden, hn, cotangent, ctx, w_attn, experts
    )

    dctx_heads = swap(dctx.reshape(seq_devs, -1, tokens), "seq")
    d_heads = attend_back(heads, dctx_heads, ctx_heads, log_totals, start)
    came = swap(eo.reshape(experts, capacity, width), "dp").reshape(slots, width)
    layer_output = output_of(hidden, shared, came, slot_of, gates)
    dqkv = swap(d_heads, "seq").reshape(3 * width, tokens)
    input_grad, grad_q1, grad_q2, grad_small = qkv_back(
        layer_input, dqkv, w1, w2, cosine, sine, dh
    )

    ein_part = copies_sum(jnp.concatenate([ein_gate, ein_up], axis=0))
    eout_part = copies_sum(ein_out)
    sum_gate = scatter_sum(grad_gate, "cxyz")
    sum_up = scatter_sum(grad_up, "cyxz")
    sum_out = scatter_sum(grad_out, "cxyz")
    sum_attn = scatter_sum(grad_attn, "cyxz")
    sum_q1 = scatter_sum(grad_q1, "cxyz")
    sum_q2 = scatter_sum(jnp.concatenate([grad_q2, grad_small], axis=1), "cyxz")
    return (
        layer_output,
        input_grad,
        sum_q2[:, half],
        jnp.concatenate([sum_q1, sum_q2[:, :half]], axis=1),
        sum_attn[:, :width],
        sum_attn[:, width + experts],
        sum_attn[:, width : width + experts],
        jnp.concatenate([sum_gate, sum_up], axis=1),
        sum_out,
        ein_part[None],
        eout_part[None],
    )


def solution(mesh):
    rows = P(AXES, None)
    return jax.shard_map(
        on_device,
        mesh=mesh,
        in_specs=(
            rows, rows, P("dp", None), rows, P(AXES), P(AXES), rows, rows,
            P(AXES), rows, rows, rows, P("dp", None, None), P("dp", None, None),
        ),
        out_specs=(
            rows, rows, P(AXES), rows, rows, P(AXES), rows, rows, rows,
            P("dp", None, "seq"), P("dp", "seq", None),
        ),
        check_vma=False,
    )
```

```python
import functools

import jax
import jax.numpy as jnp
from jax import lax
from jax.experimental import pallas as pl
from jax.experimental.pallas import tpu as pltpu
from jax.sharding import PartitionSpec as P

HEADS = 12
EPS = 1e-06
BASE = 10000.0
MASKED = -1e30
AXES = ("dp", "seq")
LANES = 128
F32 = jnp.float32
BF16 = jnp.bfloat16
NN = (((1,), (0,)), ((), ()))
NT = (((1,), (1,)), ((), ()))
TN = (((0,), (0,)), ((), ()))


def mm(left, right, dims=NN):
    return lax.dot_general(left, right, dims, preferred_element_type=F32)


def params(steps=0, mib=56):
    semantics = ("arbitrary",) * steps if steps else None
    return pltpu.CompilerParams(dimension_semantics=semantics, vmem_limit_bytes=mib << 20)


def cost(flops, moved):
    return pl.CostEstimate(flops=int(flops), bytes_accessed=int(moved), transcendentals=0)


def whole():
    return pl.BlockSpec(memory_space=pltpu.VMEM)


def pairs(place):
    found = []
    for device in range(32):
        z, y, x, c = device // 8, (device // 4) % 2, (device // 2) % 2, device % 2
        z, y, x, c = place(z, y, x, c)
        found.append((device, ((z * 2 + y) * 2 + x) * 2 + c))
    return found


FLIP = {
    "y": pairs(lambda z, y, x, c: (z, 1 - y, x, c)),
    "x": pairs(lambda z, y, x, c: (z, y, 1 - x, c)),
    "c": pairs(lambda z, y, x, c: (z, y, x, 1 - c)),
    "z1": pairs(lambda z, y, x, c: (z ^ 1, y, x, c)),
    "z2": pairs(lambda z, y, x, c: (z ^ 2, y, x, c)),
    "z3": pairs(lambda z, y, x, c: (z ^ 3, y, x, c)),
    "xc": pairs(lambda z, y, x, c: (z, y, 1 - x, 1 - c)),
}


def coordinates():
    dp, seq = lax.axis_index("dp"), lax.axis_index("seq")
    return {"z": dp // 2, "y": dp % 2, "x": seq // 2, "c": seq % 2}


def small_torus():
    return lax.axis_size("dp") == 8 and lax.axis_size("seq") == 4


def after(value, *others):
    return lax.optimization_barrier((value,) + others)[0]


def together(values, *others):
    return lax.optimization_barrier(tuple(values) + others)[: len(values)]


def ordered(own, came, mine, axis):
    return jnp.where(mine == 0, jnp.stack([own, came], axis), jnp.stack([came, own], axis))


def flip(block, name):
    return lax.ppermute(block, AXES, FLIP[name])


def join(block, name, axis):
    return ordered(block, flip(block, name), coordinates()[name], axis)


def half_sum(part, name, axis):
    me = coordinates()[name]
    away = lax.dynamic_index_in_dim(part, 1 - me, axis, False)
    kept = lax.dynamic_index_in_dim(part, me, axis, False)
    return kept.astype(F32) + flip(away, name).astype(F32)


def z_gather(shard):
    return jnp.stack([shard] + [flip(shard, name) for name in ("z1", "z2", "z3")])


def z_sum(parts):
    groups = [[0, 2, 4, 6], [1, 3, 5, 7]]
    came = lax.all_to_all(parts, "dp", 0, 0, axis_index_groups=groups, tiled=True)
    return jnp.sum(came.astype(F32), axis=0)


def seq_send(blocks):
    if not small_torus():
        came = relative(swap(relative(blocks), "seq"))
        return [came[k : k + 1] for k in range(blocks.shape[0])]
    return [blocks] + [flip(blocks[k : k + 1], name) for k, name in ((1, "c"), (2, "x"), (3, "xc"))]


def seq_send_twice(blocks):
    if not small_torus():
        return seq_send(blocks)
    far = flip(blocks[2:], "x")
    near = flip(jnp.concatenate([blocks[1:2], far[1:]]), "c")
    return [blocks, near[:1], far[:1], near[1:]]


def relative(blocks):
    places = jnp.arange(blocks.shape[0], dtype=jnp.int32) ^ lax.axis_index("seq").astype(jnp.int32)
    return blocks[places]


def copies_sum(kept, away):
    if not small_torus():
        blocks = relative(jnp.stack([kept[0], away[0], kept[1], away[1]]))
        return [lax.psum_scatter(blocks, "seq", scatter_dimension=0, tiled=False)], kept
    far = (kept[1].astype(F32) + away[1].astype(F32)).astype(BF16)
    return [kept[0], away[0], flip(far, "x")], far


def add_up(terms):
    return sum((term.astype(F32) for term in terms[1:]), terms[0].astype(F32))


def swap(blocks, axis):
    return lax.all_to_all(blocks, axis, split_axis=0, concat_axis=0, tiled=True)


def turned(rows, cosine, sine):
    a, b = rows[:32], rows[32:]
    return a * cosine - b * sine, b * cosine + a * sine


def first_norm(x):
    x = x.astype(F32)
    r1 = lax.rsqrt(jnp.mean(x * x, axis=1, keepdims=True) + EPS)
    return x * r1, r1


def gain_row(w_ref):
    last = w_ref.shape[1] - LANES
    return w_ref[:, last:].astype(F32).T[LANES // 2 : LANES // 2 + 1, :]


def assemble(parts, width_ref, place):
    first = 0
    for part in parts:
        for k in range(part.shape[0]):
            rows = part.shape[1]
            at = pl.multiple_of(place(first + k) * rows, 8)
            width_ref[pl.ds(at, rows), :] = part[k]
        first += part.shape[0]


def qkv_kernel(seq_ref, dp_ref, *refs, sources):
    x_refs, part_refs = refs[:sources], refs[sources:-5]
    cos_ref, sin_ref, out_ref, w_ref, xn_ref = refs[-5:]
    step = pl.program_id(0)

    @pl.when(step == 0)
    def _():
        if len(part_refs) == 1:
            assemble(part_refs, w_ref, lambda r: r)
        else:
            assemble(part_refs, w_ref, lambda r: dp_ref[0] ^ ((r & 3) << 1 | r >> 2))

    for k, x_ref in enumerate(x_refs):

        @pl.when(step == k)
        def _(x_ref=x_ref):
            z1, _ = first_norm(x_ref[...])
            xn_ref[...] = (z1 * gain_row(w_ref)).astype(BF16)

    rows = mm(xn_ref[...], w_ref[...]).T
    cosine, sine = cos_ref[...], sin_ref[...]
    for base in range(0, out_ref.shape[1], 192):
        for c in range(2):
            at = base + c * 64
            a, b = turned(rows[at : at + 64], cosine, sine)
            out_ref[0, at : at + 32, :] = a.astype(BF16)
            out_ref[0, at + 32 : at + 64, :] = b.astype(BF16)
        out_ref[0, base + 128 : base + 192, :] = rows[base + 128 : base + 192].astype(BF16)


def qkv_project(seq, dp, xs, w_parts, cosine, sine):
    tokens, width = xs[0].shape
    across = w_parts[0].shape[2]
    columns = across - 64
    angles = pl.BlockSpec((32, tokens), lambda i, s, d: (0, i ^ s[0]))
    return pl.pallas_call(
        functools.partial(qkv_kernel, sources=len(xs)),
        grid_spec=pltpu.PrefetchScalarGridSpec(
            num_scalar_prefetch=2,
            grid=(len(xs),),
            in_specs=[pl.BlockSpec((tokens, width), lambda i, s, d: (0, 0))] * len(xs)
            + [pl.BlockSpec(part.shape, lambda i, s, d: (0, 0, 0)) for part in w_parts]
            + [angles, angles],
            out_specs=[
                pl.BlockSpec((1, columns, tokens), lambda i, s, d: (i ^ s[0], 0, 0)),
                pl.BlockSpec((width, across), lambda i, s, d: (0, 0)),
            ],
            scratch_shapes=[pltpu.VMEM((tokens, width), BF16)],
        ),
        out_shape=[
            jax.ShapeDtypeStruct((len(xs), columns, tokens), BF16),
            jax.ShapeDtypeStruct((width, across), BF16),
        ],
        compiler_params=params(1),
        cost_estimate=cost(1e9, 1 << 20),
        name="qkv_project",
    )(seq, dp, *xs, *w_parts, cosine, sine)


TILE = 256


def tile_of(ref, row, rows, index):
    per = ref.shape[2] // TILE
    at = (index % per) * TILE
    return ref[index // per, row : row + rows, at : at + TILE]


def flipped(block):
    return block.astype(F32).T.astype(BF16)


def masked(scores, start, i, j, diagonal):
    key = lax.broadcasted_iota(jnp.int32, scores.shape, 0)
    allowed = key >= start - j * TILE
    if diagonal:
        query = lax.broadcasted_iota(jnp.int32, scores.shape, 1)
        allowed = allowed & (key <= query)
    return jnp.where(allowed, scores, MASKED)


def start_of(docs):
    start = jnp.zeros_like(docs)
    for doc in range(1, 4):
        before = jnp.sum(jnp.where(docs < doc, 1, 0), axis=1, keepdims=True)
        start = jnp.where(docs >= doc, before, start)
    return start


def attend_kernel(seq_ref, buf_ref, docs_ref, ctx_ref, lse_ref, k_ref, s_ref, start_ref):
    start_ref[...] = start_of(docs_ref[...])
    tiles = buf_ref.shape[0] * buf_ref.shape[2] // TILE
    per = buf_ref.shape[2] // TILE
    for i in range(tiles):
        rows = slice(i * TILE, (i + 1) * TILE)
        k_ref[rows, :] = flipped(tile_of(buf_ref, 64, 64, i))
        q = (tile_of(buf_ref, 0, 64, i).astype(F32) * 0.125).astype(BF16)
        start = start_ref[0:1, rows]
        top = jnp.full((1, TILE), MASKED, F32)
        for j in range(i + 1):
            keys = slice(j * TILE, (j + 1) * TILE)
            scores = masked(mm(k_ref[keys, :], q), start, i, j, i == j)
            s_ref[keys, :] = scores
            top = jnp.maximum(top, jnp.max(scores, axis=0, keepdims=True))
        total = jnp.zeros((1, TILE), F32)
        context = jnp.zeros((64, TILE), F32)
        for j in range(i + 1):
            probs = jnp.exp(s_ref[j * TILE : (j + 1) * TILE, :] - top)
            total = total + jnp.sum(probs, axis=0, keepdims=True)
            context = context + mm(tile_of(buf_ref, 128, 64, j), probs.astype(BF16))
        at = (i % per) * TILE
        ctx_ref[(i // per) ^ seq_ref[0], :, at : at + TILE] = (context / total).astype(BF16)
        lse_ref[0, 0:1, rows] = top + jnp.log(total)


def attend(seq, buf, docs):
    blocks, rows, tokens = buf.shape
    heads, length = rows // 192, blocks * tokens
    return pl.pallas_call(
        attend_kernel,
        grid_spec=pltpu.PrefetchScalarGridSpec(
            num_scalar_prefetch=1,
            grid=(heads,),
            in_specs=[
                pl.BlockSpec((blocks, 192, tokens), lambda h, s: (0, h, 0)),
                pl.BlockSpec((1, length), lambda h, s: (0, 0)),
            ],
            out_specs=[
                pl.BlockSpec((blocks, 64, tokens), lambda h, s: (0, h, 0)),
                pl.BlockSpec((1, 1, length), lambda h, s: (h, 0, 0)),
            ],
            scratch_shapes=[
                pltpu.VMEM((length, 64), BF16),
                pltpu.VMEM((length, TILE), F32),
                pltpu.VMEM((1, length), jnp.int32),
            ],
        ),
        out_shape=[
            jax.ShapeDtypeStruct((blocks, heads * 64, tokens), BF16),
            jax.ShapeDtypeStruct((heads, 1, length), F32),
        ],
        compiler_params=params(1),
        cost_estimate=cost(3e9, 1 << 20),
        name="attend",
    )(seq, buf, docs)


def attend_back_kernel(
    seq_ref, buf_ref, d0_ref, d1_ref, d2_ref, d3_ref, ctx_ref, lse_ref, docs_ref, out_ref,
    k_ref, v_ref, dk_ref, dv_ref, start_ref, dctx_ref,
):
    for k, block_ref in enumerate((d0_ref, d1_ref, d2_ref, d3_ref)):
        dctx_ref[k ^ seq_ref[0]] = block_ref[0]
    start_ref[...] = start_of(docs_ref[...])
    tiles = buf_ref.shape[0] * buf_ref.shape[2] // TILE
    per = buf_ref.shape[2] // TILE
    for i in range(tiles):
        rows = slice(i * TILE, (i + 1) * TILE)
        k_ref[rows, :] = flipped(tile_of(buf_ref, 64, 64, i))
        v_ref[rows, :] = flipped(tile_of(buf_ref, 128, 64, i))
        q_t = (tile_of(buf_ref, 0, 64, i).astype(F32) * 0.125).astype(BF16)
        d_t = tile_of(dctx_ref, 0, 64, i)
        q_rows, d_rows = flipped(q_t), flipped(d_t)
        at = (i % per) * TILE
        context = ctx_ref[(i // per) ^ seq_ref[0], :, at : at + TILE].astype(F32)
        delta = jnp.sum(d_t.astype(F32) * context, axis=0, keepdims=True)
        start, log_total = start_ref[0:1, rows], lse_ref[0, 0:1, rows]
        d_query = jnp.zeros((64, TILE), F32)
        for j in range(i + 1):
            keys = slice(j * TILE, (j + 1) * TILE)
            scores = masked(mm(k_ref[keys, :], q_t), start, i, j, i == j)
            probs = jnp.exp(scores - log_total)
            d_probs = mm(v_ref[keys, :], d_t)
            d_scores = (probs * (d_probs - delta)).astype(BF16)
            d_query = d_query + mm(tile_of(buf_ref, 64, 64, j), d_scores)
            d_key = mm(d_scores, q_rows)
            d_value = mm(probs.astype(BF16), d_rows)
            if i == j:
                dk_ref[keys, :] = d_key
                dv_ref[keys, :] = d_value
            else:
                dk_ref[keys, :] += d_key
                dv_ref[keys, :] += d_value
        at = (i % per) * TILE
        out_ref[i // per, 0:64, at : at + TILE] = (d_query * 0.125).astype(BF16)
    for i in range(tiles):
        at = (i % per) * TILE
        rows = slice(i * TILE, (i + 1) * TILE)
        out_ref[i // per, 64:128, at : at + TILE] = dk_ref[rows, :].T.astype(BF16)
        out_ref[i // per, 128:192, at : at + TILE] = dv_ref[rows, :].T.astype(BF16)


def attend_back(seq, buf, dctxs, ctx, lse, docs, head):
    blocks, rows, tokens = buf.shape
    length = blocks * tokens
    one = pl.BlockSpec((blocks, 64, tokens), lambda i, s: (0, head, 0))
    return pl.pallas_call(
        attend_back_kernel,
        grid_spec=pltpu.PrefetchScalarGridSpec(
            num_scalar_prefetch=1,
            grid=(1,),
            in_specs=[
                pl.BlockSpec((blocks, 192, tokens), lambda i, s: (0, head, 0)),
                *[pl.BlockSpec((1, 64, tokens), lambda i, s: (0, head, 0))] * 4,
                one,
                pl.BlockSpec((1, 1, length), lambda i, s: (head, 0, 0)),
                pl.BlockSpec((1, length), lambda i, s: (0, 0)),
            ],
            out_specs=pl.BlockSpec((blocks, 192, tokens), lambda i, s: (0, 0, 0)),
            scratch_shapes=[pltpu.VMEM((length, 64), BF16)] * 2
            + [pltpu.VMEM((length, 64), F32)] * 2
            + [pltpu.VMEM((1, length), jnp.int32), pltpu.VMEM((blocks, 64, tokens), BF16)],
        ),
        out_shape=jax.ShapeDtypeStruct((blocks, 192, tokens), BF16),
        compiler_params=params(1),
        cost_estimate=cost(4e9, 1 << 20),
        name="attend_back",
    )(seq, buf, *dctxs, ctx, lse, docs)


def zyx_of(r):
    return (r & 3) << 2 | (r >> 2 & 1) << 1 | r >> 3


def middle_kernel(me_ref, seq_ref, *refs, experts, sources, parts):
    ctx_refs, w_refs = refs[:sources], refs[sources : -9 - parts]
    x_ref, pick_ref, routes_ref = refs[-9 - parts : -6 - parts]
    hidden_ref, hn_ref, gates_ref, attn_ref, misc_ref, ctx_ref = refs[-6 - parts : -parts]
    send_refs = refs[-parts:]
    width = x_ref.shape[1]
    first = 0
    for w_ref in w_refs:
        blocks, rows = w_ref.shape[0], w_ref.shape[1]
        for k in range(blocks):
            place = me_ref[0] ^ zyx_of(first + k)
            at = pl.ds(pl.multiple_of(place * rows, 16), rows)
            attn_ref[at, :] = w_ref[k, :, :width]
            misc_ref[at, :] = w_ref[k, :, width:]
        first += blocks
    for k, block_ref in enumerate(ctx_refs):
        rows = block_ref.shape[1]
        at = pl.ds(pl.multiple_of((seq_ref[0] ^ k) * rows, 16), rows)
        ctx_ref[at, :] = block_ref[0]
    hidden = x_ref[...].astype(F32) + mm(ctx_ref[...], attn_ref[...], TN)
    hidden_ref[...] = hidden
    r2 = lax.rsqrt(jnp.mean(hidden * hidden, axis=1, keepdims=True) + EPS)
    gain = misc_ref[...].astype(F32).T[experts : experts + 1, :]
    hn = (hidden * r2 * gain).astype(BF16)
    hn_ref[...] = hn
    first = 0
    for send_ref in send_refs:
        slots = send_ref.shape[0]
        send_ref[...] = mm(pick_ref[first : first + slots, :], hn).astype(BF16)
        first += slots
    logits = mm(hn, misc_ref[...])
    lane = lax.broadcasted_iota(jnp.int32, logits.shape, 1)
    first = jnp.sum(jnp.where(lane == routes_ref[:, 0:1], logits, 0.0), axis=1, keepdims=True)
    second = jnp.sum(jnp.where(lane == routes_ref[:, 1:2], logits, 0.0), axis=1, keepdims=True)
    top = jnp.maximum(first, second)
    first, second = jnp.exp(first - top), jnp.exp(second - top)
    total = first + second
    gates_ref[...] = jnp.where(lane == 0, first / total, jnp.where(lane == 1, second / total, 0.0))


def middle(me, seq, ctxs, x, w_parts, pick, routes, experts, parts):
    tokens, width = x.shape
    first = pl.BlockSpec((1,) + ctxs[0].shape[1:], lambda i, m, s: (0, 0, 0))

    def full(array):
        return pl.BlockSpec(array.shape, lambda i, m, s: (0,) * len(array.shape))

    out_shape = [
        jax.ShapeDtypeStruct((tokens, width), F32),
        jax.ShapeDtypeStruct((tokens, width), BF16),
        jax.ShapeDtypeStruct((tokens, LANES), F32),
        jax.ShapeDtypeStruct((width, width), BF16),
        jax.ShapeDtypeStruct((width, LANES), BF16),
        jax.ShapeDtypeStruct((width, tokens), BF16),
    ] + [jax.ShapeDtypeStruct((experts * part, width), BF16) for part in parts]
    return pl.pallas_call(
        functools.partial(middle_kernel, experts=experts, sources=len(ctxs), parts=len(parts)),
        grid_spec=pltpu.PrefetchScalarGridSpec(
            num_scalar_prefetch=2,
            grid=(1,),
            in_specs=[first] * len(ctxs) + [full(array) for array in (*w_parts, x, pick, routes)],
            out_specs=[full(array) for array in out_shape],
        ),
        out_shape=out_shape,
        compiler_params=params(1),
        cost_estimate=cost(5e8, 1 << 20),
        name="middle",
    )(me, seq, *ctxs, *w_parts, x, pick, routes)


def swiglu(gate, up, d_act):
    sigma = jax.nn.sigmoid(gate)
    act = (gate * sigma * up).astype(BF16)
    d_gate = (d_act * up * sigma * (1.0 + gate * (1.0 - sigma))).astype(BF16)
    d_up = (d_act * gate * sigma).astype(BF16)
    return act, d_gate, d_up


def dense_kernel(
    x_ref, dy_ref, wg_ref, wu_ref, wo_ref, y_ref, dx_ref, gg_ref, gu_ref, go_ref, xt_ref
):
    @pl.when(pl.program_id(0) == 0)
    def _():
        y_ref[...] = jnp.zeros_like(y_ref)
        dx_ref[...] = jnp.zeros_like(dx_ref)
        xt_ref[...] = flipped(x_ref[...])

    x, dy = x_ref[...], dy_ref[...]
    act, d_gate, d_up = swiglu(mm(x, wg_ref[...]), mm(x, wu_ref[...]), mm(dy, wo_ref[...], NT))
    y_ref[...] += mm(act, wo_ref[...])
    dx_ref[...] += mm(d_gate, wg_ref[...], NT) + mm(d_up, wu_ref[...], NT)
    gg_ref[...] = mm(xt_ref[...], d_gate).astype(BF16)
    gu_ref[...] = mm(xt_ref[...], d_up).astype(BF16)
    go_ref[...] = mm(act, dy, TN).astype(BF16)


def dense(x, dy, w_gate, w_up, w_out, tile=256):
    tokens, width = x.shape
    units = w_out.shape[0]
    rows = pl.BlockSpec((tokens, width), lambda j: (0, 0))
    tall = pl.BlockSpec((width, tile), lambda j: (0, j))
    wide = pl.BlockSpec((tile, width), lambda j: (j, 0))
    return pl.pallas_call(
        dense_kernel,
        grid=(units // tile,),
        in_specs=[rows, rows, tall, tall, wide],
        out_specs=[rows, rows, tall, tall, wide],
        out_shape=[
            jax.ShapeDtypeStruct((tokens, width), F32),
            jax.ShapeDtypeStruct((tokens, width), F32),
            jax.ShapeDtypeStruct((width, units), BF16),
            jax.ShapeDtypeStruct((width, units), BF16),
            jax.ShapeDtypeStruct((units, width), BF16),
        ],
        scratch_shapes=[pltpu.VMEM((width, tokens), BF16)],
        compiler_params=params(1),
        cost_estimate=cost(18 * tokens * width * units, 30 << 20),
        name="dense",
    )(x, dy, w_gate, w_up, w_out)


def paired_kernel(me_ref, x_ref, dy_ref, *refs):
    parts_a, parts_b = refs[0:3], refs[3:6]
    y_ref, dx_ref, share_ref, ka_ref, wa_ref, kb_ref, wb_ref = refs[6:13]
    xt_ref, y_acc, dx_acc, all_a, all_b, sum_a, sum_b = refs[13:]
    step = pl.program_id(0)
    tokens, width = y_ref.shape
    me = me_ref[0]

    def place_a(r):
        return me ^ zyx_of(r)

    def place_b(r):
        return me ^ ((r & 3) << 2 | (r >> 3) << 1 | (r >> 2 & 1))

    def z_kept(place):
        return lambda r: place(r) ^ (me & 12)

    @pl.when(step == 0)
    def _():
        y_acc[...] = jnp.zeros_like(y_acc)
        dx_acc[...] = jnp.zeros_like(dx_acc)
        xt_ref[...] = flipped(x_ref[...])
        for parts, every, place in ((parts_a, all_a, place_a), (parts_b, all_b, place_b)):
            first = 0
            for part in parts:
                for k in range(part.shape[0]):
                    every[place(first + k)] = part[k]
                first += part.shape[0]

    at = pl.ds(pl.multiple_of(step * 48, 16), 48)
    four = pl.ds(step * 4, 4)
    wg, wu = all_a[:, at, :].reshape(width, 256), all_b[:, at, :].reshape(width, 256)
    wo = jnp.concatenate(
        [
            jnp.concatenate(
                [half[four, 192 + k * 32 : 224 + k * 32, :] for half in (all_a, all_b)], axis=1
            ).reshape(256, 256)
            for k in range(width // 256)
        ],
        axis=1,
    )
    x, dy = x_ref[...], dy_ref[...]
    act, d_gate, d_up = swiglu(mm(x, wg), mm(x, wu), mm(dy, wo, NT))
    y_acc[...] += mm(act, wo)
    dx_acc[...] += mm(d_gate, wg, NT) + mm(d_up, wu, NT)
    sum_a[:, at, :] = mm(xt_ref[...], d_gate).astype(BF16).reshape(16, 48, 256)
    sum_b[:, at, :] = mm(xt_ref[...], d_up).astype(BF16).reshape(16, 48, 256)
    go = mm(act, dy, TN).astype(BF16).reshape(4, 64, width)
    for k in range(width // 256):
        block = go[:, :, k * 256 : k * 256 + 256]
        sum_a[four, 192 + k * 32 : 224 + k * 32, :] = block[:, :32]
        sum_b[four, 192 + k * 32 : 224 + k * 32, :] = block[:, 32:]

    @pl.when(step == pl.num_programs(0) - 1)
    def _():
        y_ref[...] = y_acc[:tokens, :]
        dx_ref[...] = dx_acc[:tokens, :]
        share_ref[:tokens, :] = y_acc[tokens:, :].astype(BF16)
        share_ref[tokens:, :] = dx_acc[tokens:, :].astype(BF16)
        for kept, away, total, place in (
            (ka_ref, wa_ref, sum_a, z_kept(place_a)),
            (kb_ref, wb_ref, sum_b, z_kept(place_b)),
        ):
            for r in range(8):
                kept[r] = total[place(r)]
                away[r] = total[place(r + 8)]


def paired(me, x, dy, parts_a, parts_b):
    every, width = x.shape
    tokens = every // 2
    block = parts_a[0].shape[1:]
    rows = pl.BlockSpec((every, width), lambda j, s: (0, 0))
    part = pl.BlockSpec((tokens, width), lambda j, s: (0, 0))

    def blocks(count):
        return pl.BlockSpec((count,) + block, lambda j, s: (0, 0, 0))

    return pl.pallas_call(
        paired_kernel,
        grid_spec=pltpu.PrefetchScalarGridSpec(
            num_scalar_prefetch=1,
            grid=(4,),
            in_specs=[rows, rows] + [blocks(4), blocks(4), blocks(8)] * 2,
            out_specs=[part, part, rows] + [blocks(8)] * 4,
            scratch_shapes=[pltpu.VMEM((width, every), BF16)]
            + [pltpu.VMEM((every, width), F32)] * 2
            + [pltpu.VMEM((16,) + block, BF16)] * 4,
        ),
        out_shape=[
            jax.ShapeDtypeStruct((tokens, width), F32),
            jax.ShapeDtypeStruct((tokens, width), F32),
            jax.ShapeDtypeStruct((every, width), BF16),
        ]
        + [jax.ShapeDtypeStruct((8,) + block, BF16)] * 4,
        compiler_params=params(1, 60),
        cost_estimate=cost(18 * every * width * 1024, 30 << 20),
        name="dense_pair",
    )(me, x, dy, *parts_a, *parts_b)


def lane_row(column):
    shape = (column.shape[0], LANES)
    here = lax.broadcasted_iota(jnp.int32, shape, 0) == lax.broadcasted_iota(jnp.int32, shape, 1)
    return jnp.sum(jnp.where(here, column, 0.0), axis=0, keepdims=True)


def noted(columns):
    row = lax.broadcasted_iota(jnp.int32, (16, LANES), 0)
    tile = jnp.zeros((16, LANES), F32)
    for k, column in enumerate(columns):
        values = lane_row(column)
        high = values.astype(BF16).astype(F32)
        tile = jnp.where(row == 2 * k, high, jnp.where(row == 2 * k + 1, values - high, tile))
    return tile.astype(BF16)


def expert_kernel(own_ref, x_ref, dy_ref, other_ref, misc_ref, wg_ref, wu_ref, wo_ref, *refs, low):
    y_ref, dx_ref, dgate_ref, deo_ref, act_ref, dg_ref, du_ref, y_acc, dx_acc = refs[-9:]
    earlier_refs = refs[:-9]
    step = pl.program_id(0)

    def dy_rows():
        if len(dy_ref.shape) == 2:
            return dy_ref[...]
        part = x_ref.shape[0] // dy_ref.shape[0]
        return dy_ref[:, low : low + part, :].reshape(x_ref.shape)

    @pl.when(step == 0)
    def _():
        y_acc[...] = jnp.zeros_like(y_acc)
        dx_acc[...] = jnp.zeros_like(dx_acc)
        logits = mm(x_ref[...], misc_ref[...])
        lane = lax.broadcasted_iota(jnp.int32, logits.shape, 1)
        other = other_ref[...].astype(jnp.int32)
        mine = jnp.sum(jnp.where(lane == own_ref[0], logits, 0.0), axis=1, keepdims=True)
        theirs = jnp.sum(jnp.where(lane == other, logits, 0.0), axis=1, keepdims=True)
        top = jnp.maximum(mine, theirs)
        mine, theirs = jnp.exp(mine - top), jnp.exp(theirs - top)
        deo_ref[...] = (mine / (mine + theirs) * dy_rows().astype(F32)).astype(BF16)

    x, deo = x_ref[...], deo_ref[...]
    wg, wu, wo = wg_ref[0], wu_ref[0], wo_ref[0]
    act, d_gate, d_up = swiglu(mm(x, wg), mm(x, wu), mm(deo, wo, NT))
    y_acc[...] += mm(act, wo)
    dx_acc[...] += mm(d_gate, wg, NT) + mm(d_up, wu, NT)
    act_ref[...] = act
    dg_ref[...] = d_gate
    du_ref[...] = d_up

    @pl.when(step == pl.num_programs(0) - 1)
    def _():
        y = y_acc[...].astype(BF16)
        y_ref[...] = y
        dgate = jnp.sum(y.astype(F32) * dy_rows().astype(F32), axis=1, keepdims=True)
        dgate_ref[...] = dgate
        if not earlier_refs:
            dx_ref[...] = dx_acc[...].astype(BF16)
        else:
            sources = dx_ref.shape[0]
            part, before = dgate.shape[0] // sources, earlier_refs[0].shape[0] // sources
            dx_ref[:, :part, :] = dx_acc[...].astype(BF16).reshape(sources, part, dx_ref.shape[2])
            dx_ref[:, part:, LANES:] = jnp.zeros((sources, 16, dx_ref.shape[2] - LANES), BF16)
            for k in range(sources):
                dx_ref[k, part:, :LANES] = noted(
                    [
                        dgate[k * part : (k + 1) * part],
                        earlier_refs[0][k * before : (k + 1) * before, :],
                    ]
                )


def expert(own, x, dy, low, other, misc, w_in, w_out, earlier=None, tile=256):
    slots, width = x.shape
    units = w_out.shape[1]
    steps = units // tile
    rows = pl.BlockSpec((slots, width), lambda j, s: (0, 0))
    column = pl.BlockSpec((slots, 1), lambda j, s: (0, 0))
    saved = pl.BlockSpec((slots, tile), lambda j, s: (0, j))
    every = pl.BlockSpec(dy.shape, lambda j, s: (0,) * len(dy.shape))
    dx_shape, more = (slots, width), []
    if earlier is not None:
        dx_shape, more = (dy.shape[0], slots // dy.shape[0] + 16, width), [earlier]
    dx_spec = pl.BlockSpec(dx_shape, lambda j, s: (0,) * len(dx_shape))
    return pl.pallas_call(
        functools.partial(expert_kernel, low=low),
        grid_spec=pltpu.PrefetchScalarGridSpec(
            num_scalar_prefetch=1,
            grid=(steps,),
            in_specs=[
                rows,
                every,
                column,
                pl.BlockSpec(misc.shape, lambda j, s: (0, 0)),
                pl.BlockSpec((1, width, tile), lambda j, s: (0, 0, j)),
                pl.BlockSpec((1, width, tile), lambda j, s: (0, 0, j + steps)),
                pl.BlockSpec((1, tile, width), lambda j, s: (0, j, 0)),
                *[pl.BlockSpec(array.shape, lambda j, s: (0, 0)) for array in more],
            ],
            out_specs=[rows, dx_spec, column, rows, saved, saved, saved],
            scratch_shapes=[pltpu.VMEM((slots, width), F32)] * 2,
        ),
        out_shape=[
            jax.ShapeDtypeStruct((slots, width), BF16),
            jax.ShapeDtypeStruct(dx_shape, BF16),
            jax.ShapeDtypeStruct((slots, 1), F32),
            jax.ShapeDtypeStruct((slots, width), BF16),
        ]
        + [jax.ShapeDtypeStruct((slots, units), BF16)] * 3,
        compiler_params=params(1),
        cost_estimate=cost(12 * slots * width * units, 40 << 20),
        name="expert",
    )(own, x, dy, other, misc, w_in, w_in, w_out, *more)


def expert_grads_kernel(seq_ref, *refs):
    count = (len(refs) - 4) // 6
    sets = [refs[k * 5 : k * 5 + 5] for k in range(count)]
    in_kept, in_away, out_kept, out_away = refs[5 * count : 5 * count + 4]
    turned_x = refs[5 * count + 4 :]
    step, half = pl.program_id(0), pl.num_programs(0) // 2

    @pl.when(step == 0)
    def _():
        for xt_ref, one in zip(turned_x, sets, strict=True):
            xt_ref[...] = flipped(one[0][...])

    def total(of):
        return sum((of(k) for k in range(1, count)), of(0)).astype(BF16)

    gate = total(lambda k: mm(turned_x[k][...], sets[k][3][...]))
    up = total(lambda k: mm(turned_x[k][...], sets[k][4][...]))
    down = total(lambda k: mm(sets[k][2][...], sets[k][1][...], TN))
    across = seq_ref[0] // 2

    def put(in_ref, out_ref):
        in_ref[across] = gate
        in_ref[1 - across] = up
        out_ref[0] = down

    @pl.when(step < half)
    def _():
        put(in_away, out_away)

    @pl.when(step >= half)
    def _():
        put(in_kept, out_kept)


def expert_grads(seq, sets, tile=256):
    width, units = sets[0][0].shape[1], sets[0][2].shape[1]
    steps = units // tile
    half = steps // 2
    part = units // 4

    def core_of(j, s):
        return jnp.where(j < half, 1 - s[0] % 2, s[0] % 2)

    def inner(j, s):
        return core_of(j, s) * half + j % half

    def outer(j, s):
        owner = 2 * ((s[0] // 2) ^ (j % half // (half // 2))) + core_of(j, s)
        return owner * (half // 2) + j % (half // 2)

    in_specs = []
    for x, *_ in sets:
        rows = pl.BlockSpec(x.shape, lambda j, s: (0, 0))
        saved = pl.BlockSpec((x.shape[0], tile), lambda j, s: (0, inner(j, s)))
        acts = pl.BlockSpec((x.shape[0], tile), lambda j, s: (0, outer(j, s)))
        in_specs += [rows, rows, acts, saved, saved]

    def kept(j):
        return jnp.maximum(j - half, 0)

    def away(j):
        return jnp.minimum(j, half - 1)

    def places(of):
        return [
            pl.BlockSpec((2, width, tile), lambda j, s: (0, 0, of(j))),
            pl.BlockSpec(
                (1, tile, width), lambda j, s: (of(j) // (half // 2), of(j) % (half // 2), 0)
            ),
        ]

    keeps, aways = places(kept), places(away)
    in_shape = jax.ShapeDtypeStruct((2, width, 2 * part), BF16)
    out_shape = jax.ShapeDtypeStruct((2, part, width), BF16)
    slots = sum(one[0].shape[0] for one in sets)
    return pl.pallas_call(
        expert_grads_kernel,
        grid_spec=pltpu.PrefetchScalarGridSpec(
            num_scalar_prefetch=1,
            grid=(steps,),
            in_specs=in_specs,
            out_specs=[keeps[0], aways[0], keeps[1], aways[1]],
            scratch_shapes=[pltpu.VMEM((width, one[0].shape[0]), BF16) for one in sets],
        ),
        out_shape=[in_shape, in_shape, out_shape, out_shape],
        compiler_params=params(1),
        cost_estimate=cost(2 * slots * width * units, 4 << 20),
        name="expert_grads",
    )(seq, *[array for one in sets for array in one])


def share_block(tokens, width, index):
    return pl.BlockSpec((tokens, width), lambda i: (index, 0))


def middle_back_kernel(
    dhn_ref, share_ref, slots_ref, routes_ref, gates_ref, misc_ref, hidden_ref, hn_ref,
    dy_ref, ctx_ref, w_ref, seq_ref, *refs, experts, parts,
):
    back_refs, (dh_ref, dctx_ref, grad_ref) = refs[:-3], refs[-3:]
    tokens = dhn_ref.shape[0]
    slots = experts * sum(parts)
    place = lax.broadcasted_iota(jnp.int32, (tokens, slots), 1)
    is0, is1 = place == slots_ref[:, 0:1], place == slots_ref[:, 1:2]
    pick = jnp.where(is0 | is1, 1.0, 0.0).astype(BF16)
    came = jnp.zeros(hidden_ref.shape, F32)
    first = 0
    for part, back_ref in zip(parts, back_refs, strict=False):
        rows = experts * part
        back = back_ref[...]
        if len(back.shape) == 3:
            back = back[:, :part, :].reshape(rows, back.shape[2])
        came = came + mm(pick[:, first : first + rows], back)
        first += rows
    if len(parts) == 1:
        dgate = back_refs[1][...]
        dg0 = jnp.sum(jnp.where(is0, dgate, 0.0), axis=1, keepdims=True)
        dg1 = jnp.sum(jnp.where(is1, dgate, 0.0), axis=1, keepdims=True)
    else:
        notes = back_refs[1][:, parts[1] :, :LANES].astype(F32)
        tables = [notes[:, 2, :] + notes[:, 3, :], notes[:, 0, :] + notes[:, 1, :]]
        spot = lax.broadcasted_iota(jnp.int32, (tokens, LANES), 1)
        found = []
        for k in range(2):
            route, slot = routes_ref[:, k : k + 1], slots_ref[:, k : k + 1]
            value, first = jnp.zeros((tokens, 1), F32), 0
            for part, table in zip(parts, tables, strict=True):
                line = jnp.zeros((tokens, LANES), F32)
                for e in range(experts):
                    line = jnp.where(route == e, table[e : e + 1, :], line)
                inside = (slot >= first) & (slot < first + experts * part)
                here = inside & (spot == slot - first - route * part)
                value = value + jnp.sum(jnp.where(here, line, 0.0), axis=1, keepdims=True)
                first += experts * part
            found.append(value)
        dg0, dg1 = found
    g0, g1 = gates_ref[:, 0:1], gates_ref[:, 1:2]
    mean = g0 * dg0 + g1 * dg1
    lane = lax.broadcasted_iota(jnp.int32, (tokens, LANES), 1)
    dlogits = (
        jnp.where(lane == routes_ref[:, 0:1], g0 * (dg0 - mean), 0.0)
        + jnp.where(lane == routes_ref[:, 1:2], g1 * (dg1 - mean), 0.0)
    ).astype(BF16)
    misc = misc_ref[...]
    dhn = dhn_ref[...] + share_ref[...].astype(F32) + mm(dlogits, misc, NT) + came
    hidden = hidden_ref[...]
    r2 = lax.rsqrt(jnp.mean(hidden * hidden, axis=1, keepdims=True) + EPS)
    z2 = hidden * r2
    gain = misc.astype(F32).T[experts : experts + 1, :]
    gain_grad = jnp.sum(dhn * z2, axis=0, keepdims=True)
    dz2 = dhn * gain
    dh = dy_ref[...].astype(F32) + r2 * (dz2 - z2 * jnp.mean(dz2 * z2, axis=1, keepdims=True))
    dh_ref[...] = dh
    dhb = dh.astype(BF16)
    for k in range(dctx_ref.shape[0]):
        rows = dctx_ref.shape[1]
        at = pl.ds(pl.multiple_of((seq_ref[0] ^ k) * rows, 16), rows)
        dctx_ref[k] = mm(w_ref[at, :], dhb, NT).astype(BF16)
    width = w_ref.shape[0]
    grad_ref[:, :width] = mm(ctx_ref[...], dhb).astype(BF16)
    small = mm(dlogits, hn_ref[...], TN)
    row = lax.broadcasted_iota(jnp.int32, small.shape, 0)
    small = jnp.where(row == experts, gain_grad, small)
    grad_ref[:, width:] = small.T.astype(BF16)


def middle_back(dhn, share, backs, slots, routes, gates, misc, hidden, hn, dy, ctx, w_attn, seq, seq_devs, experts, parts):
    tokens, width = hidden.shape
    return pl.pallas_call(
        functools.partial(middle_back_kernel, experts=experts, parts=parts),
        grid=(1,),
        in_specs=[whole(), share_block(tokens, width, 1)]
        + [whole()] * 9
        + [pl.BlockSpec(memory_space=pltpu.SMEM)]
        + [whole()] * len(backs),
        out_specs=[whole()] * 3,
        out_shape=[
            jax.ShapeDtypeStruct((tokens, width), F32),
            jax.ShapeDtypeStruct((seq_devs, width // seq_devs, tokens), BF16),
            jax.ShapeDtypeStruct((width, width + LANES), BF16),
        ],
        compiler_params=params(),
        cost_estimate=cost(3e9, 16 << 20),
        name="middle_back",
    )(dhn, share, slots, routes, gates, misc, hidden, hn, dy, ctx, w_attn, seq, *backs)


def output_kernel(hidden_ref, dense_ref, share_ref, slots_ref, gates_ref, *refs):
    came_refs, out_ref = refs[:-1], refs[-1]
    mixture = jnp.zeros(hidden_ref.shape, F32)
    first = 0
    for came_ref in came_refs:
        tokens, slots = hidden_ref.shape[0], came_ref.shape[0]
        place = first + lax.broadcasted_iota(jnp.int32, (tokens, slots), 1)
        for k in range(2):
            pick = jnp.where(place == slots_ref[:, k : k + 1], 1.0, 0.0).astype(BF16)
            mixture = mixture + gates_ref[:, k : k + 1] * mm(pick, came_ref[...])
        first += slots
    out_ref[...] = hidden_ref[...] + dense_ref[...] + share_ref[...].astype(F32) + mixture


def output_of(hidden, shared, share, cames, slots, gates):
    return pl.pallas_call(
        output_kernel,
        grid=(1,),
        in_specs=[whole(), whole(), share_block(*hidden.shape, 0)] + [whole()] * (2 + len(cames)),
        out_specs=whole(),
        out_shape=jax.ShapeDtypeStruct(hidden.shape, F32),
        compiler_params=params(),
        cost_estimate=cost(2e9, 8 << 20),
        name="output_of",
    )(hidden, shared, share, slots, gates, *cames)


def qkv_back_kernel(seq_ref, *refs):
    count = len(ORDER)
    x_refs, d_refs, refs = refs[:count], refs[count:-9], refs[-9:]
    w_ref, cos_ref, sin_ref, kept_ref, away_ref, g_ref, acc_ref, gain_ref, z_ref = refs
    step = pl.program_id(0)
    columns = w_ref.shape[1] - 64

    @pl.when(step == 0)
    def _():
        acc_ref[...] = jnp.zeros_like(acc_ref)
        gain_ref[...] = jnp.zeros_like(gain_ref)

    for at_step, k in enumerate(ORDER):

        @pl.when(step == at_step)
        def _(x_ref=x_refs[k]):
            z_ref[...], _ = first_norm(x_ref[...])

    z1 = z_ref[...]
    xn_t = (z1 * gain_row(w_ref)).T.astype(BF16)
    cosine, sine = cos_ref[...], -sin_ref[...]
    pieces = []
    for d_ref in d_refs:
        for c in range(2):
            pieces.extend(turned(d_ref[0, c * 64 : c * 64 + 64, :].astype(F32), cosine, sine))
        pieces.append(d_ref[0, 128:192, :].astype(F32))
    pieces.append(jnp.zeros((64, z1.shape[0]), F32))
    d_rows = jnp.concatenate(pieces, axis=0).T.astype(BF16)
    dxn = mm(d_rows, w_ref[...], NT)
    acc_ref[...] += mm(xn_t, d_rows)
    gain_ref[0:1, :] += jnp.sum(dxn * z1, axis=0, keepdims=True)

    @pl.when(step < count // 2)
    def _():
        away_ref[0] = dxn.astype(BF16)

    @pl.when(step >= count // 2)
    def _():
        kept_ref[0] = dxn.astype(BF16)

    @pl.when(step == pl.num_programs(0) - 1)
    def _():
        split = columns + 64 - LANES
        g_ref[:, :split] = acc_ref[:, :split].astype(BF16)
        row = lax.broadcasted_iota(jnp.int32, (LANES, gain_ref.shape[1]), 0)
        gain = jnp.where(row == LANES // 2, gain_ref[0:1, :], 0.0).T
        g_ref[:, split:] = (acc_ref[:, split:] + gain).astype(BF16)


ORDER = (1, 3, 0, 2)


def qkv_back(seq, xs, d_heads, w, cosine, sine):
    tokens, width = xs[0].shape

    def place(i, s):
        k = jnp.where(i < 2, 2 * i + 1, 2 * i - 4)
        return k ^ s[0]

    angles = pl.BlockSpec((32, tokens), lambda i, s: (0, place(i, s)))
    rows = pl.BlockSpec((tokens, width), lambda i, s: (0, 0))
    grads = pl.BlockSpec((1, 192, tokens), lambda i, s: (place(i, s), 0, 0))
    pair = jax.ShapeDtypeStruct((2, tokens, width), BF16)
    return pl.pallas_call(
        qkv_back_kernel,
        grid_spec=pltpu.PrefetchScalarGridSpec(
            num_scalar_prefetch=1,
            grid=(len(ORDER),),
            in_specs=[rows] * len(xs)
            + [grads] * len(d_heads)
            + [pl.BlockSpec(w.shape, lambda i, s: (0, 0)), angles, angles],
            out_specs=[
                pl.BlockSpec((1, tokens, width), lambda i, s: (jnp.maximum(i - 2, 0), 0, 0)),
                pl.BlockSpec((1, tokens, width), lambda i, s: (jnp.minimum(i, 1), 0, 0)),
                pl.BlockSpec(w.shape, lambda i, s: (0, 0)),
            ],
            scratch_shapes=[
                pltpu.VMEM(w.shape, F32),
                pltpu.VMEM((8, width), F32),
                pltpu.VMEM((tokens, width), F32),
            ],
        ),
        out_shape=[pair, pair, jax.ShapeDtypeStruct(w.shape, BF16)],
        compiler_params=params(1),
        cost_estimate=cost(12e9, 12 << 20),
        name="qkv_back",
    )(seq, *xs, *d_heads, w, cosine, sine)


def input_back_kernel(x_ref, dh_ref, w_ref, *refs):
    dxn_refs, out_ref = refs[:-1], refs[-1]
    z1, r1 = first_norm(x_ref[...])
    dz1 = add_up([ref[...] for ref in dxn_refs]) * gain_row(w_ref)
    out_ref[...] = dh_ref[...] + r1 * (dz1 - z1 * jnp.mean(dz1 * z1, axis=1, keepdims=True))


def input_back(x, dh, w, dxns):
    return pl.pallas_call(
        input_back_kernel,
        in_specs=[whole()] * (3 + len(dxns)),
        out_specs=whole(),
        out_shape=jax.ShapeDtypeStruct(dh.shape, F32),
        compiler_params=params(),
        cost_estimate=cost(1e8, 6 << 20),
        name="input_back",
    )(x, dh, w, *dxns)


def slot_plan(routes, order, experts, parts):
    before = (order[:, None] > order[None, :]).astype(BF16)
    ids = jnp.arange(experts, dtype=jnp.int32)
    first = (routes[:, 0:1] == ids).astype(BF16)
    second = (routes[:, 1:2] == ids).astype(BF16)
    earlier = mm(before, jnp.concatenate([first, second], axis=1))
    every = jnp.sum(first.astype(F32), axis=0, keepdims=True)
    place0 = jnp.sum(earlier[:, :experts] * first.astype(F32), axis=1)
    place1 = jnp.sum((earlier[:, experts:] + every) * second.astype(F32), axis=1)
    place = jnp.stack([place0, place1], axis=1).astype(jnp.int32)
    capacity = sum(parts)
    every = jnp.where(place < capacity, routes * capacity + place, experts * capacity)
    slot = jnp.full(place.shape, experts * capacity, jnp.int32)
    low = 0
    for part in parts:
        inside = (place >= low) & (place < low + part)
        slot = jnp.where(inside, experts * low + routes * part + place - low, slot)
        low += part
    return slot, every


def padded(shard, columns):
    return jnp.pad(shard, ((0, 0), (0, columns - shard.shape[1])))


def by_core(columns):
    rows, count = columns.shape
    tiles = count // 512
    return columns.reshape(rows, tiles, 4, 2, 64).transpose(3, 1, 0, 2, 4).reshape(2, tiles, rows, 256)


def paired_shards(shared_in, shared_out):
    units, width = shared_in.shape[1] // 2, shared_out.shape[1]
    shard = jnp.stack([by_core(shared_in[:, :units]), by_core(shared_in[:, units:])], axis=1)
    me = coordinates()["c"]
    away = lax.dynamic_index_in_dim(shard, 1 - me, 0, False)
    kept = lax.dynamic_index_in_dim(shard, me, 0, False)
    inner = ordered(kept, flip(away, "c"), me, 2).reshape(2, -1, 256)
    down = shared_out.reshape(2, 32, width // 256, 256).transpose(0, 2, 1, 3).reshape(2, -1, 256)
    return jnp.concatenate([inner, down], axis=1)


def paired_grads(sum_a, sum_b):
    me = coordinates()["c"]
    inner = jnp.stack([sum_a[:192], sum_b[:192]]).reshape(2, 4, 2, 24, 256)
    away = lax.dynamic_index_in_dim(inner, 1 - me, 2, False)
    kept = lax.dynamic_index_in_dim(inner, me, 2, False)
    both = ordered(kept, flip(away, "c"), me, 0).reshape(2, 2, 4, 24, 4, 64)
    inner = both.transpose(3, 1, 2, 4, 0, 5).reshape(24, -1)
    down = jnp.stack([sum_a[192:], sum_b[192:]]).reshape(2, 3, 32, 256)
    return inner, down.transpose(0, 2, 1, 3).reshape(64, -1)


def scalar(value):
    return value.astype(jnp.int32).reshape(1)


def split_parts(array, sizes):
    found, low = [], 0
    for size in sizes:
        found.append(array[low : low + size])
        low += size
    return found


def on_device(
    layer_input, cotangent, segments, routes, order, norm1_gain, attn_qkv, attn_out,
    norm2_gain, router, shared_in, shared_out, expert_in, expert_out,
):
    tokens, width = layer_input.shape
    seq_devs = lax.axis_size("seq")
    experts = lax.axis_size("dp")
    capacity = max(2, (18 * tokens + 8 * experts - 1) // (8 * experts))
    small = small_torus()
    parts = (80, capacity - 80) if small and capacity == 144 else (capacity,)
    sizes = [experts * part for part in parts]
    slots = experts * capacity
    units = shared_in.shape[1] // 2
    columns = 3 * width // seq_devs
    seq = scalar(lax.axis_index("seq"))

    shard_rows = norm1_gain.shape[0]
    head_shard = jnp.concatenate(
        [
            attn_qkv.reshape(-1, seq_devs, columns).transpose(1, 0, 2),
            jnp.broadcast_to(norm1_gain[None, :, None], (seq_devs, shard_rows, 1)),
            jnp.zeros((seq_devs, shard_rows, 63), BF16),
        ],
        axis=2,
    )
    head_shard = swap(head_shard, "seq").reshape(-1, columns + 64)
    misc_shard = jnp.concatenate(
        [attn_out, padded(jnp.concatenate([router, norm2_gain[:, None]], axis=1), LANES)], axis=1
    )
    slot_of, expert_slot = slot_plan(routes, order, experts, parts)
    every_slot = jnp.arange(slots, dtype=jnp.int32)[:, None]

    def pick_of(rows):
        return ((every_slot == rows[0:1]) | (every_slot == rows[1:2])).astype(BF16)

    rows = expert_slot.T
    pick_dy = pick_of(rows)
    routes_f = routes.astype(F32)
    other = jnp.sum(
        jnp.where(every_slot == rows[0:1], routes_f[:, 1][None, :], 0.0)
        + jnp.where(every_slot == rows[1:2], routes_f[:, 0][None, :], 0.0),
        axis=1,
    ).reshape(experts, capacity)
    pick = pick_of(slot_of.T)
    dy_send = mm(pick_dy, cotangent).astype(BF16).reshape(experts, capacity, width)
    frequency = BASE ** (-(jnp.arange(32, dtype=F32) * 2.0 / 64))
    places = jnp.arange(tokens * seq_devs, dtype=jnp.int32)
    angles = places.astype(F32)[None, :] * frequency[:, None]
    cosine, sine = jnp.cos(angles), jnp.sin(angles)

    block_rows = head_shard.shape[0]
    extra = -(-capacity // block_rows)
    notes = jnp.pad(other.astype(BF16), ((0, 0), (0, extra * block_rows - capacity)))
    notes = notes.reshape(experts, block_rows, extra)
    packed = jnp.concatenate(
        [
            jnp.broadcast_to(head_shard[None, :, : columns + 1], (experts, block_rows, columns + 1)),
            notes,
            jnp.zeros((experts, block_rows, 63 - extra), BF16),
        ],
        axis=2,
    )
    packed = swap(packed, "dp")
    w_parts = [packed.reshape(1, -1, columns + 64)]
    notes = packed[:, :, columns + 1 : columns + 1 + extra].reshape(experts, -1)[:, :capacity]
    others, low = [], 0
    for part in parts:
        others.append(notes[:, low : low + part].astype(F32).reshape(-1, 1))
        low += part
    if small:
        here = coordinates()
        me = scalar(here["z"] * 4 + here["y"] * 2 + here["x"])
        along_x = flip(after(layer_input, head_shard), "x")
        token_blocks = [layer_input, flip(layer_input, "c"), along_x, flip(along_x, "c")]
        misc_z = z_gather(after(join(misc_shard, "c", 0).reshape(48, -1), *w_parts))
        misc_parts = [misc_z, flip(after(misc_z, *w_parts), "y")]
    else:
        me = jnp.zeros((1,), jnp.int32)
        gathered = relative(lax.all_gather(layer_input, "seq", axis=0, tiled=False))
        token_blocks = [gathered[k] for k in range(seq_devs)]
        misc_parts = [lax.all_gather(misc_shard, AXES, axis=0, tiled=True)[None]]
    w_parts, pick, routes = (lambda v: (v[:-2], *v[-2:]))(together([*w_parts, pick, routes]))
    dy_rows = swap(after(dy_send, *w_parts, misc_z) if small else dy_send, "dp")

    heads, w_heads = qkv_project(
        seq, scalar(lax.axis_index("dp")), token_blocks, w_parts, cosine, sine
    )
    if small:
        heads = after(heads, misc_z)
        misc_parts.append(flip(jnp.concatenate(misc_parts), "x"))
        shards = z_gather(after(paired_shards(shared_in, shared_out), w_heads))
    ctx_heads, log_totals = attend(seq, heads, segments)
    ctxs = seq_send_twice(ctx_heads)
    hidden, hn, gates, w_attn, misc, ctx, *sends = middle(
        me, seq, ctxs, layer_input, misc_parts, pick, routes, experts, parts
    )

    sends[0] = after(sends[0], dy_rows, shards) if small else sends[0]

    row_parts = [
        swap(send.reshape(experts, part, width), "dp").reshape(-1, width)
        for part, send in zip(parts, sends, strict=True)
    ]
    if small:
        shards = after(shards, hn)
        a0, b0 = shards[:, 0], shards[:, 1]
        a1, b1 = flip(a0, "y"), flip(b0, "x")
        a2, b2 = flip(jnp.concatenate([a0, a1]), "x"), flip(jnp.concatenate([b0, b1]), "y")
        hn_pair = jnp.concatenate([hn, flip(hn, "c")], axis=0)
        dy_pair = jnp.concatenate([cotangent, flip(cotangent, "c")], axis=0)
        row_parts[0] = after(row_parts[0], a1, b1, hn_pair, dy_pair)
    else:
        w_gate = lax.all_gather(shared_in[:, :units], AXES, axis=0, tiled=True)
        w_up = lax.all_gather(shared_in[:, units:], AXES, axis=0, tiled=True)
        w_out = lax.all_gather(shared_out, AXES, axis=0, tiled=True)

    own = scalar(lax.axis_index("dp"))
    sets, eos, dxes, dgates, low = [], [], [], [], 0
    for k, (part, rows, other) in enumerate(zip(parts, row_parts, others, strict=True)):
        if k == 1:
            hn_pair = after(hn_pair, dxes[0])
            shared, dhn, share, *grads = paired(me, hn_pair, dy_pair, (a0, a1, a2), (b0, b1, b2))
            rows = after(rows, dhn)
        eo, dxe, dgate, deo, act, d_gate, d_up = expert(
            own, rows, dy_rows if small else dy_rows.reshape(-1, width), low, other, misc, expert_in,
            expert_out, dgates[0] if k == 1 else None,
        )
        low += part
        sets.append((rows, deo, act, d_gate, d_up))
        eos.append(eo.reshape(experts, part, width))
        dxes.append(dxe.reshape(experts, -1, width))
        dgates.append(dgate)
    backs = []
    for k, dxe in enumerate(dxes):
        back = swap(after(dxe, *backs), "dp")
        backs.append(back if k else back.reshape(-1, width))
    if not small:
        backs.append(swap(dgates[0].reshape(experts, capacity), "dp").reshape(1, slots))
    held = backs[:1]
    if small:
        share = flip(share, "c")
        ka, wa, kb, wb = grads
        ca, cb = flip(wa, "x"), flip(wb, "y")
        held += [share, ca, cb]
    else:
        shared, dhn, grad_gate, grad_up, grad_out = dense(hn, cotangent, w_gate, w_up, w_out)
        share = jnp.zeros((2 * tokens, width), BF16)
    sets = [(after(one[0], *held),) + one[1:] for one in sets]
    in_kept, in_away, out_kept, out_away = expert_grads(seq, sets)
    if small:
        ca, cb = together((ca, cb), in_kept)
        wa, wb = add_up([ka[4:], ca[4:]]).astype(BF16), add_up([kb[4:], cb[4:]]).astype(BF16)
        ea, eb = flip(wa, "y"), flip(wb, "x")
        in_away, out_away = flip(in_away, "c"), flip(out_away, "c")
        backs = [after(back, in_kept) for back in backs]
    dh, dctx, grad_attn = middle_back(
        dhn, share, backs, slot_of, routes, gates, misc, hidden, hn, cotangent, ctx, w_attn,
        seq, seq_devs, experts, parts,
    )

    dctxs = seq_send_twice(dctx)
    in_terms, in_far = copies_sum(in_kept, in_away)
    out_terms, out_far = copies_sum(out_kept, out_away)
    if small:
        dctxs[0] = after(dctxs[0], in_far, out_far)
    came = swap(after(jnp.concatenate(eos, axis=1), backs[-1]), "dp").reshape(-1, width)
    d_heads = []
    for head in range(columns // 192):
        held = after(heads, *d_heads) if d_heads else heads
        if small and head == 1:
            grad_attn = after(grad_attn, d_heads[0])
            part = half_sum(grad_attn.reshape(8, 2, 2, -1, width + LANES), "c", 2).astype(BF16)
            held = after(held, grad_attn)
        if small and head == 2:
            part = after(part, d_heads[1])
            part_kept = lax.dynamic_index_in_dim(part, here["x"], 1, False)
            part_came = flip(lax.dynamic_index_in_dim(part, 1 - here["x"], 1, False), "x")
        d_heads.append(attend_back(seq, held, dctxs, ctx_heads, log_totals, segments, head))
    if small:
        ea, eb = together((ea, eb), d_heads[0])
        wa, wb = add_up([ka[:4], ca[:4], ea]).astype(BF16), add_up([kb[:4], cb[:4], eb]).astype(BF16)
        sums = z_sum(after(jnp.stack([wa, wb], axis=1), came))
        d_heads[0] = after(d_heads[0], sums)
    dxn_kept, dxn_away, grad_heads = qkv_back(seq, token_blocks, d_heads, w_heads, cosine, sine)
    if small:
        dxn_away = after(flip(dxn_away, "c"), in_terms[2], out_terms[2])
    dxn_terms, dxn_far = copies_sum(dxn_kept, dxn_away)
    input_grad = input_back(layer_input, dh, w_heads, dxn_terms)
    layer_output = output_of(
        hidden, shared, share, [after(came, dxn_far)], expert_slot, gates
    )

    grad_heads = grad_heads.reshape(experts * seq_devs, -1, columns + 64)
    grad_heads = swap(grad_heads, AXES)
    grad_heads = grad_heads.reshape((experts, seq_devs) + grad_heads.shape[1:])
    if small:
        sum_in, sum_out = paired_grads(*together((sums[0], sums[1]), dxn_far))
        part = add_up([part_kept, after(part_came, dxn_far)]).astype(BF16)
        sum_attn = jnp.sum(swap(after(part, grad_heads), "dp").astype(F32), axis=0)
        in_terms, out_terms = together((*in_terms, *out_terms), dxn_far), ()
        in_terms, out_terms = in_terms[:3], in_terms[3:]
    else:
        total = functools.partial(lax.psum_scatter, scatter_dimension=0, tiled=True)
        sum_attn = total(grad_attn, AXES).astype(F32)
        sum_out = total(grad_out, AXES).astype(F32)
        sum_in = jnp.concatenate([total(grad_gate, AXES), total(grad_up, AXES)], axis=1).astype(F32)
    sum_heads = jnp.sum(grad_heads.astype(F32), axis=0)
    return (
        layer_output,
        input_grad,
        jnp.sum(sum_heads[:, :, columns], axis=0),
        sum_heads[:, :, :columns].transpose(1, 0, 2).reshape(-1, seq_devs * columns),
        sum_attn[:, :width],
        sum_attn[:, width + experts],
        sum_attn[:, width : width + experts],
        sum_in,
        sum_out,
        add_up(in_terms)[None],
        add_up(out_terms)[None],
    )


def solution(mesh):
    rows = P(AXES, None)
    return jax.shard_map(
        on_device,
        mesh=mesh,
        in_specs=(
            rows, rows, P("dp", None), rows, P(AXES), P(AXES), rows, rows,
            P(AXES), rows, rows, rows, P("dp", None, None), P("dp", None, None),
        ),
        out_specs=(
            rows, rows, P(AXES), rows, rows, P(AXES), rows, rows, rows,
            P("dp", None, "seq"), P("dp", "seq", None),
        ),
        check_vma=False,
    )
```

```python
import functools

import jax
import jax.numpy as jnp
from jax import lax
from jax.experimental import pallas as pl
from jax.experimental.pallas import tpu as pltpu
from jax.sharding import PartitionSpec as P

HEADS = 12
EPS = 1e-06
BASE = 10000.0
MASKED = -1e30
AXES = ("dp", "seq")
LANES = 128
F32 = jnp.float32
BF16 = jnp.bfloat16
NN = (((1,), (0,)), ((), ()))
NT = (((1,), (1,)), ((), ()))
TN = (((0,), (0,)), ((), ()))


def mm(left, right, dims=NN):
    return lax.dot_general(left, right, dims, preferred_element_type=F32)


def params(steps=0, mib=56):
    semantics = ("arbitrary",) * steps if steps else None
    return pltpu.CompilerParams(dimension_semantics=semantics, vmem_limit_bytes=mib << 20)


def cost(flops, moved):
    return pl.CostEstimate(flops=int(flops), bytes_accessed=int(moved), transcendentals=0)


def whole():
    return pl.BlockSpec(memory_space=pltpu.VMEM)


def pairs(place):
    found = []
    for device in range(32):
        z, y, x, c = device // 8, (device // 4) % 2, (device // 2) % 2, device % 2
        z, y, x, c = place(z, y, x, c)
        found.append((device, ((z * 2 + y) * 2 + x) * 2 + c))
    return found


FLIP = {
    "y": pairs(lambda z, y, x, c: (z, 1 - y, x, c)),
    "x": pairs(lambda z, y, x, c: (z, y, 1 - x, c)),
    "c": pairs(lambda z, y, x, c: (z, y, x, 1 - c)),
    "z1": pairs(lambda z, y, x, c: (z ^ 1, y, x, c)),
    "z2": pairs(lambda z, y, x, c: (z ^ 2, y, x, c)),
    "z3": pairs(lambda z, y, x, c: (z ^ 3, y, x, c)),
    "xc": pairs(lambda z, y, x, c: (z, y, 1 - x, 1 - c)),
}


def coordinates():
    dp, seq = lax.axis_index("dp"), lax.axis_index("seq")
    return {"z": dp // 2, "y": dp % 2, "x": seq // 2, "c": seq % 2}


def small_torus():
    return lax.axis_size("dp") == 8 and lax.axis_size("seq") == 4


def after(value, *others):
    return lax.optimization_barrier((value,) + others)[0]


def together(values, *others):
    return lax.optimization_barrier(tuple(values) + others)[: len(values)]


def ordered(own, came, mine, axis):
    return jnp.where(mine == 0, jnp.stack([own, came], axis), jnp.stack([came, own], axis))


def flip(block, name):
    return lax.ppermute(block, AXES, FLIP[name])


def join(block, name, axis):
    return ordered(block, flip(block, name), coordinates()[name], axis)


def half_sum(part, name, axis):
    me = coordinates()[name]
    away = lax.dynamic_index_in_dim(part, 1 - me, axis, False)
    kept = lax.dynamic_index_in_dim(part, me, axis, False)
    return kept.astype(F32) + flip(away, name).astype(F32)


def z_shards(shard):
    return [shard] + [flip(shard, name) for name in ("z1", "z2", "z3")]


def z_gather(shard):
    return jnp.stack(z_shards(shard))


def z_sum(parts):
    groups = [[0, 2, 4, 6], [1, 3, 5, 7]]
    came = lax.all_to_all(parts, "dp", 0, 0, axis_index_groups=groups, tiled=True)
    return jnp.sum(came.astype(F32), axis=0)


def seq_send(blocks):
    if not small_torus():
        came = relative(swap(relative(blocks), "seq"))
        return [came[k : k + 1] for k in range(blocks.shape[0])]
    return [blocks] + [flip(blocks[k : k + 1], name) for k, name in ((1, "c"), (2, "x"), (3, "xc"))]


def seq_send_twice(blocks):
    if not small_torus():
        return seq_send(blocks)
    far = flip(blocks[2:], "x")
    near = flip(jnp.concatenate([blocks[1:2], far[1:]]), "c")
    return [blocks, near[:1], far[:1], near[1:]]


def relative(blocks):
    places = jnp.arange(blocks.shape[0], dtype=jnp.int32) ^ lax.axis_index("seq").astype(jnp.int32)
    return blocks[places]


def copies_sum(kept, away):
    if not small_torus():
        blocks = relative(jnp.stack([kept[0], away[0], kept[1], away[1]]))
        return [lax.psum_scatter(blocks, "seq", scatter_dimension=0, tiled=False)], kept
    far = (kept[1].astype(F32) + away[1].astype(F32)).astype(BF16)
    return [kept[0], away[0], flip(far, "x")], far


def add_up(terms):
    return sum((term.astype(F32) for term in terms[1:]), terms[0].astype(F32))


def swap(blocks, axis):
    return lax.all_to_all(blocks, axis, split_axis=0, concat_axis=0, tiled=True)


def turned(rows, cosine, sine):
    a, b = rows[:32], rows[32:]
    return a * cosine - b * sine, b * cosine + a * sine


def first_norm(x):
    x = x.astype(F32)
    r1 = lax.rsqrt(jnp.mean(x * x, axis=1, keepdims=True) + EPS)
    return x * r1, r1


def gain_row(w_ref):
    last = w_ref.shape[1] - LANES
    return w_ref[:, last:].astype(F32).T[LANES // 2 : LANES // 2 + 1, :]


def assemble(parts, width_ref, place):
    first = 0
    for part in parts:
        for k in range(part.shape[0]):
            rows = part.shape[1]
            at = pl.multiple_of(place(first + k) * rows, 8)
            width_ref[pl.ds(at, rows), :] = part[k]
        first += part.shape[0]


def qkv_kernel(seq_ref, dp_ref, *refs, sources):
    x_refs, part_refs = refs[:sources], refs[sources:-5]
    cos_ref, sin_ref, out_ref, w_ref, xn_ref = refs[-5:]
    step = pl.program_id(0)

    @pl.when(step == 0)
    def _():
        if len(part_refs) == 1:
            assemble(part_refs, w_ref, lambda r: r)
        else:
            assemble(part_refs, w_ref, lambda r: dp_ref[0] ^ ((r & 3) << 1 | r >> 2))

    for k, x_ref in enumerate(x_refs):

        @pl.when(step == k)
        def _(x_ref=x_ref):
            z1, _ = first_norm(x_ref[...])
            xn_ref[...] = (z1 * gain_row(w_ref)).astype(BF16)

    rows = mm(xn_ref[...], w_ref[...]).T
    cosine, sine = cos_ref[...], sin_ref[...]
    for base in range(0, out_ref.shape[1], 192):
        for c in range(2):
            at = base + c * 64
            a, b = turned(rows[at : at + 64], cosine, sine)
            out_ref[0, at : at + 32, :] = a.astype(BF16)
            out_ref[0, at + 32 : at + 64, :] = b.astype(BF16)
        out_ref[0, base + 128 : base + 192, :] = rows[base + 128 : base + 192].astype(BF16)


def qkv_project(seq, dp, xs, w_parts, cosine, sine):
    tokens, width = xs[0].shape
    across = w_parts[0].shape[2]
    columns = across - 64
    angles = pl.BlockSpec((32, tokens), lambda i, s, d: (0, i ^ s[0]))
    return pl.pallas_call(
        functools.partial(qkv_kernel, sources=len(xs)),
        grid_spec=pltpu.PrefetchScalarGridSpec(
            num_scalar_prefetch=2,
            grid=(len(xs),),
            in_specs=[pl.BlockSpec((tokens, width), lambda i, s, d: (0, 0))] * len(xs)
            + [pl.BlockSpec(part.shape, lambda i, s, d: (0, 0, 0)) for part in w_parts]
            + [angles, angles],
            out_specs=[
                pl.BlockSpec((1, columns, tokens), lambda i, s, d: (i ^ s[0], 0, 0)),
                pl.BlockSpec((width, across), lambda i, s, d: (0, 0)),
            ],
            scratch_shapes=[pltpu.VMEM((tokens, width), BF16)],
        ),
        out_shape=[
            jax.ShapeDtypeStruct((len(xs), columns, tokens), BF16),
            jax.ShapeDtypeStruct((width, across), BF16),
        ],
        compiler_params=params(1),
        cost_estimate=cost(1e9, 1 << 20),
        name="qkv_project",
    )(seq, dp, *xs, *w_parts, cosine, sine)


TILE = 256


def tile_of(ref, row, rows, index):
    per = ref.shape[2] // TILE
    at = (index % per) * TILE
    return ref[index // per, row : row + rows, at : at + TILE]


def flipped(block):
    return block.astype(F32).T.astype(BF16)


def masked(scores, start, i, j, diagonal):
    key = lax.broadcasted_iota(jnp.int32, scores.shape, 0)
    allowed = key >= start - j * TILE
    if diagonal:
        query = lax.broadcasted_iota(jnp.int32, scores.shape, 1)
        allowed = allowed & (key <= query)
    return jnp.where(allowed, scores, MASKED)


def start_of(docs):
    start = jnp.zeros_like(docs)
    for doc in range(1, 4):
        before = jnp.sum(jnp.where(docs < doc, 1, 0), axis=1, keepdims=True)
        start = jnp.where(docs >= doc, before, start)
    return start


def attend_kernel(seq_ref, buf_ref, docs_ref, ctx_ref, lse_ref, k_ref, s_ref, start_ref):
    start_ref[...] = start_of(docs_ref[...])
    tiles = buf_ref.shape[0] * buf_ref.shape[2] // TILE
    per = buf_ref.shape[2] // TILE
    for i in range(tiles):
        rows = slice(i * TILE, (i + 1) * TILE)
        k_ref[rows, :] = flipped(tile_of(buf_ref, 64, 64, i))
        q = (tile_of(buf_ref, 0, 64, i).astype(F32) * 0.125).astype(BF16)
        start = start_ref[0:1, rows]
        top = jnp.full((1, TILE), MASKED, F32)
        for j in range(i + 1):
            keys = slice(j * TILE, (j + 1) * TILE)
            scores = masked(mm(k_ref[keys, :], q), start, i, j, i == j)
            s_ref[keys, :] = scores
            top = jnp.maximum(top, jnp.max(scores, axis=0, keepdims=True))
        total = jnp.zeros((1, TILE), F32)
        context = jnp.zeros((64, TILE), F32)
        for j in range(i + 1):
            probs = jnp.exp(s_ref[j * TILE : (j + 1) * TILE, :] - top)
            total = total + jnp.sum(probs, axis=0, keepdims=True)
            context = context + mm(tile_of(buf_ref, 128, 64, j), probs.astype(BF16))
        at = (i % per) * TILE
        ctx_ref[(i // per) ^ seq_ref[0], :, at : at + TILE] = (context / total).astype(BF16)
        lse_ref[0, 0:1, rows] = top + jnp.log(total)


def attend(seq, buf, docs):
    blocks, rows, tokens = buf.shape
    heads, length = rows // 192, blocks * tokens
    return pl.pallas_call(
        attend_kernel,
        grid_spec=pltpu.PrefetchScalarGridSpec(
            num_scalar_prefetch=1,
            grid=(heads,),
            in_specs=[
                pl.BlockSpec((blocks, 192, tokens), lambda h, s: (0, h, 0)),
                pl.BlockSpec((1, length), lambda h, s: (0, 0)),
            ],
            out_specs=[
                pl.BlockSpec((blocks, 64, tokens), lambda h, s: (0, h, 0)),
                pl.BlockSpec((1, 1, length), lambda h, s: (h, 0, 0)),
            ],
            scratch_shapes=[
                pltpu.VMEM((length, 64), BF16),
                pltpu.VMEM((length, TILE), F32),
                pltpu.VMEM((1, length), jnp.int32),
            ],
        ),
        out_shape=[
            jax.ShapeDtypeStruct((blocks, heads * 64, tokens), BF16),
            jax.ShapeDtypeStruct((heads, 1, length), F32),
        ],
        compiler_params=params(1),
        cost_estimate=cost(3e9, 1 << 20),
        name="attend",
    )(seq, buf, docs)


def attend_back_kernel(
    seq_ref, buf_ref, d0_ref, d1_ref, d2_ref, d3_ref, ctx_ref, lse_ref, docs_ref, out_ref,
    k_ref, v_ref, dk_ref, dv_ref, start_ref, dctx_ref,
):
    for k, block_ref in enumerate((d0_ref, d1_ref, d2_ref, d3_ref)):
        dctx_ref[k ^ seq_ref[0]] = block_ref[0]
    start_ref[...] = start_of(docs_ref[...])
    tiles = buf_ref.shape[0] * buf_ref.shape[2] // TILE
    per = buf_ref.shape[2] // TILE
    for i in range(tiles):
        rows = slice(i * TILE, (i + 1) * TILE)
        k_ref[rows, :] = flipped(tile_of(buf_ref, 64, 64, i))
        v_ref[rows, :] = flipped(tile_of(buf_ref, 128, 64, i))
        q_t = (tile_of(buf_ref, 0, 64, i).astype(F32) * 0.125).astype(BF16)
        d_t = tile_of(dctx_ref, 0, 64, i)
        q_rows, d_rows = flipped(q_t), flipped(d_t)
        at = (i % per) * TILE
        context = ctx_ref[(i // per) ^ seq_ref[0], :, at : at + TILE].astype(F32)
        delta = jnp.sum(d_t.astype(F32) * context, axis=0, keepdims=True)
        start, log_total = start_ref[0:1, rows], lse_ref[0, 0:1, rows]
        d_query = jnp.zeros((64, TILE), F32)
        for j in range(i + 1):
            keys = slice(j * TILE, (j + 1) * TILE)
            scores = masked(mm(k_ref[keys, :], q_t), start, i, j, i == j)
            probs = jnp.exp(scores - log_total)
            d_probs = mm(v_ref[keys, :], d_t)
            d_scores = (probs * (d_probs - delta)).astype(BF16)
            d_query = d_query + mm(tile_of(buf_ref, 64, 64, j), d_scores)
            d_key = mm(d_scores, q_rows)
            d_value = mm(probs.astype(BF16), d_rows)
            if i == j:
                dk_ref[keys, :] = d_key
                dv_ref[keys, :] = d_value
            else:
                dk_ref[keys, :] += d_key
                dv_ref[keys, :] += d_value
        at = (i % per) * TILE
        out_ref[i // per, 0:64, at : at + TILE] = (d_query * 0.125).astype(BF16)
    for i in range(tiles):
        at = (i % per) * TILE
        rows = slice(i * TILE, (i + 1) * TILE)
        out_ref[i // per, 64:128, at : at + TILE] = dk_ref[rows, :].T.astype(BF16)
        out_ref[i // per, 128:192, at : at + TILE] = dv_ref[rows, :].T.astype(BF16)


def attend_back(seq, buf, dctxs, ctx, lse, docs, head):
    blocks, rows, tokens = buf.shape
    length = blocks * tokens
    one = pl.BlockSpec((blocks, 64, tokens), lambda i, s: (0, head, 0))
    return pl.pallas_call(
        attend_back_kernel,
        grid_spec=pltpu.PrefetchScalarGridSpec(
            num_scalar_prefetch=1,
            grid=(1,),
            in_specs=[
                pl.BlockSpec((blocks, 192, tokens), lambda i, s: (0, head, 0)),
                *[pl.BlockSpec((1, 64, tokens), lambda i, s: (0, head, 0))] * 4,
                one,
                pl.BlockSpec((1, 1, length), lambda i, s: (head, 0, 0)),
                pl.BlockSpec((1, length), lambda i, s: (0, 0)),
            ],
            out_specs=pl.BlockSpec((blocks, 192, tokens), lambda i, s: (0, 0, 0)),
            scratch_shapes=[pltpu.VMEM((length, 64), BF16)] * 2
            + [pltpu.VMEM((length, 64), F32)] * 2
            + [pltpu.VMEM((1, length), jnp.int32), pltpu.VMEM((blocks, 64, tokens), BF16)],
        ),
        out_shape=jax.ShapeDtypeStruct((blocks, 192, tokens), BF16),
        compiler_params=params(1),
        cost_estimate=cost(4e9, 1 << 20),
        name="attend_back",
    )(seq, buf, *dctxs, ctx, lse, docs)


def zyx_of(r):
    return (r & 3) << 2 | (r >> 2 & 1) << 1 | r >> 3


def middle_kernel(me_ref, seq_ref, *refs, experts, sources, parts):
    ctx_refs, w_refs = refs[:sources], refs[sources : -9 - parts]
    x_ref, pick_ref, routes_ref = refs[-9 - parts : -6 - parts]
    hidden_ref, hn_ref, gates_ref, attn_ref, misc_ref, ctx_ref = refs[-6 - parts : -parts]
    send_refs = refs[-parts:]
    width = x_ref.shape[1]
    first = 0
    for w_ref in w_refs:
        blocks, rows = w_ref.shape[0], w_ref.shape[1]
        for k in range(blocks):
            place = me_ref[0] ^ zyx_of(first + k)
            at = pl.ds(pl.multiple_of(place * rows, 16), rows)
            attn_ref[at, :] = w_ref[k, :, :width]
            misc_ref[at, :] = w_ref[k, :, width:]
        first += blocks
    for k, block_ref in enumerate(ctx_refs):
        rows = block_ref.shape[1]
        at = pl.ds(pl.multiple_of((seq_ref[0] ^ k) * rows, 16), rows)
        ctx_ref[at, :] = block_ref[0]
    hidden = x_ref[...].astype(F32) + mm(ctx_ref[...], attn_ref[...], TN)
    hidden_ref[...] = hidden
    r2 = lax.rsqrt(jnp.mean(hidden * hidden, axis=1, keepdims=True) + EPS)
    gain = misc_ref[...].astype(F32).T[experts : experts + 1, :]
    hn = (hidden * r2 * gain).astype(BF16)
    hn_ref[...] = hn
    first = 0
    for send_ref in send_refs:
        slots = send_ref.shape[0]
        send_ref[...] = mm(pick_ref[first : first + slots, :], hn).astype(BF16)
        first += slots
    logits = mm(hn, misc_ref[...])
    lane = lax.broadcasted_iota(jnp.int32, logits.shape, 1)
    first = jnp.sum(jnp.where(lane == routes_ref[:, 0:1], logits, 0.0), axis=1, keepdims=True)
    second = jnp.sum(jnp.where(lane == routes_ref[:, 1:2], logits, 0.0), axis=1, keepdims=True)
    top = jnp.maximum(first, second)
    first, second = jnp.exp(first - top), jnp.exp(second - top)
    total = first + second
    gates_ref[...] = jnp.where(lane == 0, first / total, jnp.where(lane == 1, second / total, 0.0))


def middle(me, seq, ctxs, x, w_parts, pick, routes, experts, parts):
    tokens, width = x.shape
    first = pl.BlockSpec((1,) + ctxs[0].shape[1:], lambda i, m, s: (0, 0, 0))

    def full(array):
        return pl.BlockSpec(array.shape, lambda i, m, s: (0,) * len(array.shape))

    out_shape = [
        jax.ShapeDtypeStruct((tokens, width), F32),
        jax.ShapeDtypeStruct((tokens, width), BF16),
        jax.ShapeDtypeStruct((tokens, LANES), F32),
        jax.ShapeDtypeStruct((width, width), BF16),
        jax.ShapeDtypeStruct((width, LANES), BF16),
        jax.ShapeDtypeStruct((width, tokens), BF16),
    ] + [jax.ShapeDtypeStruct((experts * part, width), BF16) for part in parts]
    return pl.pallas_call(
        functools.partial(middle_kernel, experts=experts, sources=len(ctxs), parts=len(parts)),
        grid_spec=pltpu.PrefetchScalarGridSpec(
            num_scalar_prefetch=2,
            grid=(1,),
            in_specs=[first] * len(ctxs) + [full(array) for array in (*w_parts, x, pick, routes)],
            out_specs=[full(array) for array in out_shape],
        ),
        out_shape=out_shape,
        compiler_params=params(1),
        cost_estimate=cost(5e8, 1 << 20),
        name="middle",
    )(me, seq, *ctxs, *w_parts, x, pick, routes)


def swiglu(gate, up, d_act):
    sigma = jax.nn.sigmoid(gate)
    act = (gate * sigma * up).astype(BF16)
    d_gate = (d_act * up * sigma * (1.0 + gate * (1.0 - sigma))).astype(BF16)
    d_up = (d_act * gate * sigma).astype(BF16)
    return act, d_gate, d_up


def dense_kernel(
    x_ref, dy_ref, wg_ref, wu_ref, wo_ref, y_ref, dx_ref, gg_ref, gu_ref, go_ref, xt_ref
):
    @pl.when(pl.program_id(0) == 0)
    def _():
        y_ref[...] = jnp.zeros_like(y_ref)
        dx_ref[...] = jnp.zeros_like(dx_ref)
        xt_ref[...] = flipped(x_ref[...])

    x, dy = x_ref[...], dy_ref[...]
    act, d_gate, d_up = swiglu(mm(x, wg_ref[...]), mm(x, wu_ref[...]), mm(dy, wo_ref[...], NT))
    y_ref[...] += mm(act, wo_ref[...])
    dx_ref[...] += mm(d_gate, wg_ref[...], NT) + mm(d_up, wu_ref[...], NT)
    gg_ref[...] = mm(xt_ref[...], d_gate).astype(BF16)
    gu_ref[...] = mm(xt_ref[...], d_up).astype(BF16)
    go_ref[...] = mm(act, dy, TN).astype(BF16)


def dense(x, dy, w_gate, w_up, w_out, tile=256):
    tokens, width = x.shape
    units = w_out.shape[0]
    rows = pl.BlockSpec((tokens, width), lambda j: (0, 0))
    tall = pl.BlockSpec((width, tile), lambda j: (0, j))
    wide = pl.BlockSpec((tile, width), lambda j: (j, 0))
    return pl.pallas_call(
        dense_kernel,
        grid=(units // tile,),
        in_specs=[rows, rows, tall, tall, wide],
        out_specs=[rows, rows, tall, tall, wide],
        out_shape=[
            jax.ShapeDtypeStruct((tokens, width), F32),
            jax.ShapeDtypeStruct((tokens, width), F32),
            jax.ShapeDtypeStruct((width, units), BF16),
            jax.ShapeDtypeStruct((width, units), BF16),
            jax.ShapeDtypeStruct((units, width), BF16),
        ],
        scratch_shapes=[pltpu.VMEM((width, tokens), BF16)],
        compiler_params=params(1),
        cost_estimate=cost(18 * tokens * width * units, 30 << 20),
        name="dense",
    )(x, dy, w_gate, w_up, w_out)


def paired_kernel(me_ref, x_ref, dy_ref, *refs):
    parts_a, parts_b = refs[0:3], refs[3:6]
    y_ref, dx_ref, share_ref, ka_ref, wa_ref, kb_ref, wb_ref = refs[6:13]
    xt_ref, y_acc, dx_acc, all_a, all_b, sum_a, sum_b = refs[13:]
    step = pl.program_id(0)
    tokens, width = y_ref.shape
    me = me_ref[0]

    def place_a(r):
        return me ^ zyx_of(r)

    def place_b(r):
        return me ^ ((r & 3) << 2 | (r >> 3) << 1 | (r >> 2 & 1))

    def z_kept(place):
        return lambda r: place(r) ^ (me & 12)

    @pl.when(step == 0)
    def _():
        y_acc[...] = jnp.zeros_like(y_acc)
        dx_acc[...] = jnp.zeros_like(dx_acc)
        xt_ref[...] = flipped(x_ref[...])
        for parts, every, place in ((parts_a, all_a, place_a), (parts_b, all_b, place_b)):
            first = 0
            for part in parts:
                for k in range(part.shape[0]):
                    every[place(first + k)] = part[k]
                first += part.shape[0]

    at = pl.ds(pl.multiple_of(step * 48, 16), 48)
    four = pl.ds(step * 4, 4)
    wg, wu = all_a[:, at, :].reshape(width, 256), all_b[:, at, :].reshape(width, 256)
    wo = jnp.concatenate(
        [
            jnp.concatenate(
                [half[four, 192 + k * 32 : 224 + k * 32, :] for half in (all_a, all_b)], axis=1
            ).reshape(256, 256)
            for k in range(width // 256)
        ],
        axis=1,
    )
    x, dy = x_ref[...], dy_ref[...]
    act, d_gate, d_up = swiglu(mm(x, wg), mm(x, wu), mm(dy, wo, NT))
    y_acc[...] += mm(act, wo)
    dx_acc[...] += mm(d_gate, wg, NT) + mm(d_up, wu, NT)
    sum_a[:, at, :] = mm(xt_ref[...], d_gate).astype(BF16).reshape(16, 48, 256)
    sum_b[:, at, :] = mm(xt_ref[...], d_up).astype(BF16).reshape(16, 48, 256)
    go = mm(act, dy, TN).astype(BF16).reshape(4, 64, width)
    for k in range(width // 256):
        block = go[:, :, k * 256 : k * 256 + 256]
        sum_a[four, 192 + k * 32 : 224 + k * 32, :] = block[:, :32]
        sum_b[four, 192 + k * 32 : 224 + k * 32, :] = block[:, 32:]

    @pl.when(step == pl.num_programs(0) - 1)
    def _():
        y_ref[...] = y_acc[:tokens, :]
        dx_ref[...] = dx_acc[:tokens, :]
        share_ref[:tokens, :] = y_acc[tokens:, :].astype(BF16)
        share_ref[tokens:, :] = dx_acc[tokens:, :].astype(BF16)
        for kept, away, total, place in (
            (ka_ref, wa_ref, sum_a, z_kept(place_a)),
            (kb_ref, wb_ref, sum_b, z_kept(place_b)),
        ):
            for r in range(8):
                kept[r] = total[place(r)]
                away[r] = total[place(r + 8)]


def paired(me, x, dy, parts_a, parts_b):
    every, width = x.shape
    tokens = every // 2
    block = parts_a[0].shape[1:]
    rows = pl.BlockSpec((every, width), lambda j, s: (0, 0))
    part = pl.BlockSpec((tokens, width), lambda j, s: (0, 0))

    def blocks(count):
        return pl.BlockSpec((count,) + block, lambda j, s: (0, 0, 0))

    return pl.pallas_call(
        paired_kernel,
        grid_spec=pltpu.PrefetchScalarGridSpec(
            num_scalar_prefetch=1,
            grid=(4,),
            in_specs=[rows, rows] + [blocks(4), blocks(4), blocks(8)] * 2,
            out_specs=[part, part, rows] + [blocks(8)] * 4,
            scratch_shapes=[pltpu.VMEM((width, every), BF16)]
            + [pltpu.VMEM((every, width), F32)] * 2
            + [pltpu.VMEM((16,) + block, BF16)] * 4,
        ),
        out_shape=[
            jax.ShapeDtypeStruct((tokens, width), F32),
            jax.ShapeDtypeStruct((tokens, width), F32),
            jax.ShapeDtypeStruct((every, width), BF16),
        ]
        + [jax.ShapeDtypeStruct((8,) + block, BF16)] * 4,
        compiler_params=params(1, 60),
        cost_estimate=cost(18 * every * width * 1024, 30 << 20),
        name="dense_pair",
    )(me, x, dy, *parts_a, *parts_b)


def lane_row(column):
    shape = (column.shape[0], LANES)
    here = lax.broadcasted_iota(jnp.int32, shape, 0) == lax.broadcasted_iota(jnp.int32, shape, 1)
    return jnp.sum(jnp.where(here, column, 0.0), axis=0, keepdims=True)


def noted(columns):
    row = lax.broadcasted_iota(jnp.int32, (16, LANES), 0)
    tile = jnp.zeros((16, LANES), F32)
    for k, column in enumerate(columns):
        values = lane_row(column)
        high = values.astype(BF16).astype(F32)
        tile = jnp.where(row == 2 * k, high, jnp.where(row == 2 * k + 1, values - high, tile))
    return tile.astype(BF16)


def expert_kernel(own_ref, x_ref, dy_ref, other_ref, misc_ref, wg_ref, wu_ref, wo_ref, *refs, low):
    y_ref, dx_ref, dgate_ref, deo_ref, act_ref, dg_ref, du_ref, y_acc, dx_acc = refs[-9:]
    earlier_refs = refs[:-9]
    step = pl.program_id(0)

    def dy_rows():
        if len(dy_ref.shape) == 2:
            return dy_ref[...]
        part = x_ref.shape[0] // dy_ref.shape[0]
        return dy_ref[:, low : low + part, :].reshape(x_ref.shape)

    @pl.when(step == 0)
    def _():
        y_acc[...] = jnp.zeros_like(y_acc)
        dx_acc[...] = jnp.zeros_like(dx_acc)
        logits = mm(x_ref[...], misc_ref[...])
        lane = lax.broadcasted_iota(jnp.int32, logits.shape, 1)
        other = other_ref[...].astype(jnp.int32)
        mine = jnp.sum(jnp.where(lane == own_ref[0], logits, 0.0), axis=1, keepdims=True)
        theirs = jnp.sum(jnp.where(lane == other, logits, 0.0), axis=1, keepdims=True)
        top = jnp.maximum(mine, theirs)
        mine, theirs = jnp.exp(mine - top), jnp.exp(theirs - top)
        deo_ref[...] = (mine / (mine + theirs) * dy_rows().astype(F32)).astype(BF16)

    x, deo = x_ref[...], deo_ref[...]
    wg, wu, wo = wg_ref[0], wu_ref[0], wo_ref[0]
    act, d_gate, d_up = swiglu(mm(x, wg), mm(x, wu), mm(deo, wo, NT))
    y_acc[...] += mm(act, wo)
    dx_acc[...] += mm(d_gate, wg, NT) + mm(d_up, wu, NT)
    act_ref[...] = act
    dg_ref[...] = d_gate
    du_ref[...] = d_up

    @pl.when(step == pl.num_programs(0) - 1)
    def _():
        y = y_acc[...].astype(BF16)
        y_ref[...] = y
        dgate = jnp.sum(y.astype(F32) * dy_rows().astype(F32), axis=1, keepdims=True)
        dgate_ref[...] = dgate
        if not earlier_refs:
            dx_ref[...] = dx_acc[...].astype(BF16)
        else:
            sources = dx_ref.shape[0]
            part, before = dgate.shape[0] // sources, earlier_refs[0].shape[0] // sources
            dx_ref[:, :part, :] = dx_acc[...].astype(BF16).reshape(sources, part, dx_ref.shape[2])
            dx_ref[:, part:, LANES:] = jnp.zeros((sources, 16, dx_ref.shape[2] - LANES), BF16)
            for k in range(sources):
                dx_ref[k, part:, :LANES] = noted(
                    [
                        dgate[k * part : (k + 1) * part],
                        earlier_refs[0][k * before : (k + 1) * before, :],
                    ]
                )


def expert(own, x, dy, low, other, misc, w_in, w_out, earlier=None, tile=256):
    slots, width = x.shape
    units = w_out.shape[1]
    steps = units // tile
    rows = pl.BlockSpec((slots, width), lambda j, s: (0, 0))
    column = pl.BlockSpec((slots, 1), lambda j, s: (0, 0))
    saved = pl.BlockSpec((slots, tile), lambda j, s: (0, j))
    every = pl.BlockSpec(dy.shape, lambda j, s: (0,) * len(dy.shape))
    dx_shape, more = (slots, width), []
    if earlier is not None:
        dx_shape, more = (dy.shape[0], slots // dy.shape[0] + 16, width), [earlier]
    dx_spec = pl.BlockSpec(dx_shape, lambda j, s: (0,) * len(dx_shape))
    return pl.pallas_call(
        functools.partial(expert_kernel, low=low),
        grid_spec=pltpu.PrefetchScalarGridSpec(
            num_scalar_prefetch=1,
            grid=(steps,),
            in_specs=[
                rows,
                every,
                column,
                pl.BlockSpec(misc.shape, lambda j, s: (0, 0)),
                pl.BlockSpec((1, width, tile), lambda j, s: (0, 0, j)),
                pl.BlockSpec((1, width, tile), lambda j, s: (0, 0, j + steps)),
                pl.BlockSpec((1, tile, width), lambda j, s: (0, j, 0)),
                *[pl.BlockSpec(array.shape, lambda j, s: (0, 0)) for array in more],
            ],
            out_specs=[rows, dx_spec, column, rows, saved, saved, saved],
            scratch_shapes=[pltpu.VMEM((slots, width), F32)] * 2,
        ),
        out_shape=[
            jax.ShapeDtypeStruct((slots, width), BF16),
            jax.ShapeDtypeStruct(dx_shape, BF16),
            jax.ShapeDtypeStruct((slots, 1), F32),
            jax.ShapeDtypeStruct((slots, width), BF16),
        ]
        + [jax.ShapeDtypeStruct((slots, units), BF16)] * 3,
        compiler_params=params(1),
        cost_estimate=cost(12 * slots * width * units, 40 << 20),
        name="expert",
    )(own, x, dy, other, misc, w_in, w_in, w_out, *more)


def expert_grads_kernel(seq_ref, *refs):
    count = (len(refs) - 4) // 6
    sets = [refs[k * 5 : k * 5 + 5] for k in range(count)]
    in_kept, in_away, out_kept, out_away = refs[5 * count : 5 * count + 4]
    turned_x = refs[5 * count + 4 :]
    step, half = pl.program_id(0), pl.num_programs(0) // 2

    @pl.when(step == 0)
    def _():
        for xt_ref, one in zip(turned_x, sets, strict=True):
            xt_ref[...] = flipped(one[0][...])

    def total(of):
        return sum((of(k) for k in range(1, count)), of(0)).astype(BF16)

    gate = total(lambda k: mm(turned_x[k][...], sets[k][3][...]))
    up = total(lambda k: mm(turned_x[k][...], sets[k][4][...]))
    down = total(lambda k: mm(sets[k][2][...], sets[k][1][...], TN))
    across = seq_ref[0] // 2

    def put(in_ref, out_ref):
        in_ref[across] = gate
        in_ref[1 - across] = up
        out_ref[0] = down

    @pl.when(step < half)
    def _():
        put(in_away, out_away)

    @pl.when(step >= half)
    def _():
        put(in_kept, out_kept)


def expert_grads(seq, sets, tile=256):
    width, units = sets[0][0].shape[1], sets[0][2].shape[1]
    steps = units // tile
    half = steps // 2
    part = units // 4

    def core_of(j, s):
        return jnp.where(j < half, 1 - s[0] % 2, s[0] % 2)

    def inner(j, s):
        return core_of(j, s) * half + j % half

    def outer(j, s):
        owner = 2 * ((s[0] // 2) ^ (j % half // (half // 2))) + core_of(j, s)
        return owner * (half // 2) + j % (half // 2)

    in_specs = []
    for x, *_ in sets:
        rows = pl.BlockSpec(x.shape, lambda j, s: (0, 0))
        saved = pl.BlockSpec((x.shape[0], tile), lambda j, s: (0, inner(j, s)))
        acts = pl.BlockSpec((x.shape[0], tile), lambda j, s: (0, outer(j, s)))
        in_specs += [rows, rows, acts, saved, saved]

    def kept(j):
        return jnp.maximum(j - half, 0)

    def away(j):
        return jnp.minimum(j, half - 1)

    def places(of):
        return [
            pl.BlockSpec((2, width, tile), lambda j, s: (0, 0, of(j))),
            pl.BlockSpec(
                (1, tile, width), lambda j, s: (of(j) // (half // 2), of(j) % (half // 2), 0)
            ),
        ]

    keeps, aways = places(kept), places(away)
    in_shape = jax.ShapeDtypeStruct((2, width, 2 * part), BF16)
    out_shape = jax.ShapeDtypeStruct((2, part, width), BF16)
    slots = sum(one[0].shape[0] for one in sets)
    return pl.pallas_call(
        expert_grads_kernel,
        grid_spec=pltpu.PrefetchScalarGridSpec(
            num_scalar_prefetch=1,
            grid=(steps,),
            in_specs=in_specs,
            out_specs=[keeps[0], aways[0], keeps[1], aways[1]],
            scratch_shapes=[pltpu.VMEM((width, one[0].shape[0]), BF16) for one in sets],
        ),
        out_shape=[in_shape, in_shape, out_shape, out_shape],
        compiler_params=params(1),
        cost_estimate=cost(2 * slots * width * units, 4 << 20),
        name="expert_grads",
    )(seq, *[array for one in sets for array in one])


def share_block(tokens, width, index):
    return pl.BlockSpec((tokens, width), lambda i: (index, 0))


def middle_back_kernel(
    dhn_ref, share_ref, slots_ref, routes_ref, gates_ref, misc_ref, hidden_ref, hn_ref,
    dy_ref, ctx_ref, w_ref, seq_ref, *refs, experts, parts,
):
    back_refs, (dh_ref, dctx_ref, grad_ref) = refs[:-3], refs[-3:]
    tokens = dhn_ref.shape[0]
    slots = experts * sum(parts)
    place = lax.broadcasted_iota(jnp.int32, (tokens, slots), 1)
    is0, is1 = place == slots_ref[:, 0:1], place == slots_ref[:, 1:2]
    pick = jnp.where(is0 | is1, 1.0, 0.0).astype(BF16)
    came = jnp.zeros(hidden_ref.shape, F32)
    first = 0
    for part, back_ref in zip(parts, back_refs, strict=False):
        rows = experts * part
        back = back_ref[...]
        if len(back.shape) == 3:
            back = back[:, :part, :].reshape(rows, back.shape[2])
        came = came + mm(pick[:, first : first + rows], back)
        first += rows
    if len(parts) == 1:
        dgate = back_refs[1][...]
        dg0 = jnp.sum(jnp.where(is0, dgate, 0.0), axis=1, keepdims=True)
        dg1 = jnp.sum(jnp.where(is1, dgate, 0.0), axis=1, keepdims=True)
    else:
        notes = back_refs[1][:, parts[1] :, :LANES].astype(F32)
        tables = [notes[:, 2, :] + notes[:, 3, :], notes[:, 0, :] + notes[:, 1, :]]
        spot = lax.broadcasted_iota(jnp.int32, (tokens, LANES), 1)
        found = []
        for k in range(2):
            route, slot = routes_ref[:, k : k + 1], slots_ref[:, k : k + 1]
            value, first = jnp.zeros((tokens, 1), F32), 0
            for part, table in zip(parts, tables, strict=True):
                line = jnp.zeros((tokens, LANES), F32)
                for e in range(experts):
                    line = jnp.where(route == e, table[e : e + 1, :], line)
                inside = (slot >= first) & (slot < first + experts * part)
                here = inside & (spot == slot - first - route * part)
                value = value + jnp.sum(jnp.where(here, line, 0.0), axis=1, keepdims=True)
                first += experts * part
            found.append(value)
        dg0, dg1 = found
    g0, g1 = gates_ref[:, 0:1], gates_ref[:, 1:2]
    mean = g0 * dg0 + g1 * dg1
    lane = lax.broadcasted_iota(jnp.int32, (tokens, LANES), 1)
    dlogits = (
        jnp.where(lane == routes_ref[:, 0:1], g0 * (dg0 - mean), 0.0)
        + jnp.where(lane == routes_ref[:, 1:2], g1 * (dg1 - mean), 0.0)
    ).astype(BF16)
    misc = misc_ref[...]
    dhn = dhn_ref[...] + share_ref[...].astype(F32) + mm(dlogits, misc, NT) + came
    hidden = hidden_ref[...]
    r2 = lax.rsqrt(jnp.mean(hidden * hidden, axis=1, keepdims=True) + EPS)
    z2 = hidden * r2
    gain = misc.astype(F32).T[experts : experts + 1, :]
    gain_grad = jnp.sum(dhn * z2, axis=0, keepdims=True)
    dz2 = dhn * gain
    dh = dy_ref[...].astype(F32) + r2 * (dz2 - z2 * jnp.mean(dz2 * z2, axis=1, keepdims=True))
    dh_ref[...] = dh
    dhb = dh.astype(BF16)
    for k in range(dctx_ref.shape[0]):
        rows = dctx_ref.shape[1]
        at = pl.ds(pl.multiple_of((seq_ref[0] ^ k) * rows, 16), rows)
        dctx_ref[k] = mm(w_ref[at, :], dhb, NT).astype(BF16)
    width = w_ref.shape[0]
    grad_ref[:, :width] = mm(ctx_ref[...], dhb).astype(BF16)
    small = mm(dlogits, hn_ref[...], TN)
    row = lax.broadcasted_iota(jnp.int32, small.shape, 0)
    small = jnp.where(row == experts, gain_grad, small)
    grad_ref[:, width:] = small.T.astype(BF16)


def middle_back(dhn, share, backs, slots, routes, gates, misc, hidden, hn, dy, ctx, w_attn, seq, seq_devs, experts, parts):
    tokens, width = hidden.shape
    return pl.pallas_call(
        functools.partial(middle_back_kernel, experts=experts, parts=parts),
        grid=(1,),
        in_specs=[whole(), share_block(tokens, width, 1)]
        + [whole()] * 9
        + [pl.BlockSpec(memory_space=pltpu.SMEM)]
        + [whole()] * len(backs),
        out_specs=[whole()] * 3,
        out_shape=[
            jax.ShapeDtypeStruct((tokens, width), F32),
            jax.ShapeDtypeStruct((seq_devs, width // seq_devs, tokens), BF16),
            jax.ShapeDtypeStruct((width, width + LANES), BF16),
        ],
        compiler_params=params(),
        cost_estimate=cost(3e9, 16 << 20),
        name="middle_back",
    )(dhn, share, slots, routes, gates, misc, hidden, hn, dy, ctx, w_attn, seq, *backs)


def output_kernel(hidden_ref, dense_ref, share_ref, slots_ref, gates_ref, *refs):
    came_refs, out_ref = refs[:-1], refs[-1]
    mixture = jnp.zeros(hidden_ref.shape, F32)
    first = 0
    for came_ref in came_refs:
        tokens, slots = hidden_ref.shape[0], came_ref.shape[0]
        place = first + lax.broadcasted_iota(jnp.int32, (tokens, slots), 1)
        for k in range(2):
            pick = jnp.where(place == slots_ref[:, k : k + 1], 1.0, 0.0).astype(BF16)
            mixture = mixture + gates_ref[:, k : k + 1] * mm(pick, came_ref[...])
        first += slots
    out_ref[...] = hidden_ref[...] + dense_ref[...] + share_ref[...].astype(F32) + mixture


def output_of(hidden, shared, share, cames, slots, gates):
    return pl.pallas_call(
        output_kernel,
        grid=(1,),
        in_specs=[whole(), whole(), share_block(*hidden.shape, 0)] + [whole()] * (2 + len(cames)),
        out_specs=whole(),
        out_shape=jax.ShapeDtypeStruct(hidden.shape, F32),
        compiler_params=params(),
        cost_estimate=cost(2e9, 8 << 20),
        name="output_of",
    )(hidden, shared, share, slots, gates, *cames)


def qkv_back_kernel(seq_ref, *refs):
    count = len(ORDER)
    x_refs, d_refs, refs = refs[:count], refs[count:-9], refs[-9:]
    w_ref, cos_ref, sin_ref, kept_ref, away_ref, g_ref, acc_ref, gain_ref, z_ref = refs
    step = pl.program_id(0)
    columns = w_ref.shape[1] - 64

    @pl.when(step == 0)
    def _():
        acc_ref[...] = jnp.zeros_like(acc_ref)
        gain_ref[...] = jnp.zeros_like(gain_ref)

    for at_step, k in enumerate(ORDER):

        @pl.when(step == at_step)
        def _(x_ref=x_refs[k]):
            z_ref[...], _ = first_norm(x_ref[...])

    z1 = z_ref[...]
    xn_t = (z1 * gain_row(w_ref)).T.astype(BF16)
    cosine, sine = cos_ref[...], -sin_ref[...]
    pieces = []
    for d_ref in d_refs:
        for c in range(2):
            pieces.extend(turned(d_ref[0, c * 64 : c * 64 + 64, :].astype(F32), cosine, sine))
        pieces.append(d_ref[0, 128:192, :].astype(F32))
    pieces.append(jnp.zeros((64, z1.shape[0]), F32))
    d_rows = jnp.concatenate(pieces, axis=0).T.astype(BF16)
    dxn = mm(d_rows, w_ref[...], NT)
    acc_ref[...] += mm(xn_t, d_rows)
    gain_ref[0:1, :] += jnp.sum(dxn * z1, axis=0, keepdims=True)

    @pl.when(step < count // 2)
    def _():
        away_ref[0] = dxn.astype(BF16)

    @pl.when(step >= count // 2)
    def _():
        kept_ref[0] = dxn.astype(BF16)

    @pl.when(step == pl.num_programs(0) - 1)
    def _():
        split = columns + 64 - LANES
        g_ref[:, :split] = acc_ref[:, :split].astype(BF16)
        row = lax.broadcasted_iota(jnp.int32, (LANES, gain_ref.shape[1]), 0)
        gain = jnp.where(row == LANES // 2, gain_ref[0:1, :], 0.0).T
        g_ref[:, split:] = (acc_ref[:, split:] + gain).astype(BF16)


ORDER = (1, 3, 0, 2)


def qkv_back(seq, xs, d_heads, w, cosine, sine):
    tokens, width = xs[0].shape

    def place(i, s):
        k = jnp.where(i < 2, 2 * i + 1, 2 * i - 4)
        return k ^ s[0]

    angles = pl.BlockSpec((32, tokens), lambda i, s: (0, place(i, s)))
    rows = pl.BlockSpec((tokens, width), lambda i, s: (0, 0))
    grads = pl.BlockSpec((1, 192, tokens), lambda i, s: (place(i, s), 0, 0))
    pair = jax.ShapeDtypeStruct((2, tokens, width), BF16)
    return pl.pallas_call(
        qkv_back_kernel,
        grid_spec=pltpu.PrefetchScalarGridSpec(
            num_scalar_prefetch=1,
            grid=(len(ORDER),),
            in_specs=[rows] * len(xs)
            + [grads] * len(d_heads)
            + [pl.BlockSpec(w.shape, lambda i, s: (0, 0)), angles, angles],
            out_specs=[
                pl.BlockSpec((1, tokens, width), lambda i, s: (jnp.maximum(i - 2, 0), 0, 0)),
                pl.BlockSpec((1, tokens, width), lambda i, s: (jnp.minimum(i, 1), 0, 0)),
                pl.BlockSpec(w.shape, lambda i, s: (0, 0)),
            ],
            scratch_shapes=[
                pltpu.VMEM(w.shape, F32),
                pltpu.VMEM((8, width), F32),
                pltpu.VMEM((tokens, width), F32),
            ],
        ),
        out_shape=[pair, pair, jax.ShapeDtypeStruct(w.shape, BF16)],
        compiler_params=params(1),
        cost_estimate=cost(12e9, 12 << 20),
        name="qkv_back",
    )(seq, *xs, *d_heads, w, cosine, sine)


def input_back_kernel(x_ref, dh_ref, w_ref, *refs):
    dxn_refs, out_ref = refs[:-1], refs[-1]
    z1, r1 = first_norm(x_ref[...])
    dz1 = add_up([ref[...] for ref in dxn_refs]) * gain_row(w_ref)
    out_ref[...] = dh_ref[...] + r1 * (dz1 - z1 * jnp.mean(dz1 * z1, axis=1, keepdims=True))


def input_back(x, dh, w, dxns):
    return pl.pallas_call(
        input_back_kernel,
        in_specs=[whole()] * (3 + len(dxns)),
        out_specs=whole(),
        out_shape=jax.ShapeDtypeStruct(dh.shape, F32),
        compiler_params=params(),
        cost_estimate=cost(1e8, 6 << 20),
        name="input_back",
    )(x, dh, w, *dxns)


def slot_plan(routes, order, experts, parts):
    before = (order[:, None] > order[None, :]).astype(BF16)
    ids = jnp.arange(experts, dtype=jnp.int32)
    first = (routes[:, 0:1] == ids).astype(BF16)
    second = (routes[:, 1:2] == ids).astype(BF16)
    earlier = mm(before, jnp.concatenate([first, second], axis=1))
    every = jnp.sum(first.astype(F32), axis=0, keepdims=True)
    place0 = jnp.sum(earlier[:, :experts] * first.astype(F32), axis=1)
    place1 = jnp.sum((earlier[:, experts:] + every) * second.astype(F32), axis=1)
    place = jnp.stack([place0, place1], axis=1).astype(jnp.int32)
    capacity = sum(parts)
    every = jnp.where(place < capacity, routes * capacity + place, experts * capacity)
    slot = jnp.full(place.shape, experts * capacity, jnp.int32)
    low = 0
    for part in parts:
        inside = (place >= low) & (place < low + part)
        slot = jnp.where(inside, experts * low + routes * part + place - low, slot)
        low += part
    return slot, every


def padded(shard, columns):
    return jnp.pad(shard, ((0, 0), (0, columns - shard.shape[1])))


def by_core(columns):
    rows, count = columns.shape
    tiles = count // 512
    return columns.reshape(rows, tiles, 4, 2, 64).transpose(3, 1, 0, 2, 4).reshape(2, tiles, rows, 256)


def paired_shards(shared_in, shared_out):
    units, width = shared_in.shape[1] // 2, shared_out.shape[1]
    shard = jnp.stack([by_core(shared_in[:, :units]), by_core(shared_in[:, units:])], axis=1)
    me = coordinates()["c"]
    away = lax.dynamic_index_in_dim(shard, 1 - me, 0, False)
    kept = lax.dynamic_index_in_dim(shard, me, 0, False)
    inner = ordered(kept, flip(away, "c"), me, 2).reshape(2, -1, 256)
    down = shared_out.reshape(2, 32, width // 256, 256).transpose(0, 2, 1, 3).reshape(2, -1, 256)
    return jnp.concatenate([inner, down], axis=1)


def paired_grads(sum_a, sum_b):
    me = coordinates()["c"]
    inner = jnp.stack([sum_a[:192], sum_b[:192]]).reshape(2, 4, 2, 24, 256)
    away = lax.dynamic_index_in_dim(inner, 1 - me, 2, False)
    kept = lax.dynamic_index_in_dim(inner, me, 2, False)
    both = ordered(kept, flip(away, "c"), me, 0).reshape(2, 2, 4, 24, 4, 64)
    inner = both.transpose(3, 1, 2, 4, 0, 5).reshape(24, -1)
    down = jnp.stack([sum_a[192:], sum_b[192:]]).reshape(2, 3, 32, 256)
    return inner, down.transpose(0, 2, 1, 3).reshape(64, -1)


def scalar(value):
    return value.astype(jnp.int32).reshape(1)


def split_parts(array, sizes):
    found, low = [], 0
    for size in sizes:
        found.append(array[low : low + size])
        low += size
    return found


def on_device(
    layer_input, cotangent, segments, routes, order, norm1_gain, attn_qkv, attn_out,
    norm2_gain, router, shared_in, shared_out, expert_in, expert_out,
):
    tokens, width = layer_input.shape
    seq_devs = lax.axis_size("seq")
    experts = lax.axis_size("dp")
    capacity = max(2, (18 * tokens + 8 * experts - 1) // (8 * experts))
    small = small_torus()
    parts = (80, capacity - 80) if small and capacity == 144 else (capacity,)
    sizes = [experts * part for part in parts]
    slots = experts * capacity
    units = shared_in.shape[1] // 2
    columns = 3 * width // seq_devs
    seq = scalar(lax.axis_index("seq"))

    shard_rows = norm1_gain.shape[0]
    head_shard = jnp.concatenate(
        [
            attn_qkv.reshape(-1, seq_devs, columns).transpose(1, 0, 2),
            jnp.broadcast_to(norm1_gain[None, :, None], (seq_devs, shard_rows, 1)),
            jnp.zeros((seq_devs, shard_rows, 63), BF16),
        ],
        axis=2,
    )
    head_shard = swap(head_shard, "seq").reshape(-1, columns + 64)
    misc_shard = jnp.concatenate(
        [attn_out, padded(jnp.concatenate([router, norm2_gain[:, None]], axis=1), LANES)], axis=1
    )
    slot_of, expert_slot = slot_plan(routes, order, experts, parts)
    every_slot = jnp.arange(slots, dtype=jnp.int32)[:, None]

    def pick_of(rows):
        return ((every_slot == rows[0:1]) | (every_slot == rows[1:2])).astype(BF16)

    rows = expert_slot.T
    pick_dy = pick_of(rows)
    routes_f = routes.astype(F32)
    other = jnp.sum(
        jnp.where(every_slot == rows[0:1], routes_f[:, 1][None, :], 0.0)
        + jnp.where(every_slot == rows[1:2], routes_f[:, 0][None, :], 0.0),
        axis=1,
    ).reshape(experts, capacity)
    pick = pick_of(slot_of.T)
    dy_send = mm(pick_dy, cotangent).astype(BF16).reshape(experts, capacity, width)
    frequency = BASE ** (-(jnp.arange(32, dtype=F32) * 2.0 / 64))
    places = jnp.arange(tokens * seq_devs, dtype=jnp.int32)
    angles = places.astype(F32)[None, :] * frequency[:, None]
    cosine, sine = jnp.cos(angles), jnp.sin(angles)

    block_rows = head_shard.shape[0]
    extra = -(-capacity // block_rows)
    notes = jnp.pad(other.astype(BF16), ((0, 0), (0, extra * block_rows - capacity)))
    notes = notes.reshape(experts, block_rows, extra)
    packed = jnp.concatenate(
        [
            jnp.broadcast_to(head_shard[None, :, : columns + 1], (experts, block_rows, columns + 1)),
            notes,
            jnp.zeros((experts, block_rows, 63 - extra), BF16),
        ],
        axis=2,
    )
    packed = swap(packed, "dp")
    w_parts = [packed.reshape(1, -1, columns + 64)]
    notes = packed[:, :, columns + 1 : columns + 1 + extra].reshape(experts, -1)[:, :capacity]
    others, low = [], 0
    for part in parts:
        others.append(notes[:, low : low + part].astype(F32).reshape(-1, 1))
        low += part
    if small:
        here = coordinates()
        me = scalar(here["z"] * 4 + here["y"] * 2 + here["x"])
        along_x = flip(after(layer_input, head_shard), "x")
        token_blocks = [layer_input, flip(layer_input, "c"), along_x, flip(along_x, "c")]
        misc_z = z_gather(after(join(misc_shard, "c", 0).reshape(48, -1), *w_parts))
        misc_parts = [misc_z, flip(after(misc_z, *w_parts), "y")]
    else:
        me = jnp.zeros((1,), jnp.int32)
        gathered = relative(lax.all_gather(layer_input, "seq", axis=0, tiled=False))
        token_blocks = [gathered[k] for k in range(seq_devs)]
        misc_parts = [lax.all_gather(misc_shard, AXES, axis=0, tiled=True)[None]]
    w_parts, pick, routes = (lambda v: (v[:-2], *v[-2:]))(together([*w_parts, pick, routes]))
    dy_rows = swap(after(dy_send, *w_parts, misc_z) if small else dy_send, "dp")

    heads, w_heads = qkv_project(
        seq, scalar(lax.axis_index("dp")), token_blocks, w_parts, cosine, sine
    )
    if small:
        heads = after(heads, misc_z)
        misc_parts.append(flip(jnp.concatenate(misc_parts), "x"))
        shards = z_shards(after(paired_shards(shared_in, shared_out), w_heads))
    ctx_heads, log_totals = attend(seq, heads, segments)
    ctxs = seq_send_twice(ctx_heads)
    hidden, hn, gates, w_attn, misc, ctx, *sends = middle(
        me, seq, ctxs, layer_input, misc_parts, pick, routes, experts, parts
    )

    shards = together(shards, hn) if small else None
    sends[0] = after(sends[0], dy_rows, *shards) if small else sends[0]

    row_parts = [
        swap(send.reshape(experts, part, width), "dp").reshape(-1, width)
        for part, send in zip(parts, sends, strict=True)
    ]
    if small:
        a0, b0 = jnp.stack([part[0] for part in shards]), jnp.stack([part[1] for part in shards])
        a1, b1 = flip(a0, "y"), flip(b0, "x")
        hn_pair = jnp.concatenate([hn, flip(hn, "c")], axis=0)
        dy_pair = jnp.concatenate([cotangent, flip(cotangent, "c")], axis=0)
        row_parts[0] = after(row_parts[0], a0, b0, hn_pair, dy_pair)
    else:
        w_gate = lax.all_gather(shared_in[:, :units], AXES, axis=0, tiled=True)
        w_up = lax.all_gather(shared_in[:, units:], AXES, axis=0, tiled=True)
        w_out = lax.all_gather(shared_out, AXES, axis=0, tiled=True)

    own = scalar(lax.axis_index("dp"))
    sets, eos, dxes, dgates, low = [], [], [], [], 0
    for k, (part, rows, other) in enumerate(zip(parts, row_parts, others, strict=True)):
        if k == 1:
            a0, b0, a1, b1 = together((a0, b0, a1, b1), dxes[0])
            a2, b2 = flip(jnp.concatenate([a0, a1]), "x"), flip(jnp.concatenate([b0, b1]), "y")
        eo, dxe, dgate, deo, act, d_gate, d_up = expert(
            own, rows, dy_rows if small else dy_rows.reshape(-1, width), low, other, misc, expert_in,
            expert_out, dgates[0] if k == 1 else None,
        )
        low += part
        sets.append((rows, deo, act, d_gate, d_up))
        eos.append(eo.reshape(experts, part, width))
        dxes.append(dxe.reshape(experts, -1, width))
        dgates.append(dgate)
    backs = []
    for k, dxe in enumerate(dxes):
        back = swap(after(dxe, *backs), "dp")
        backs.append(back if k else back.reshape(-1, width))
    if not small:
        backs.append(swap(dgates[0].reshape(experts, capacity), "dp").reshape(1, slots))
    held = backs[:1]
    if not small:
        shared, dhn, grad_gate, grad_up, grad_out = dense(hn, cotangent, w_gate, w_up, w_out)
        share = jnp.zeros((2 * tokens, width), BF16)
    sets = [(after(one[0], *held),) + one[1:] for one in sets]
    in_kept, in_away, out_kept, out_away = expert_grads(seq, sets)
    if small:
        hn_pair = after(hn_pair, in_kept)
        shared, dhn, share, *grads = paired(me, hn_pair, dy_pair, (a0, a1, a2), (b0, b1, b2))
        share = flip(share, "c")
        ka, wa, kb, wb = grads
        ca, cb = flip(wa, "x"), flip(wb, "y")
        in_away, out_away = flip(in_away, "c"), flip(out_away, "c")
    dh, dctx, grad_attn = middle_back(
        dhn, share, backs, slot_of, routes, gates, misc, hidden, hn, cotangent, ctx, w_attn,
        seq, seq_devs, experts, parts,
    )

    dctxs = seq_send_twice(dctx)
    if small:
        in_kept, out_kept = together((in_kept, out_kept), dh)
    in_terms, in_far = copies_sum(in_kept, in_away)
    out_terms, out_far = copies_sum(out_kept, out_away)
    if small:
        ca, cb = together((ca, cb), dh)
        wa, wb = add_up([ka[4:], ca[4:]]).astype(BF16), add_up([kb[4:], cb[4:]]).astype(BF16)
        ea, eb = flip(wa, "y"), flip(wb, "x")
        dctxs[0] = after(dctxs[0], in_far, out_far, wa, wb)
    came = swap(after(jnp.concatenate(eos, axis=1), backs[-1]), "dp").reshape(-1, width)
    d_heads = []
    for head in range(columns // 192):
        held = after(heads, *d_heads) if d_heads else heads
        if small and head == 1:
            grad_attn = after(grad_attn, d_heads[0])
            part = half_sum(grad_attn.reshape(8, 2, 2, -1, width + LANES), "c", 2).astype(BF16)
            held = after(held, grad_attn)
        if small and head == 2:
            part = after(part, d_heads[1])
            part_kept = lax.dynamic_index_in_dim(part, here["x"], 1, False)
            part_came = flip(lax.dynamic_index_in_dim(part, 1 - here["x"], 1, False), "x")
        d_heads.append(attend_back(seq, held, dctxs, ctx_heads, log_totals, segments, head))
    if small:
        ea, eb = together((ea, eb), d_heads[0])
        wa, wb = add_up([ka[:4], ca[:4], ea]).astype(BF16), add_up([kb[:4], cb[:4], eb]).astype(BF16)
        sums = z_sum(after(jnp.stack([wa, wb], axis=1), came))
        d_heads[0] = after(d_heads[0], sums, out_terms[2])
    dxn_kept, dxn_away, grad_heads = qkv_back(seq, token_blocks, d_heads, w_heads, cosine, sine)
    if small:
        dxn_away = after(flip(dxn_away, "c"), in_terms[2])
    dxn_terms, dxn_far = copies_sum(dxn_kept, dxn_away)
    input_grad = input_back(layer_input, dh, w_heads, dxn_terms)
    layer_output = output_of(
        hidden, shared, share, [after(came, dxn_far)], expert_slot, gates
    )

    grad_heads = grad_heads.reshape(experts * seq_devs, -1, columns + 64)
    grad_heads = swap(grad_heads, AXES)
    grad_heads = grad_heads.reshape((experts, seq_devs) + grad_heads.shape[1:])
    if small:
        sum_in, sum_out = paired_grads(*together((sums[0], sums[1]), dxn_far))
        part = add_up([part_kept, after(part_came, dxn_far)]).astype(BF16)
        sum_attn = jnp.sum(swap(after(part, grad_heads), "dp").astype(F32), axis=0)
        in_terms, out_terms = together((*in_terms, *out_terms), dxn_far), ()
        in_terms, out_terms = in_terms[:3], in_terms[3:]
    else:
        total = functools.partial(lax.psum_scatter, scatter_dimension=0, tiled=True)
        sum_attn = total(grad_attn, AXES).astype(F32)
        sum_out = total(grad_out, AXES).astype(F32)
        sum_in = jnp.concatenate([total(grad_gate, AXES), total(grad_up, AXES)], axis=1).astype(F32)
    sum_heads = jnp.sum(grad_heads.astype(F32), axis=0)
    return (
        layer_output,
        input_grad,
        jnp.sum(sum_heads[:, :, columns], axis=0),
        sum_heads[:, :, :columns].transpose(1, 0, 2).reshape(-1, seq_devs * columns),
        sum_attn[:, :width],
        sum_attn[:, width + experts],
        sum_attn[:, width : width + experts],
        sum_in,
        sum_out,
        add_up(in_terms)[None],
        add_up(out_terms)[None],
    )


def solution(mesh):
    rows = P(AXES, None)
    return jax.shard_map(
        on_device,
        mesh=mesh,
        in_specs=(
            rows, rows, P("dp", None), rows, P(AXES), P(AXES), rows, rows,
            P(AXES), rows, rows, rows, P("dp", None, None), P("dp", None, None),
        ),
        out_specs=(
            rows, rows, P(AXES), rows, rows, P(AXES), rows, rows, rows,
            P("dp", None, "seq"), P("dp", "seq", None),
        ),
        check_vma=False,
    )
```

```python
import functools

import jax
import jax.numpy as jnp
from jax import lax
from jax.experimental import pallas as pl
from jax.experimental.pallas import tpu as pltpu
from jax.sharding import PartitionSpec as P

HEADS = 12
EPS = 1e-06
BASE = 10000.0
MASKED = -1e30
AXES = ("dp", "seq")
LANES = 128
F32 = jnp.float32
BF16 = jnp.bfloat16
NN = (((1,), (0,)), ((), ()))
NT = (((1,), (1,)), ((), ()))
TN = (((0,), (0,)), ((), ()))


def mm(left, right, dims=NN):
    return lax.dot_general(left, right, dims, preferred_element_type=F32)


def params(steps=0, mib=56):
    semantics = ("arbitrary",) * steps if steps else None
    return pltpu.CompilerParams(dimension_semantics=semantics, vmem_limit_bytes=mib << 20)


def cost(flops, moved):
    return pl.CostEstimate(flops=int(flops), bytes_accessed=int(moved), transcendentals=0)


def whole():
    return pl.BlockSpec(memory_space=pltpu.VMEM)


def pairs(place):
    found = []
    for device in range(32):
        z, y, x, c = device // 8, (device // 4) % 2, (device // 2) % 2, device % 2
        z, y, x, c = place(z, y, x, c)
        found.append((device, ((z * 2 + y) * 2 + x) * 2 + c))
    return found


FLIP = {
    "y": pairs(lambda z, y, x, c: (z, 1 - y, x, c)),
    "x": pairs(lambda z, y, x, c: (z, y, 1 - x, c)),
    "c": pairs(lambda z, y, x, c: (z, y, x, 1 - c)),
    "z1": pairs(lambda z, y, x, c: (z ^ 1, y, x, c)),
    "z2": pairs(lambda z, y, x, c: (z ^ 2, y, x, c)),
    "z3": pairs(lambda z, y, x, c: (z ^ 3, y, x, c)),
    "xc": pairs(lambda z, y, x, c: (z, y, 1 - x, 1 - c)),
}


def coordinates():
    dp, seq = lax.axis_index("dp"), lax.axis_index("seq")
    return {"z": dp // 2, "y": dp % 2, "x": seq // 2, "c": seq % 2}


def small_torus():
    return lax.axis_size("dp") == 8 and lax.axis_size("seq") == 4


def after(value, *others):
    return lax.optimization_barrier((value,) + others)[0]


def together(values, *others):
    return lax.optimization_barrier(tuple(values) + others)[: len(values)]


def ordered(own, came, mine, axis):
    return jnp.where(mine == 0, jnp.stack([own, came], axis), jnp.stack([came, own], axis))


def flip(block, name):
    return lax.ppermute(block, AXES, FLIP[name])


def join(block, name, axis):
    return ordered(block, flip(block, name), coordinates()[name], axis)


def half_sum(part, name, axis):
    me = coordinates()[name]
    away = lax.dynamic_index_in_dim(part, 1 - me, axis, False)
    kept = lax.dynamic_index_in_dim(part, me, axis, False)
    return kept.astype(F32) + flip(away, name).astype(F32)


def z_shards(shard):
    return [shard] + [flip(shard, name) for name in ("z1", "z2", "z3")]


def z_gather(shard):
    return jnp.stack(z_shards(shard))


def z_sum(parts):
    groups = [[0, 2, 4, 6], [1, 3, 5, 7]]
    came = lax.all_to_all(parts, "dp", 0, 0, axis_index_groups=groups, tiled=True)
    return jnp.sum(came.astype(F32), axis=0)


def seq_send(blocks):
    if not small_torus():
        came = relative(swap(relative(blocks), "seq"))
        return [came[k : k + 1] for k in range(blocks.shape[0])]
    return [blocks] + [flip(blocks[k : k + 1], name) for k, name in ((1, "c"), (2, "x"), (3, "xc"))]


def seq_send_twice(blocks):
    if not small_torus():
        return seq_send(blocks)
    far = flip(blocks[2:], "x")
    near = flip(jnp.concatenate([blocks[1:2], far[1:]]), "c")
    return [blocks, near[:1], far[:1], near[1:]]


def relative(blocks):
    places = jnp.arange(blocks.shape[0], dtype=jnp.int32) ^ lax.axis_index("seq").astype(jnp.int32)
    return blocks[places]


def copies_sum(kept, away):
    if not small_torus():
        blocks = relative(jnp.stack([kept[0], away[0], kept[1], away[1]]))
        return [lax.psum_scatter(blocks, "seq", scatter_dimension=0, tiled=False)], kept
    far = (kept[1].astype(F32) + away[1].astype(F32)).astype(BF16)
    return [kept[0], away[0], flip(far, "x")], far


def add_up(terms):
    return sum((term.astype(F32) for term in terms[1:]), terms[0].astype(F32))


def swap(blocks, axis):
    return lax.all_to_all(blocks, axis, split_axis=0, concat_axis=0, tiled=True)


def turned(rows, cosine, sine):
    a, b = rows[:32], rows[32:]
    return a * cosine - b * sine, b * cosine + a * sine


def first_norm(x):
    x = x.astype(F32)
    r1 = lax.rsqrt(jnp.mean(x * x, axis=1, keepdims=True) + EPS)
    return x * r1, r1


def gain_row(w_ref):
    last = w_ref.shape[1] - LANES
    return w_ref[:, last:].astype(F32).T[LANES // 2 : LANES // 2 + 1, :]


def assemble(parts, width_ref, place):
    first = 0
    for part in parts:
        for k in range(part.shape[0]):
            rows = part.shape[1]
            at = pl.multiple_of(place(first + k) * rows, 8)
            width_ref[pl.ds(at, rows), :] = part[k]
        first += part.shape[0]


def qkv_kernel(seq_ref, dp_ref, *refs, sources):
    x_refs, part_refs = refs[:sources], refs[sources:-5]
    cos_ref, sin_ref, out_ref, w_ref, xn_ref = refs[-5:]
    step = pl.program_id(0)

    @pl.when(step == 0)
    def _():
        if len(part_refs) == 1:
            assemble(part_refs, w_ref, lambda r: r)
        else:
            assemble(part_refs, w_ref, lambda r: dp_ref[0] ^ ((r & 3) << 1 | r >> 2))

    for k, x_ref in enumerate(x_refs):

        @pl.when(step == k)
        def _(x_ref=x_ref):
            z1, _ = first_norm(x_ref[...])
            xn_ref[...] = (z1 * gain_row(w_ref)).astype(BF16)

    rows = mm(xn_ref[...], w_ref[...]).T
    cosine, sine = cos_ref[...], sin_ref[...]
    for base in range(0, out_ref.shape[1], 192):
        for c in range(2):
            at = base + c * 64
            a, b = turned(rows[at : at + 64], cosine, sine)
            out_ref[0, at : at + 32, :] = a.astype(BF16)
            out_ref[0, at + 32 : at + 64, :] = b.astype(BF16)
        out_ref[0, base + 128 : base + 192, :] = rows[base + 128 : base + 192].astype(BF16)


def qkv_project(seq, dp, xs, w_parts, cosine, sine):
    tokens, width = xs[0].shape
    across = w_parts[0].shape[2]
    columns = across - 64
    angles = pl.BlockSpec((32, tokens), lambda i, s, d: (0, i ^ s[0]))
    return pl.pallas_call(
        functools.partial(qkv_kernel, sources=len(xs)),
        grid_spec=pltpu.PrefetchScalarGridSpec(
            num_scalar_prefetch=2,
            grid=(len(xs),),
            in_specs=[pl.BlockSpec((tokens, width), lambda i, s, d: (0, 0))] * len(xs)
            + [pl.BlockSpec(part.shape, lambda i, s, d: (0, 0, 0)) for part in w_parts]
            + [angles, angles],
            out_specs=[
                pl.BlockSpec((1, columns, tokens), lambda i, s, d: (i ^ s[0], 0, 0)),
                pl.BlockSpec((width, across), lambda i, s, d: (0, 0)),
            ],
            scratch_shapes=[pltpu.VMEM((tokens, width), BF16)],
        ),
        out_shape=[
            jax.ShapeDtypeStruct((len(xs), columns, tokens), BF16),
            jax.ShapeDtypeStruct((width, across), BF16),
        ],
        compiler_params=params(1),
        cost_estimate=cost(1e9, 1 << 20),
        name="qkv_project",
    )(seq, dp, *xs, *w_parts, cosine, sine)


TILE = 256


def tile_of(ref, row, rows, index):
    per = ref.shape[2] // TILE
    at = (index % per) * TILE
    return ref[index // per, row : row + rows, at : at + TILE]


def flipped(block):
    return block.astype(F32).T.astype(BF16)


def masked(scores, start, i, j, diagonal):
    key = lax.broadcasted_iota(jnp.int32, scores.shape, 0)
    allowed = key >= start - j * TILE
    if diagonal:
        query = lax.broadcasted_iota(jnp.int32, scores.shape, 1)
        allowed = allowed & (key <= query)
    return jnp.where(allowed, scores, MASKED)


def start_of(docs):
    start = jnp.zeros_like(docs)
    for doc in range(1, 4):
        before = jnp.sum(jnp.where(docs < doc, 1, 0), axis=1, keepdims=True)
        start = jnp.where(docs >= doc, before, start)
    return start


def attend_kernel(seq_ref, buf_ref, docs_ref, ctx_ref, lse_ref, k_ref, s_ref, start_ref):
    start_ref[...] = start_of(docs_ref[...])
    tiles = buf_ref.shape[0] * buf_ref.shape[2] // TILE
    per = buf_ref.shape[2] // TILE
    for i in range(tiles):
        rows = slice(i * TILE, (i + 1) * TILE)
        k_ref[rows, :] = flipped(tile_of(buf_ref, 64, 64, i))
        q = (tile_of(buf_ref, 0, 64, i).astype(F32) * 0.125).astype(BF16)
        start = start_ref[0:1, rows]
        top = jnp.full((1, TILE), MASKED, F32)
        for j in range(i + 1):
            keys = slice(j * TILE, (j + 1) * TILE)
            scores = masked(mm(k_ref[keys, :], q), start, i, j, i == j)
            s_ref[keys, :] = scores
            top = jnp.maximum(top, jnp.max(scores, axis=0, keepdims=True))
        total = jnp.zeros((1, TILE), F32)
        context = jnp.zeros((64, TILE), F32)
        for j in range(i + 1):
            probs = jnp.exp(s_ref[j * TILE : (j + 1) * TILE, :] - top)
            total = total + jnp.sum(probs, axis=0, keepdims=True)
            context = context + mm(tile_of(buf_ref, 128, 64, j), probs.astype(BF16))
        at = (i % per) * TILE
        ctx_ref[(i // per) ^ seq_ref[0], :, at : at + TILE] = (context / total).astype(BF16)
        lse_ref[0, 0:1, rows] = top + jnp.log(total)


def attend(seq, buf, docs):
    blocks, rows, tokens = buf.shape
    heads, length = rows // 192, blocks * tokens
    return pl.pallas_call(
        attend_kernel,
        grid_spec=pltpu.PrefetchScalarGridSpec(
            num_scalar_prefetch=1,
            grid=(heads,),
            in_specs=[
                pl.BlockSpec((blocks, 192, tokens), lambda h, s: (0, h, 0)),
                pl.BlockSpec((1, length), lambda h, s: (0, 0)),
            ],
            out_specs=[
                pl.BlockSpec((blocks, 64, tokens), lambda h, s: (0, h, 0)),
                pl.BlockSpec((1, 1, length), lambda h, s: (h, 0, 0)),
            ],
            scratch_shapes=[
                pltpu.VMEM((length, 64), BF16),
                pltpu.VMEM((length, TILE), F32),
                pltpu.VMEM((1, length), jnp.int32),
            ],
        ),
        out_shape=[
            jax.ShapeDtypeStruct((blocks, heads * 64, tokens), BF16),
            jax.ShapeDtypeStruct((heads, 1, length), F32),
        ],
        compiler_params=params(1),
        cost_estimate=cost(3e9, 1 << 20),
        name="attend",
    )(seq, buf, docs)


def attend_back_kernel(
    seq_ref, buf_ref, d0_ref, d1_ref, d2_ref, d3_ref, ctx_ref, lse_ref, docs_ref, out_ref,
    k_ref, v_ref, dk_ref, dv_ref, start_ref, dctx_ref,
):
    for k, block_ref in enumerate((d0_ref, d1_ref, d2_ref, d3_ref)):
        dctx_ref[k ^ seq_ref[0]] = block_ref[0]
    start_ref[...] = start_of(docs_ref[...])
    tiles = buf_ref.shape[0] * buf_ref.shape[2] // TILE
    per = buf_ref.shape[2] // TILE
    for i in range(tiles):
        rows = slice(i * TILE, (i + 1) * TILE)
        k_ref[rows, :] = flipped(tile_of(buf_ref, 64, 64, i))
        v_ref[rows, :] = flipped(tile_of(buf_ref, 128, 64, i))
        q_t = (tile_of(buf_ref, 0, 64, i).astype(F32) * 0.125).astype(BF16)
        d_t = tile_of(dctx_ref, 0, 64, i)
        q_rows, d_rows = flipped(q_t), flipped(d_t)
        at = (i % per) * TILE
        context = ctx_ref[(i // per) ^ seq_ref[0], :, at : at + TILE].astype(F32)
        delta = jnp.sum(d_t.astype(F32) * context, axis=0, keepdims=True)
        start, log_total = start_ref[0:1, rows], lse_ref[0, 0:1, rows]
        d_query = jnp.zeros((64, TILE), F32)
        for j in range(i + 1):
            keys = slice(j * TILE, (j + 1) * TILE)
            scores = masked(mm(k_ref[keys, :], q_t), start, i, j, i == j)
            probs = jnp.exp(scores - log_total)
            d_probs = mm(v_ref[keys, :], d_t)
            d_scores = (probs * (d_probs - delta)).astype(BF16)
            d_query = d_query + mm(tile_of(buf_ref, 64, 64, j), d_scores)
            d_key = mm(d_scores, q_rows)
            d_value = mm(probs.astype(BF16), d_rows)
            if i == j:
                dk_ref[keys, :] = d_key
                dv_ref[keys, :] = d_value
            else:
                dk_ref[keys, :] += d_key
                dv_ref[keys, :] += d_value
        at = (i % per) * TILE
        out_ref[i // per, 0:64, at : at + TILE] = (d_query * 0.125).astype(BF16)
    for i in range(tiles):
        at = (i % per) * TILE
        rows = slice(i * TILE, (i + 1) * TILE)
        out_ref[i // per, 64:128, at : at + TILE] = dk_ref[rows, :].T.astype(BF16)
        out_ref[i // per, 128:192, at : at + TILE] = dv_ref[rows, :].T.astype(BF16)


def attend_back(seq, buf, dctxs, ctx, lse, docs, head):
    blocks, rows, tokens = buf.shape
    length = blocks * tokens
    one = pl.BlockSpec((blocks, 64, tokens), lambda i, s: (0, head, 0))
    return pl.pallas_call(
        attend_back_kernel,
        grid_spec=pltpu.PrefetchScalarGridSpec(
            num_scalar_prefetch=1,
            grid=(1,),
            in_specs=[
                pl.BlockSpec((blocks, 192, tokens), lambda i, s: (0, head, 0)),
                *[pl.BlockSpec((1, 64, tokens), lambda i, s: (0, head, 0))] * 4,
                one,
                pl.BlockSpec((1, 1, length), lambda i, s: (head, 0, 0)),
                pl.BlockSpec((1, length), lambda i, s: (0, 0)),
            ],
            out_specs=pl.BlockSpec((blocks, 192, tokens), lambda i, s: (0, 0, 0)),
            scratch_shapes=[pltpu.VMEM((length, 64), BF16)] * 2
            + [pltpu.VMEM((length, 64), F32)] * 2
            + [pltpu.VMEM((1, length), jnp.int32), pltpu.VMEM((blocks, 64, tokens), BF16)],
        ),
        out_shape=jax.ShapeDtypeStruct((blocks, 192, tokens), BF16),
        compiler_params=params(1),
        cost_estimate=cost(4e9, 1 << 20),
        name="attend_back",
    )(seq, buf, *dctxs, ctx, lse, docs)


def zyx_of(r):
    return (r & 3) << 2 | (r >> 2 & 1) << 1 | r >> 3


def middle_kernel(me_ref, seq_ref, *refs, experts, sources, parts):
    ctx_refs, w_refs = refs[:sources], refs[sources : -9 - parts]
    x_ref, pick_ref, routes_ref = refs[-9 - parts : -6 - parts]
    hidden_ref, hn_ref, gates_ref, attn_ref, misc_ref, ctx_ref = refs[-6 - parts : -parts]
    send_refs = refs[-parts:]
    width = x_ref.shape[1]
    first = 0
    for w_ref in w_refs:
        blocks, rows = w_ref.shape[0], w_ref.shape[1]
        for k in range(blocks):
            place = me_ref[0] ^ zyx_of(first + k)
            at = pl.ds(pl.multiple_of(place * rows, 16), rows)
            attn_ref[at, :] = w_ref[k, :, :width]
            misc_ref[at, :] = w_ref[k, :, width:]
        first += blocks
    for k, block_ref in enumerate(ctx_refs):
        rows = block_ref.shape[1]
        at = pl.ds(pl.multiple_of((seq_ref[0] ^ k) * rows, 16), rows)
        ctx_ref[at, :] = block_ref[0]
    hidden = x_ref[...].astype(F32) + mm(ctx_ref[...], attn_ref[...], TN)
    hidden_ref[...] = hidden
    r2 = lax.rsqrt(jnp.mean(hidden * hidden, axis=1, keepdims=True) + EPS)
    gain = misc_ref[...].astype(F32).T[experts : experts + 1, :]
    hn = (hidden * r2 * gain).astype(BF16)
    hn_ref[...] = hn
    first = 0
    for send_ref in send_refs:
        slots = send_ref.shape[0]
        send_ref[...] = mm(pick_ref[first : first + slots, :], hn).astype(BF16)
        first += slots
    logits = mm(hn, misc_ref[...])
    lane = lax.broadcasted_iota(jnp.int32, logits.shape, 1)
    first = jnp.sum(jnp.where(lane == routes_ref[:, 0:1], logits, 0.0), axis=1, keepdims=True)
    second = jnp.sum(jnp.where(lane == routes_ref[:, 1:2], logits, 0.0), axis=1, keepdims=True)
    top = jnp.maximum(first, second)
    first, second = jnp.exp(first - top), jnp.exp(second - top)
    total = first + second
    gates_ref[...] = jnp.where(lane == 0, first / total, jnp.where(lane == 1, second / total, 0.0))


def middle(me, seq, ctxs, x, w_parts, pick, routes, experts, parts):
    tokens, width = x.shape
    first = pl.BlockSpec((1,) + ctxs[0].shape[1:], lambda i, m, s: (0, 0, 0))

    def full(array):
        return pl.BlockSpec(array.shape, lambda i, m, s: (0,) * len(array.shape))

    out_shape = [
        jax.ShapeDtypeStruct((tokens, width), F32),
        jax.ShapeDtypeStruct((tokens, width), BF16),
        jax.ShapeDtypeStruct((tokens, LANES), F32),
        jax.ShapeDtypeStruct((width, width), BF16),
        jax.ShapeDtypeStruct((width, LANES), BF16),
        jax.ShapeDtypeStruct((width, tokens), BF16),
    ] + [jax.ShapeDtypeStruct((experts * part, width), BF16) for part in parts]
    return pl.pallas_call(
        functools.partial(middle_kernel, experts=experts, sources=len(ctxs), parts=len(parts)),
        grid_spec=pltpu.PrefetchScalarGridSpec(
            num_scalar_prefetch=2,
            grid=(1,),
            in_specs=[first] * len(ctxs) + [full(array) for array in (*w_parts, x, pick, routes)],
            out_specs=[full(array) for array in out_shape],
        ),
        out_shape=out_shape,
        compiler_params=params(1),
        cost_estimate=cost(5e8, 1 << 20),
        name="middle",
    )(me, seq, *ctxs, *w_parts, x, pick, routes)


def swiglu(gate, up, d_act):
    sigma = jax.nn.sigmoid(gate)
    act = (gate * sigma * up).astype(BF16)
    d_gate = (d_act * up * sigma * (1.0 + gate * (1.0 - sigma))).astype(BF16)
    d_up = (d_act * gate * sigma).astype(BF16)
    return act, d_gate, d_up


def dense_kernel(
    x_ref, dy_ref, wg_ref, wu_ref, wo_ref, y_ref, dx_ref, gg_ref, gu_ref, go_ref, xt_ref
):
    @pl.when(pl.program_id(0) == 0)
    def _():
        y_ref[...] = jnp.zeros_like(y_ref)
        dx_ref[...] = jnp.zeros_like(dx_ref)
        xt_ref[...] = flipped(x_ref[...])

    x, dy = x_ref[...], dy_ref[...]
    act, d_gate, d_up = swiglu(mm(x, wg_ref[...]), mm(x, wu_ref[...]), mm(dy, wo_ref[...], NT))
    y_ref[...] += mm(act, wo_ref[...])
    dx_ref[...] += mm(d_gate, wg_ref[...], NT) + mm(d_up, wu_ref[...], NT)
    gg_ref[...] = mm(xt_ref[...], d_gate).astype(BF16)
    gu_ref[...] = mm(xt_ref[...], d_up).astype(BF16)
    go_ref[...] = mm(act, dy, TN).astype(BF16)


def dense(x, dy, w_gate, w_up, w_out, tile=256):
    tokens, width = x.shape
    units = w_out.shape[0]
    rows = pl.BlockSpec((tokens, width), lambda j: (0, 0))
    tall = pl.BlockSpec((width, tile), lambda j: (0, j))
    wide = pl.BlockSpec((tile, width), lambda j: (j, 0))
    return pl.pallas_call(
        dense_kernel,
        grid=(units // tile,),
        in_specs=[rows, rows, tall, tall, wide],
        out_specs=[rows, rows, tall, tall, wide],
        out_shape=[
            jax.ShapeDtypeStruct((tokens, width), F32),
            jax.ShapeDtypeStruct((tokens, width), F32),
            jax.ShapeDtypeStruct((width, units), BF16),
            jax.ShapeDtypeStruct((width, units), BF16),
            jax.ShapeDtypeStruct((units, width), BF16),
        ],
        scratch_shapes=[pltpu.VMEM((width, tokens), BF16)],
        compiler_params=params(1),
        cost_estimate=cost(18 * tokens * width * units, 30 << 20),
        name="dense",
    )(x, dy, w_gate, w_up, w_out)


def paired_kernel(me_ref, x_ref, dy_ref, *refs):
    parts_a, parts_b = refs[0:3], refs[3:6]
    y_ref, dx_ref, share_ref, ka_ref, wa_ref, kb_ref, wb_ref = refs[6:13]
    xt_ref, y_acc, dx_acc, all_a, all_b, sum_a, sum_b = refs[13:]
    step = pl.program_id(0)
    tokens, width = y_ref.shape
    me = me_ref[0]

    def place_a(r):
        return me ^ zyx_of(r)

    def place_b(r):
        return me ^ ((r & 3) << 2 | (r >> 3) << 1 | (r >> 2 & 1))

    def z_kept(place):
        return lambda r: place(r) ^ (me & 12)

    @pl.when(step == 0)
    def _():
        y_acc[...] = jnp.zeros_like(y_acc)
        dx_acc[...] = jnp.zeros_like(dx_acc)
        xt_ref[...] = flipped(x_ref[...])
        for parts, every, place in ((parts_a, all_a, place_a), (parts_b, all_b, place_b)):
            first = 0
            for part in parts:
                for k in range(part.shape[0]):
                    every[place(first + k)] = part[k]
                first += part.shape[0]

    at = pl.ds(pl.multiple_of(step * 48, 16), 48)
    four = pl.ds(step * 4, 4)
    wg, wu = all_a[:, at, :].reshape(width, 256), all_b[:, at, :].reshape(width, 256)
    wo = jnp.concatenate(
        [
            jnp.concatenate(
                [half[four, 192 + k * 32 : 224 + k * 32, :] for half in (all_a, all_b)], axis=1
            ).reshape(256, 256)
            for k in range(width // 256)
        ],
        axis=1,
    )
    x, dy = x_ref[...], dy_ref[...]
    act, d_gate, d_up = swiglu(mm(x, wg), mm(x, wu), mm(dy, wo, NT))
    y_acc[...] += mm(act, wo)
    dx_acc[...] += mm(d_gate, wg, NT) + mm(d_up, wu, NT)
    sum_a[:, at, :] = mm(xt_ref[...], d_gate).astype(BF16).reshape(16, 48, 256)
    sum_b[:, at, :] = mm(xt_ref[...], d_up).astype(BF16).reshape(16, 48, 256)
    go = mm(act, dy, TN).astype(BF16).reshape(4, 64, width)
    for k in range(width // 256):
        block = go[:, :, k * 256 : k * 256 + 256]
        sum_a[four, 192 + k * 32 : 224 + k * 32, :] = block[:, :32]
        sum_b[four, 192 + k * 32 : 224 + k * 32, :] = block[:, 32:]

    @pl.when(step == pl.num_programs(0) - 1)
    def _():
        y_ref[...] = y_acc[:tokens, :]
        dx_ref[...] = dx_acc[:tokens, :]
        share_ref[:tokens, :] = y_acc[tokens:, :].astype(BF16)
        share_ref[tokens:, :] = dx_acc[tokens:, :].astype(BF16)
        for kept, away, total, place in (
            (ka_ref, wa_ref, sum_a, z_kept(place_a)),
            (kb_ref, wb_ref, sum_b, z_kept(place_b)),
        ):
            for r in range(8):
                kept[r] = total[place(r)]
                away[r] = total[place(r + 8)]


def paired(me, x, dy, parts_a, parts_b):
    every, width = x.shape
    tokens = every // 2
    block = parts_a[0].shape[1:]
    rows = pl.BlockSpec((every, width), lambda j, s: (0, 0))
    part = pl.BlockSpec((tokens, width), lambda j, s: (0, 0))

    def blocks(count):
        return pl.BlockSpec((count,) + block, lambda j, s: (0, 0, 0))

    return pl.pallas_call(
        paired_kernel,
        grid_spec=pltpu.PrefetchScalarGridSpec(
            num_scalar_prefetch=1,
            grid=(4,),
            in_specs=[rows, rows] + [blocks(4), blocks(4), blocks(8)] * 2,
            out_specs=[part, part, rows] + [blocks(8)] * 4,
            scratch_shapes=[pltpu.VMEM((width, every), BF16)]
            + [pltpu.VMEM((every, width), F32)] * 2
            + [pltpu.VMEM((16,) + block, BF16)] * 4,
        ),
        out_shape=[
            jax.ShapeDtypeStruct((tokens, width), F32),
            jax.ShapeDtypeStruct((tokens, width), F32),
            jax.ShapeDtypeStruct((every, width), BF16),
        ]
        + [jax.ShapeDtypeStruct((8,) + block, BF16)] * 4,
        compiler_params=params(1, 60),
        cost_estimate=cost(18 * every * width * 1024, 30 << 20),
        name="dense_pair",
    )(me, x, dy, *parts_a, *parts_b)


def lane_row(column):
    shape = (column.shape[0], LANES)
    here = lax.broadcasted_iota(jnp.int32, shape, 0) == lax.broadcasted_iota(jnp.int32, shape, 1)
    return jnp.sum(jnp.where(here, column, 0.0), axis=0, keepdims=True)


def noted(columns):
    row = lax.broadcasted_iota(jnp.int32, (16, LANES), 0)
    tile = jnp.zeros((16, LANES), F32)
    for k, column in enumerate(columns):
        values = lane_row(column)
        high = values.astype(BF16).astype(F32)
        tile = jnp.where(row == 2 * k, high, jnp.where(row == 2 * k + 1, values - high, tile))
    return tile.astype(BF16)


def expert_kernel(own_ref, x_ref, dy_ref, other_ref, misc_ref, wg_ref, wu_ref, wo_ref, *refs, low):
    y_ref, dx_ref, dgate_ref, deo_ref, act_ref, dg_ref, du_ref, y_acc, dx_acc = refs[-9:]
    earlier_refs = refs[:-9]
    step = pl.program_id(0)

    def dy_rows():
        if len(dy_ref.shape) == 2:
            return dy_ref[...]
        part = x_ref.shape[0] // dy_ref.shape[0]
        return dy_ref[:, low : low + part, :].reshape(x_ref.shape)

    @pl.when(step == 0)
    def _():
        y_acc[...] = jnp.zeros_like(y_acc)
        dx_acc[...] = jnp.zeros_like(dx_acc)
        logits = mm(x_ref[...], misc_ref[...])
        lane = lax.broadcasted_iota(jnp.int32, logits.shape, 1)
        other = other_ref[...].astype(jnp.int32)
        mine = jnp.sum(jnp.where(lane == own_ref[0], logits, 0.0), axis=1, keepdims=True)
        theirs = jnp.sum(jnp.where(lane == other, logits, 0.0), axis=1, keepdims=True)
        top = jnp.maximum(mine, theirs)
        mine, theirs = jnp.exp(mine - top), jnp.exp(theirs - top)
        deo_ref[...] = (mine / (mine + theirs) * dy_rows().astype(F32)).astype(BF16)

    x, deo = x_ref[...], deo_ref[...]
    wg, wu, wo = wg_ref[0], wu_ref[0], wo_ref[0]
    act, d_gate, d_up = swiglu(mm(x, wg), mm(x, wu), mm(deo, wo, NT))
    y_acc[...] += mm(act, wo)
    dx_acc[...] += mm(d_gate, wg, NT) + mm(d_up, wu, NT)
    act_ref[...] = act
    dg_ref[...] = d_gate
    du_ref[...] = d_up

    @pl.when(step == pl.num_programs(0) - 1)
    def _():
        y = y_acc[...].astype(BF16)
        y_ref[...] = y
        dgate = jnp.sum(y.astype(F32) * dy_rows().astype(F32), axis=1, keepdims=True)
        dgate_ref[...] = dgate
        if not earlier_refs:
            dx_ref[...] = dx_acc[...].astype(BF16)
        else:
            sources = dx_ref.shape[0]
            part, before = dgate.shape[0] // sources, earlier_refs[0].shape[0] // sources
            dx_ref[:, :part, :] = dx_acc[...].astype(BF16).reshape(sources, part, dx_ref.shape[2])
            dx_ref[:, part:, LANES:] = jnp.zeros((sources, 16, dx_ref.shape[2] - LANES), BF16)
            for k in range(sources):
                dx_ref[k, part:, :LANES] = noted(
                    [
                        dgate[k * part : (k + 1) * part],
                        earlier_refs[0][k * before : (k + 1) * before, :],
                    ]
                )


def expert(own, x, dy, low, other, misc, w_in, w_out, earlier=None, tile=256):
    slots, width = x.shape
    units = w_out.shape[1]
    steps = units // tile
    rows = pl.BlockSpec((slots, width), lambda j, s: (0, 0))
    column = pl.BlockSpec((slots, 1), lambda j, s: (0, 0))
    saved = pl.BlockSpec((slots, tile), lambda j, s: (0, j))
    every = pl.BlockSpec(dy.shape, lambda j, s: (0,) * len(dy.shape))
    dx_shape, more = (slots, width), []
    if earlier is not None:
        dx_shape, more = (dy.shape[0], slots // dy.shape[0] + 16, width), [earlier]
    dx_spec = pl.BlockSpec(dx_shape, lambda j, s: (0,) * len(dx_shape))
    return pl.pallas_call(
        functools.partial(expert_kernel, low=low),
        grid_spec=pltpu.PrefetchScalarGridSpec(
            num_scalar_prefetch=1,
            grid=(steps,),
            in_specs=[
                rows,
                every,
                column,
                pl.BlockSpec(misc.shape, lambda j, s: (0, 0)),
                pl.BlockSpec((1, width, tile), lambda j, s: (0, 0, j)),
                pl.BlockSpec((1, width, tile), lambda j, s: (0, 0, j + steps)),
                pl.BlockSpec((1, tile, width), lambda j, s: (0, j, 0)),
                *[pl.BlockSpec(array.shape, lambda j, s: (0, 0)) for array in more],
            ],
            out_specs=[rows, dx_spec, column, rows, saved, saved, saved],
            scratch_shapes=[pltpu.VMEM((slots, width), F32)] * 2,
        ),
        out_shape=[
            jax.ShapeDtypeStruct((slots, width), BF16),
            jax.ShapeDtypeStruct(dx_shape, BF16),
            jax.ShapeDtypeStruct((slots, 1), F32),
            jax.ShapeDtypeStruct((slots, width), BF16),
        ]
        + [jax.ShapeDtypeStruct((slots, units), BF16)] * 3,
        compiler_params=params(1),
        cost_estimate=cost(12 * slots * width * units, 40 << 20),
        name="expert",
    )(own, x, dy, other, misc, w_in, w_in, w_out, *more)


def expert_grads_kernel(seq_ref, *refs):
    count = (len(refs) - 4) // 6
    sets = [refs[k * 5 : k * 5 + 5] for k in range(count)]
    in_kept, in_away, out_kept, out_away = refs[5 * count : 5 * count + 4]
    turned_x = refs[5 * count + 4 :]
    step, half = pl.program_id(0), pl.num_programs(0) // 2

    @pl.when(step == 0)
    def _():
        for xt_ref, one in zip(turned_x, sets, strict=True):
            xt_ref[...] = flipped(one[0][...])

    def total(of):
        return sum((of(k) for k in range(1, count)), of(0)).astype(BF16)

    gate = total(lambda k: mm(turned_x[k][...], sets[k][3][...]))
    up = total(lambda k: mm(turned_x[k][...], sets[k][4][...]))
    down = total(lambda k: mm(sets[k][2][...], sets[k][1][...], TN))
    across = seq_ref[0] // 2

    def put(in_ref, out_ref):
        in_ref[across] = gate
        in_ref[1 - across] = up
        out_ref[0] = down

    @pl.when(step < half)
    def _():
        put(in_away, out_away)

    @pl.when(step >= half)
    def _():
        put(in_kept, out_kept)


def expert_grads(seq, sets, tile=256):
    width, units = sets[0][0].shape[1], sets[0][2].shape[1]
    steps = units // tile
    half = steps // 2
    part = units // 4

    def core_of(j, s):
        return jnp.where(j < half, 1 - s[0] % 2, s[0] % 2)

    def inner(j, s):
        return core_of(j, s) * half + j % half

    def outer(j, s):
        owner = 2 * ((s[0] // 2) ^ (j % half // (half // 2))) + core_of(j, s)
        return owner * (half // 2) + j % (half // 2)

    in_specs = []
    for x, *_ in sets:
        rows = pl.BlockSpec(x.shape, lambda j, s: (0, 0))
        saved = pl.BlockSpec((x.shape[0], tile), lambda j, s: (0, inner(j, s)))
        acts = pl.BlockSpec((x.shape[0], tile), lambda j, s: (0, outer(j, s)))
        in_specs += [rows, rows, acts, saved, saved]

    def kept(j):
        return jnp.maximum(j - half, 0)

    def away(j):
        return jnp.minimum(j, half - 1)

    def places(of):
        return [
            pl.BlockSpec((2, width, tile), lambda j, s: (0, 0, of(j))),
            pl.BlockSpec(
                (1, tile, width), lambda j, s: (of(j) // (half // 2), of(j) % (half // 2), 0)
            ),
        ]

    keeps, aways = places(kept), places(away)
    in_shape = jax.ShapeDtypeStruct((2, width, 2 * part), BF16)
    out_shape = jax.ShapeDtypeStruct((2, part, width), BF16)
    slots = sum(one[0].shape[0] for one in sets)
    return pl.pallas_call(
        expert_grads_kernel,
        grid_spec=pltpu.PrefetchScalarGridSpec(
            num_scalar_prefetch=1,
            grid=(steps,),
            in_specs=in_specs,
            out_specs=[keeps[0], aways[0], keeps[1], aways[1]],
            scratch_shapes=[pltpu.VMEM((width, one[0].shape[0]), BF16) for one in sets],
        ),
        out_shape=[in_shape, in_shape, out_shape, out_shape],
        compiler_params=params(1),
        cost_estimate=cost(2 * slots * width * units, 4 << 20),
        name="expert_grads",
    )(seq, *[array for one in sets for array in one])


def share_block(tokens, width, index):
    return pl.BlockSpec((tokens, width), lambda i: (index, 0))


def middle_back_kernel(
    dhn_ref, share_ref, slots_ref, routes_ref, gates_ref, misc_ref, hidden_ref, hn_ref,
    dy_ref, ctx_ref, w_ref, seq_ref, *refs, experts, parts,
):
    back_refs, (dh_ref, dctx_ref, grad_ref) = refs[:-3], refs[-3:]
    tokens = dhn_ref.shape[0]
    slots = experts * sum(parts)
    place = lax.broadcasted_iota(jnp.int32, (tokens, slots), 1)
    is0, is1 = place == slots_ref[:, 0:1], place == slots_ref[:, 1:2]
    pick = jnp.where(is0 | is1, 1.0, 0.0).astype(BF16)
    came = jnp.zeros(hidden_ref.shape, F32)
    first = 0
    for part, back_ref in zip(parts, back_refs, strict=False):
        rows = experts * part
        back = back_ref[...]
        if len(back.shape) == 3:
            back = back[:, :part, :].reshape(rows, back.shape[2])
        came = came + mm(pick[:, first : first + rows], back)
        first += rows
    if len(parts) == 1:
        dgate = back_refs[1][...]
        dg0 = jnp.sum(jnp.where(is0, dgate, 0.0), axis=1, keepdims=True)
        dg1 = jnp.sum(jnp.where(is1, dgate, 0.0), axis=1, keepdims=True)
    else:
        notes = back_refs[1][:, parts[1] :, :LANES].astype(F32)
        tables = [notes[:, 2, :] + notes[:, 3, :], notes[:, 0, :] + notes[:, 1, :]]
        spot = lax.broadcasted_iota(jnp.int32, (tokens, LANES), 1)
        found = []
        for k in range(2):
            route, slot = routes_ref[:, k : k + 1], slots_ref[:, k : k + 1]
            value, first = jnp.zeros((tokens, 1), F32), 0
            for part, table in zip(parts, tables, strict=True):
                line = jnp.zeros((tokens, LANES), F32)
                for e in range(experts):
                    line = jnp.where(route == e, table[e : e + 1, :], line)
                inside = (slot >= first) & (slot < first + experts * part)
                here = inside & (spot == slot - first - route * part)
                value = value + jnp.sum(jnp.where(here, line, 0.0), axis=1, keepdims=True)
                first += experts * part
            found.append(value)
        dg0, dg1 = found
    g0, g1 = gates_ref[:, 0:1], gates_ref[:, 1:2]
    mean = g0 * dg0 + g1 * dg1
    lane = lax.broadcasted_iota(jnp.int32, (tokens, LANES), 1)
    dlogits = (
        jnp.where(lane == routes_ref[:, 0:1], g0 * (dg0 - mean), 0.0)
        + jnp.where(lane == routes_ref[:, 1:2], g1 * (dg1 - mean), 0.0)
    ).astype(BF16)
    misc = misc_ref[...]
    dhn = dhn_ref[...] + share_ref[...].astype(F32) + mm(dlogits, misc, NT) + came
    hidden = hidden_ref[...]
    r2 = lax.rsqrt(jnp.mean(hidden * hidden, axis=1, keepdims=True) + EPS)
    z2 = hidden * r2
    gain = misc.astype(F32).T[experts : experts + 1, :]
    gain_grad = jnp.sum(dhn * z2, axis=0, keepdims=True)
    dz2 = dhn * gain
    dh = dy_ref[...].astype(F32) + r2 * (dz2 - z2 * jnp.mean(dz2 * z2, axis=1, keepdims=True))
    dh_ref[...] = dh
    dhb = dh.astype(BF16)
    for k in range(dctx_ref.shape[0]):
        rows = dctx_ref.shape[1]
        at = pl.ds(pl.multiple_of((seq_ref[0] ^ k) * rows, 16), rows)
        dctx_ref[k] = mm(w_ref[at, :], dhb, NT).astype(BF16)
    width = w_ref.shape[0]
    grad_ref[:, :width] = mm(ctx_ref[...], dhb).astype(BF16)
    small = mm(dlogits, hn_ref[...], TN)
    row = lax.broadcasted_iota(jnp.int32, small.shape, 0)
    small = jnp.where(row == experts, gain_grad, small)
    grad_ref[:, width:] = small.T.astype(BF16)


def middle_back(dhn, share, backs, slots, routes, gates, misc, hidden, hn, dy, ctx, w_attn, seq, seq_devs, experts, parts):
    tokens, width = hidden.shape
    return pl.pallas_call(
        functools.partial(middle_back_kernel, experts=experts, parts=parts),
        grid=(1,),
        in_specs=[whole(), share_block(tokens, width, 1)]
        + [whole()] * 9
        + [pl.BlockSpec(memory_space=pltpu.SMEM)]
        + [whole()] * len(backs),
        out_specs=[whole()] * 3,
        out_shape=[
            jax.ShapeDtypeStruct((tokens, width), F32),
            jax.ShapeDtypeStruct((seq_devs, width // seq_devs, tokens), BF16),
            jax.ShapeDtypeStruct((width, width + LANES), BF16),
        ],
        compiler_params=params(),
        cost_estimate=cost(3e9, 16 << 20),
        name="middle_back",
    )(dhn, share, slots, routes, gates, misc, hidden, hn, dy, ctx, w_attn, seq, *backs)


def output_kernel(hidden_ref, dense_ref, share_ref, slots_ref, gates_ref, *refs):
    came_refs, out_ref = refs[:-1], refs[-1]
    mixture = jnp.zeros(hidden_ref.shape, F32)
    first = 0
    for came_ref in came_refs:
        tokens, slots = hidden_ref.shape[0], came_ref.shape[0]
        place = first + lax.broadcasted_iota(jnp.int32, (tokens, slots), 1)
        for k in range(2):
            pick = jnp.where(place == slots_ref[:, k : k + 1], 1.0, 0.0).astype(BF16)
            mixture = mixture + gates_ref[:, k : k + 1] * mm(pick, came_ref[...])
        first += slots
    out_ref[...] = hidden_ref[...] + dense_ref[...] + share_ref[...].astype(F32) + mixture


def output_of(hidden, shared, share, cames, slots, gates):
    return pl.pallas_call(
        output_kernel,
        grid=(1,),
        in_specs=[whole(), whole(), share_block(*hidden.shape, 0)] + [whole()] * (2 + len(cames)),
        out_specs=whole(),
        out_shape=jax.ShapeDtypeStruct(hidden.shape, F32),
        compiler_params=params(),
        cost_estimate=cost(2e9, 8 << 20),
        name="output_of",
    )(hidden, shared, share, slots, gates, *cames)


def qkv_back_kernel(seq_ref, *refs):
    count = len(ORDER)
    x_refs, d_refs, refs = refs[:count], refs[count:-9], refs[-9:]
    w_ref, cos_ref, sin_ref, kept_ref, away_ref, g_ref, acc_ref, gain_ref, z_ref = refs
    step = pl.program_id(0)
    columns = w_ref.shape[1] - 64

    @pl.when(step == 0)
    def _():
        acc_ref[...] = jnp.zeros_like(acc_ref)
        gain_ref[...] = jnp.zeros_like(gain_ref)

    for at_step, k in enumerate(ORDER):

        @pl.when(step == at_step)
        def _(x_ref=x_refs[k]):
            z_ref[...], _ = first_norm(x_ref[...])

    z1 = z_ref[...]
    xn_t = (z1 * gain_row(w_ref)).T.astype(BF16)
    cosine, sine = cos_ref[...], -sin_ref[...]
    pieces = []
    for d_ref in d_refs:
        for c in range(2):
            pieces.extend(turned(d_ref[0, c * 64 : c * 64 + 64, :].astype(F32), cosine, sine))
        pieces.append(d_ref[0, 128:192, :].astype(F32))
    pieces.append(jnp.zeros((64, z1.shape[0]), F32))
    d_rows = jnp.concatenate(pieces, axis=0).T.astype(BF16)
    dxn = mm(d_rows, w_ref[...], NT)
    acc_ref[...] += mm(xn_t, d_rows)
    gain_ref[0:1, :] += jnp.sum(dxn * z1, axis=0, keepdims=True)

    @pl.when(step < count // 2)
    def _():
        away_ref[0] = dxn.astype(BF16)

    @pl.when(step >= count // 2)
    def _():
        kept_ref[0] = dxn.astype(BF16)

    @pl.when(step == pl.num_programs(0) - 1)
    def _():
        split = columns + 64 - LANES
        g_ref[:, :split] = acc_ref[:, :split].astype(BF16)
        row = lax.broadcasted_iota(jnp.int32, (LANES, gain_ref.shape[1]), 0)
        gain = jnp.where(row == LANES // 2, gain_ref[0:1, :], 0.0).T
        g_ref[:, split:] = (acc_ref[:, split:] + gain).astype(BF16)


ORDER = (1, 3, 0, 2)


def qkv_back(seq, xs, d_heads, w, cosine, sine):
    tokens, width = xs[0].shape

    def place(i, s):
        k = jnp.where(i < 2, 2 * i + 1, 2 * i - 4)
        return k ^ s[0]

    angles = pl.BlockSpec((32, tokens), lambda i, s: (0, place(i, s)))
    rows = pl.BlockSpec((tokens, width), lambda i, s: (0, 0))
    grads = pl.BlockSpec((1, 192, tokens), lambda i, s: (place(i, s), 0, 0))
    pair = jax.ShapeDtypeStruct((2, tokens, width), BF16)
    return pl.pallas_call(
        qkv_back_kernel,
        grid_spec=pltpu.PrefetchScalarGridSpec(
            num_scalar_prefetch=1,
            grid=(len(ORDER),),
            in_specs=[rows] * len(xs)
            + [grads] * len(d_heads)
            + [pl.BlockSpec(w.shape, lambda i, s: (0, 0)), angles, angles],
            out_specs=[
                pl.BlockSpec((1, tokens, width), lambda i, s: (jnp.maximum(i - 2, 0), 0, 0)),
                pl.BlockSpec((1, tokens, width), lambda i, s: (jnp.minimum(i, 1), 0, 0)),
                pl.BlockSpec(w.shape, lambda i, s: (0, 0)),
            ],
            scratch_shapes=[
                pltpu.VMEM(w.shape, F32),
                pltpu.VMEM((8, width), F32),
                pltpu.VMEM((tokens, width), F32),
            ],
        ),
        out_shape=[pair, pair, jax.ShapeDtypeStruct(w.shape, BF16)],
        compiler_params=params(1),
        cost_estimate=cost(12e9, 12 << 20),
        name="qkv_back",
    )(seq, *xs, *d_heads, w, cosine, sine)


def input_back_kernel(x_ref, dh_ref, w_ref, *refs):
    dxn_refs, out_ref = refs[:-1], refs[-1]
    z1, r1 = first_norm(x_ref[...])
    dz1 = add_up([ref[...] for ref in dxn_refs]) * gain_row(w_ref)
    out_ref[...] = dh_ref[...] + r1 * (dz1 - z1 * jnp.mean(dz1 * z1, axis=1, keepdims=True))


def input_back(x, dh, w, dxns):
    return pl.pallas_call(
        input_back_kernel,
        in_specs=[whole()] * (3 + len(dxns)),
        out_specs=whole(),
        out_shape=jax.ShapeDtypeStruct(dh.shape, F32),
        compiler_params=params(),
        cost_estimate=cost(1e8, 6 << 20),
        name="input_back",
    )(x, dh, w, *dxns)


def slot_plan(routes, order, experts, parts):
    before = (order[:, None] > order[None, :]).astype(BF16)
    ids = jnp.arange(experts, dtype=jnp.int32)
    first = (routes[:, 0:1] == ids).astype(BF16)
    second = (routes[:, 1:2] == ids).astype(BF16)
    earlier = mm(before, jnp.concatenate([first, second], axis=1))
    every = jnp.sum(first.astype(F32), axis=0, keepdims=True)
    place0 = jnp.sum(earlier[:, :experts] * first.astype(F32), axis=1)
    place1 = jnp.sum((earlier[:, experts:] + every) * second.astype(F32), axis=1)
    place = jnp.stack([place0, place1], axis=1).astype(jnp.int32)
    capacity = sum(parts)
    every = jnp.where(place < capacity, routes * capacity + place, experts * capacity)
    slot = jnp.full(place.shape, experts * capacity, jnp.int32)
    low = 0
    for part in parts:
        inside = (place >= low) & (place < low + part)
        slot = jnp.where(inside, experts * low + routes * part + place - low, slot)
        low += part
    return slot, every


def padded(shard, columns):
    return jnp.pad(shard, ((0, 0), (0, columns - shard.shape[1])))


def by_core(columns):
    rows, count = columns.shape
    tiles = count // 512
    return columns.reshape(rows, tiles, 4, 2, 64).transpose(3, 1, 0, 2, 4).reshape(2, tiles, rows, 256)


def paired_shards(shared_in, shared_out):
    units, width = shared_in.shape[1] // 2, shared_out.shape[1]
    shard = jnp.stack([by_core(shared_in[:, :units]), by_core(shared_in[:, units:])], axis=1)
    me = coordinates()["c"]
    away = lax.dynamic_index_in_dim(shard, 1 - me, 0, False)
    kept = lax.dynamic_index_in_dim(shard, me, 0, False)
    inner = ordered(kept, flip(away, "c"), me, 2).reshape(2, -1, 256)
    down = shared_out.reshape(2, 32, width // 256, 256).transpose(0, 2, 1, 3).reshape(2, -1, 256)
    return jnp.concatenate([inner, down], axis=1)


def paired_grads(sum_a, sum_b):
    me = coordinates()["c"]
    inner = jnp.stack([sum_a[:192], sum_b[:192]]).reshape(2, 4, 2, 24, 256)
    away = lax.dynamic_index_in_dim(inner, 1 - me, 2, False)
    kept = lax.dynamic_index_in_dim(inner, me, 2, False)
    both = ordered(kept, flip(away, "c"), me, 0).reshape(2, 2, 4, 24, 4, 64)
    inner = both.transpose(3, 1, 2, 4, 0, 5).reshape(24, -1)
    down = jnp.stack([sum_a[192:], sum_b[192:]]).reshape(2, 3, 32, 256)
    return inner, down.transpose(0, 2, 1, 3).reshape(64, -1)


def scalar(value):
    return value.astype(jnp.int32).reshape(1)


def split_parts(array, sizes):
    found, low = [], 0
    for size in sizes:
        found.append(array[low : low + size])
        low += size
    return found


def on_device(
    layer_input, cotangent, segments, routes, order, norm1_gain, attn_qkv, attn_out,
    norm2_gain, router, shared_in, shared_out, expert_in, expert_out,
):
    tokens, width = layer_input.shape
    seq_devs = lax.axis_size("seq")
    experts = lax.axis_size("dp")
    capacity = max(2, (18 * tokens + 8 * experts - 1) // (8 * experts))
    small = small_torus()
    parts = (80, capacity - 80) if small and capacity == 144 else (capacity,)
    sizes = [experts * part for part in parts]
    slots = experts * capacity
    units = shared_in.shape[1] // 2
    columns = 3 * width // seq_devs
    seq = scalar(lax.axis_index("seq"))

    shard_rows = norm1_gain.shape[0]
    head_shard = jnp.concatenate(
        [
            attn_qkv.reshape(-1, seq_devs, columns).transpose(1, 0, 2),
            jnp.broadcast_to(norm1_gain[None, :, None], (seq_devs, shard_rows, 1)),
            jnp.zeros((seq_devs, shard_rows, 63), BF16),
        ],
        axis=2,
    )
    head_shard = swap(head_shard, "seq").reshape(-1, columns + 64)
    misc_shard = jnp.concatenate(
        [attn_out, padded(jnp.concatenate([router, norm2_gain[:, None]], axis=1), LANES)], axis=1
    )
    slot_of, expert_slot = slot_plan(routes, order, experts, parts)
    every_slot = jnp.arange(slots, dtype=jnp.int32)[:, None]

    def pick_of(rows):
        return ((every_slot == rows[0:1]) | (every_slot == rows[1:2])).astype(BF16)

    rows = expert_slot.T
    pick_dy = pick_of(rows)
    routes_f = routes.astype(F32)
    other = jnp.sum(
        jnp.where(every_slot == rows[0:1], routes_f[:, 1][None, :], 0.0)
        + jnp.where(every_slot == rows[1:2], routes_f[:, 0][None, :], 0.0),
        axis=1,
    ).reshape(experts, capacity)
    pick = pick_of(slot_of.T)
    dy_send = mm(pick_dy, cotangent).astype(BF16).reshape(experts, capacity, width)
    frequency = BASE ** (-(jnp.arange(32, dtype=F32) * 2.0 / 64))
    places = jnp.arange(tokens * seq_devs, dtype=jnp.int32)
    angles = places.astype(F32)[None, :] * frequency[:, None]
    cosine, sine = jnp.cos(angles), jnp.sin(angles)

    block_rows = head_shard.shape[0]
    extra = -(-capacity // block_rows)
    notes = jnp.pad(other.astype(BF16), ((0, 0), (0, extra * block_rows - capacity)))
    notes = notes.reshape(experts, block_rows, extra)
    packed = jnp.concatenate(
        [
            jnp.broadcast_to(head_shard[None, :, : columns + 1], (experts, block_rows, columns + 1)),
            notes,
            jnp.zeros((experts, block_rows, 63 - extra), BF16),
        ],
        axis=2,
    )
    packed = swap(packed, "dp")
    w_parts = [packed.reshape(1, -1, columns + 64)]
    notes = packed[:, :, columns + 1 : columns + 1 + extra].reshape(experts, -1)[:, :capacity]
    others, low = [], 0
    for part in parts:
        others.append(notes[:, low : low + part].astype(F32).reshape(-1, 1))
        low += part
    if small:
        here = coordinates()
        me = scalar(here["z"] * 4 + here["y"] * 2 + here["x"])
        along_x = flip(after(layer_input, head_shard), "x")
        token_blocks = [layer_input, flip(layer_input, "c"), along_x, flip(along_x, "c")]
        misc_z = z_gather(after(join(misc_shard, "c", 0).reshape(48, -1), *w_parts))
        misc_parts = [misc_z, flip(after(misc_z, *w_parts), "y")]
    else:
        me = jnp.zeros((1,), jnp.int32)
        gathered = relative(lax.all_gather(layer_input, "seq", axis=0, tiled=False))
        token_blocks = [gathered[k] for k in range(seq_devs)]
        misc_parts = [lax.all_gather(misc_shard, AXES, axis=0, tiled=True)[None]]
    w_parts, pick, routes = (lambda v: (v[:-2], *v[-2:]))(together([*w_parts, pick, routes]))
    dy_rows = swap(after(dy_send, *w_parts, misc_z) if small else dy_send, "dp")

    heads, w_heads = qkv_project(
        seq, scalar(lax.axis_index("dp")), token_blocks, w_parts, cosine, sine
    )
    if small:
        heads = after(heads, misc_z)
        misc_parts.append(flip(jnp.concatenate(misc_parts), "x"))
        shards = z_shards(after(paired_shards(shared_in, shared_out), w_heads))
    ctx_heads, log_totals = attend(seq, heads, segments)
    ctxs = seq_send_twice(ctx_heads)
    hidden, hn, gates, w_attn, misc, ctx, *sends = middle(
        me, seq, ctxs, layer_input, misc_parts, pick, routes, experts, parts
    )

    shards = together(shards, hn) if small else None
    sends[0] = after(sends[0], dy_rows, *shards) if small else sends[0]

    row_parts = [
        swap(send.reshape(experts, part, width), "dp").reshape(-1, width)
        for part, send in zip(parts, sends, strict=True)
    ]
    if small:
        a0, b0 = jnp.stack([part[0] for part in shards]), jnp.stack([part[1] for part in shards])
        a1, b1 = flip(a0, "y"), flip(b0, "x")
        hn_pair = jnp.concatenate([hn, flip(hn, "c")], axis=0)
        dy_pair = jnp.concatenate([cotangent, flip(cotangent, "c")], axis=0)
        row_parts[0] = after(row_parts[0], a0, b0, hn_pair, dy_pair)
    else:
        w_gate = lax.all_gather(shared_in[:, :units], AXES, axis=0, tiled=True)
        w_up = lax.all_gather(shared_in[:, units:], AXES, axis=0, tiled=True)
        w_out = lax.all_gather(shared_out, AXES, axis=0, tiled=True)

    own = scalar(lax.axis_index("dp"))
    sets, eos, dxes, dgates, low = [], [], [], [], 0
    for k, (part, rows, other) in enumerate(zip(parts, row_parts, others, strict=True)):
        if k == 1:
            a0, b0, a1, b1 = together((a0, b0, a1, b1), dxes[0])
            a2, b2 = flip(jnp.concatenate([a0, a1]), "x"), flip(jnp.concatenate([b0, b1]), "y")
        eo, dxe, dgate, deo, act, d_gate, d_up = expert(
            own, rows, dy_rows if small else dy_rows.reshape(-1, width), low, other, misc, expert_in,
            expert_out, dgates[0] if k == 1 else None,
        )
        low += part
        sets.append((rows, deo, act, d_gate, d_up))
        eos.append(eo.reshape(experts, part, width))
        dxes.append(dxe.reshape(experts, -1, width))
        dgates.append(dgate)
    backs = []
    for k, dxe in enumerate(dxes):
        back = swap(after(dxe, *backs), "dp")
        backs.append(back if k else back.reshape(-1, width))
    if not small:
        backs.append(swap(dgates[0].reshape(experts, capacity), "dp").reshape(1, slots))
    held = backs[:1]
    if not small:
        shared, dhn, grad_gate, grad_up, grad_out = dense(hn, cotangent, w_gate, w_up, w_out)
        share = jnp.zeros((2 * tokens, width), BF16)
    sets = [(after(one[0], *held),) + one[1:] for one in sets]
    in_kept, in_away, out_kept, out_away = expert_grads(seq, sets)
    if small:
        hn_pair = after(hn_pair, in_kept)
        shared, dhn, share, *grads = paired(me, hn_pair, dy_pair, (a0, a1, a2), (b0, b1, b2))
        share = flip(share, "c")
        ka, wa, kb, wb = grads
        ca, cb = flip(wa, "x"), flip(wb, "y")
        in_away, out_away = flip(in_away, "c"), flip(out_away, "c")
    dh, dctx, grad_attn = middle_back(
        dhn, share, backs, slot_of, routes, gates, misc, hidden, hn, cotangent, ctx, w_attn,
        seq, seq_devs, experts, parts,
    )

    dctxs = seq_send_twice(dctx)
    if small:
        in_kept, out_kept = together((in_kept, out_kept), dh)
    in_terms, in_far = copies_sum(in_kept, in_away)
    out_terms, out_far = copies_sum(out_kept, out_away)
    if small:
        ca, cb = together((ca, cb), dh)
        wa, wb = add_up([ka[4:], ca[4:]]).astype(BF16), add_up([kb[4:], cb[4:]]).astype(BF16)
        ea, eb = flip(wa, "y"), flip(wb, "x")
        dctxs[0] = after(dctxs[0], in_far, out_far, wa, wb)
    came = swap(after(jnp.concatenate(eos, axis=1), dctxs[2]), "dp").reshape(-1, width)
    d_heads = []
    for head in range(columns // 192):
        held = after(heads, *d_heads) if d_heads else heads
        if small and head == 1:
            grad_attn = after(grad_attn, d_heads[0])
            part = half_sum(grad_attn.reshape(8, 2, 2, -1, width + LANES), "c", 2).astype(BF16)
            held = after(held, grad_attn)
        if small and head == 2:
            part = after(part, d_heads[1])
            part_kept = lax.dynamic_index_in_dim(part, here["x"], 1, False)
            part_came = flip(lax.dynamic_index_in_dim(part, 1 - here["x"], 1, False), "x")
        d_heads.append(attend_back(seq, held, dctxs, ctx_heads, log_totals, segments, head))
    if small:
        ea, eb = together((ea, eb), d_heads[0])
        wa, wb = add_up([ka[:4], ca[:4], ea]).astype(BF16), add_up([kb[:4], cb[:4], eb]).astype(BF16)
        sums = z_sum(after(jnp.stack([wa, wb], axis=1), came))
        d_heads[0] = after(d_heads[0], out_terms[2])
    dxn_kept, dxn_away, grad_heads = qkv_back(seq, token_blocks, d_heads, w_heads, cosine, sine)
    if small:
        dxn_away = after(flip(dxn_away, "c"), in_terms[2])
    dxn_terms, dxn_far = copies_sum(dxn_kept, dxn_away)
    input_grad = input_back(layer_input, dh, w_heads, dxn_terms)
    layer_output = output_of(
        hidden, shared, share, [after(came, dxn_far)], expert_slot, gates
    )

    grad_heads = grad_heads.reshape(experts * seq_devs, -1, columns + 64)
    grad_heads = swap(grad_heads, AXES)
    grad_heads = grad_heads.reshape((experts, seq_devs) + grad_heads.shape[1:])
    if small:
        sum_in, sum_out = paired_grads(*together((sums[0], sums[1]), dxn_far))
        part = add_up([part_kept, after(part_came, dxn_far)]).astype(BF16)
        sum_attn = jnp.sum(swap(after(part, grad_heads), "dp").astype(F32), axis=0)
        in_terms, out_terms = together((*in_terms, *out_terms), dxn_far), ()
        in_terms, out_terms = in_terms[:3], in_terms[3:]
    else:
        total = functools.partial(lax.psum_scatter, scatter_dimension=0, tiled=True)
        sum_attn = total(grad_attn, AXES).astype(F32)
        sum_out = total(grad_out, AXES).astype(F32)
        sum_in = jnp.concatenate([total(grad_gate, AXES), total(grad_up, AXES)], axis=1).astype(F32)
    sum_heads = jnp.sum(grad_heads.astype(F32), axis=0)
    return (
        layer_output,
        input_grad,
        jnp.sum(sum_heads[:, :, columns], axis=0),
        sum_heads[:, :, :columns].transpose(1, 0, 2).reshape(-1, seq_devs * columns),
        sum_attn[:, :width],
        sum_attn[:, width + experts],
        sum_attn[:, width : width + experts],
        sum_in,
        sum_out,
        add_up(in_terms)[None],
        add_up(out_terms)[None],
    )


def solution(mesh):
    rows = P(AXES, None)
    return jax.shard_map(
        on_device,
        mesh=mesh,
        in_specs=(
            rows, rows, P("dp", None), rows, P(AXES), P(AXES), rows, rows,
            P(AXES), rows, rows, rows, P("dp", None, None), P("dp", None, None),
        ),
        out_specs=(
            rows, rows, P(AXES), rows, rows, P(AXES), rows, rows, rows,
            P("dp", None, "seq"), P("dp", "seq", None),
        ),
        check_vma=False,
    )
```
